32 devices in a mesh: group: 2 (over x), src: 8 (over z, y), tile: 2 (over core).
Axes of the slice: x: 2, y: 2, z: 4, core: 2. Of those that a mesh axis runs over, the one named last changes fastest.
Arguments:
- near_field: bfloat16 [4, 64, 2, 3, 512], P(('group', 'tile'), 'src'), parts along dimension 0, may hold values from -6 to 6
- x_taps: bfloat16 [8, 2, 8, 65], P('src'), may hold values from -0.5 to 0.5
- y_taps: bfloat16 [8, 2, 8, 65], P('src'), may hold values from -0.1875 to 0.1875
- source_weight: float32 [8], P('src'), may hold values from 0.0125 to 0.125
Outputs:
- intensity: float32 [4, 64, 512], P(('group', 'tile'), 'src'), parts along dimension 0
The draws below stay inside these ranges and needn't reach their ends.
There are 2 independent parts, one for each index of `group`. The reference program is written for one: setup_inputs(seed, part) draws one part's arguments, and reference() takes and returns one part's arrays. A program takes and returns all parts, laid end to end along the dimension named above; an argument that names none is the same for every part. Nothing has to cross between parts.
All inputs are finite; a program needn't handle non-finite values.
Results may differ from the reference program's by a relative error of at most 0.00054.
Values may be sent and summed in bfloat16 or wider, within the bound.
No kernel may reach another device: no remote copies, remote signals or barrier semaphores. Data moves between devices by JAX's collectives and lax.ppermute only.
A program may use at most 128 MiB of HBM per device.

```python
import math
import jax
import jax.numpy as jnp
from jax import lax

COMPS = 3
RANK = 8
TAPS = 65
W = 512
TR = 64
SOURCES = 8
N_TILE = 2


def steps_of(key, shape, cuts, least, largest):
    def one(dim, blocks):
        steps = jax.random.uniform(jax.random.fold_in(jax.random.fold_in(key, 6), dim), (blocks,), jnp.float32, least / len(cuts), largest / len(cuts))
        return jnp.repeat(jnp.exp(steps), shape[dim] // blocks).reshape((-1,) + (1,) * (len(shape) - dim - 1))

    gain = one(*cuts[0])
    for cut in cuts[1:]:
        gain = gain * one(*cut)
    return gain


def centred(rng, extent, scale, reach, split=(), held_as=jnp.bfloat16):
    values = jax.random.normal(rng, extent, jnp.float32) * scale
    if len(split) > 0:
        values = steps_of(rng, extent, split, -0.22, 0.18) * values
    return jnp.clip(values, min=-reach, max=reach).astype(held_as)


def setup_inputs(seed: int = 0, part: int = 0) -> dict:
    seeds = jax.random.split(jax.random.key(seed), 5)
    part_splits = jax.random.split(jax.random.fold_in(seeds[4], part), 5)
    return {
        "near_field": centred(part_splits[0], (N_TILE, TR, 2, COMPS, W), 1.0, 6.0, ((0, 2), (1, 8))),
        "x_taps": centred(seeds[1], (SOURCES, 2, RANK, TAPS), (2 * TAPS) ** -0.5, 0.5, ((0, 8),)),
        "y_taps": centred(seeds[2], (SOURCES, 2, RANK, TAPS), (2 * RANK * TAPS) ** -0.5, 0.1875, ((0, 8),)),
        "source_weight": jnp.clip(jnp.exp(math.log(0.125) - 2.3025851 * jax.random.uniform(seeds[3], (SOURCES,), jnp.float32) ** steps_of(seeds[3], (SOURCES,), ((0, 8),), -0.2, 0.2)), 0.0125, 0.125),
    }


def reference(near_field, x_taps, y_taps, source_weight):
    tiles, tile_rows, _, comps, width = near_field.shape
    slab_rows = tiles * tile_rows
    ranks = x_taps.shape[2]
    rim_width = (x_taps.shape[-1] - 1) // 2
    field = near_field.astype(jnp.float32).reshape(slab_rows, 2, comps, width)
    lhs_columns = field.transpose(0, 2, 1, 3).reshape(slab_rows * comps, 2, width)

    def one_source(total, inputs):
        column_taps, row_taps, weight = inputs
        column_f = column_taps.astype(jnp.float32)
        col_re, col_im = column_f[0], column_f[1]
        kernel_x = jnp.stack([jnp.stack([col_re, -col_im], axis=1), jnp.stack([col_im, col_re], axis=1)], axis=0)
        kernel_x = kernel_x.reshape(2 * ranks, 2, -1)
        passed = lax.conv_general_dilated(lhs_columns, kernel_x, (1,), [(rim_width, rim_width)],
                                          dimension_numbers=("NCH", "OIH", "NCH"),
                                          precision=lax.Precision.HIGHEST)
        passed = lax.optimization_barrier(passed.astype(jnp.bfloat16)).astype(jnp.float32)
        passed = passed.reshape(slab_rows, comps, 2, ranks, width)
        lhs_rows = passed.transpose(1, 4, 2, 3, 0).reshape(comps * width, 2 * ranks, slab_rows)
        row_f = row_taps.astype(jnp.float32)
        row_re, row_im = row_f[0], row_f[1]
        kernel_y = jnp.stack([jnp.stack([row_re, -row_im], axis=0), jnp.stack([row_im, row_re], axis=0)], axis=0)
        kernel_y = kernel_y.reshape(2, 2 * ranks, -1)
        image = lax.conv_general_dilated(lhs_rows, kernel_y, (1,), [(rim_width, rim_width)],
                                         dimension_numbers=("NCH", "OIH", "NCH"),
                                         precision=lax.Precision.HIGHEST)
        power = jnp.sum((image * image).reshape(comps, width, 2, slab_rows), axis=(0, 2))
        return total + weight * power.T, None

    start_total = jnp.zeros((slab_rows, width), jnp.float32)
    total, _ = lax.scan(one_source, start_total, (x_taps, y_taps, source_weight))
    return total.reshape(tiles, tile_rows, width)
```

```python
import jax
import jax.numpy as jnp
from jax import lax
from jax.sharding import PartitionSpec as P


def padded_2(cells, sides, width):
    for axis, dim in sides:
        count = lax.axis_size(axis)
        ends = count - 1
        head = lax.slice_in_dim(cells, 0, width, axis=dim)
        tail = lax.slice_in_dim(cells, cells.shape[dim] - width, cells.shape[dim], axis=dim)
        cells = jnp.concatenate(
            [
                lax.ppermute(tail, axis, [(i, (i + 1) % count) for i in range(ends)]),
                cells,
                lax.ppermute(head, axis, [((i + 1) % count, i) for i in range(ends)]),
            ],
            axis=dim,
        )
    return cells


def column_mats(taps):
    tap_count = taps.shape[-1]
    shift = lax.broadcasted_iota(jnp.int32, (tap_count, 256, 128), 0)
    inner = lax.broadcasted_iota(jnp.int32, (tap_count, 256, 128), 1)
    outer = lax.broadcasted_iota(jnp.int32, (tap_count, 256, 128), 2)
    select = (inner - outer == shift).astype(jnp.float32)
    coef = jnp.einsum(
        "xprt,tqj->xpqrj", taps.astype(jnp.float32), select, precision=lax.Precision.HIGHEST
    )
    real_part, imag_part = (coef[:, 0], coef[:, 1])
    full = jnp.stack(
        [jnp.stack([real_part, imag_part], axis=2), jnp.stack([-imag_part, real_part], axis=2)],
        axis=1,
    ).astype(jnp.bfloat16)
    return (full[:, :, :128], full[:, :, 128:])


def column_pass(rows_field, lower_mat, upper_mat, rim_width):
    count_rows, _, comps, width = rows_field.shape
    padded = jnp.pad(rows_field, ((0, 0), (0, 0), (0, 0), (rim_width, 128 - rim_width)))
    pieces = padded.reshape(count_rows, 2, comps, width // 128 + 1, 128)
    result = jnp.einsum(
        "ipcbq,xpqsrj->ixsrcbj", pieces[:, :, :, :-1], lower_mat, preferred_element_type=jnp.float32
    )
    result = result + jnp.einsum(
        "ipcbq,xpqsrj->ixsrcbj", pieces[:, :, :, 1:], upper_mat, preferred_element_type=jnp.float32
    )
    sources, ranks = (lower_mat.shape[0], lower_mat.shape[4])
    return result.reshape(count_rows, sources, 2, ranks, comps, width).astype(jnp.bfloat16)


def row_matrices(taps, block_rows, rim_width):
    tap_count = taps.shape[-1]
    span = block_rows + 2 * rim_width
    shift = lax.broadcasted_iota(jnp.int32, (tap_count, block_rows, span), 0)
    out_row = lax.broadcasted_iota(jnp.int32, (tap_count, block_rows, span), 1)
    in_row = lax.broadcasted_iota(jnp.int32, (tap_count, block_rows, span), 2)
    select = (in_row - out_row == shift).astype(jnp.float32)
    coef = jnp.einsum(
        "xprt,tik->xpirk", taps.astype(jnp.float32), select, precision=lax.Precision.HIGHEST
    )
    real_part, imag_part = (coef[:, 0], coef[:, 1])
    full = jnp.stack(
        [jnp.stack([real_part, -imag_part], axis=2), jnp.stack([imag_part, real_part], axis=2)],
        axis=1,
    )
    return full.astype(jnp.bfloat16)


def per_device(near_field, x_taps, y_taps, source_weight):
    rim_width = (x_taps.shape[-1] - 1) // 2
    width = near_field.shape[-1]
    local_rows = near_field.shape[1]
    count = lax.axis_size("src")
    spread = jnp.broadcast_to(near_field, (count,) + near_field.shape[1:])
    whole_tile = lax.all_to_all(spread, "src", 0, 0).reshape(
        (1, count * local_rows) + near_field.shape[2:]
    )
    padded_field = padded_2(whole_tile, (("tile", 1),), rim_width)
    lower_mat, upper_mat = column_mats(x_taps)
    padded_pass = column_pass(padded_field[0], lower_mat, upper_mat, rim_width)
    tile_rows = padded_pass.shape[0] - 2 * rim_width
    block_rows = 64
    row_mats = row_matrices(y_taps, block_rows, rim_width)

    def one_block(index):
        first_row = index * block_rows
        window = lax.dynamic_slice_in_dim(padded_pass, first_row, block_rows + 2 * rim_width, 0)
        image = jnp.einsum(
            "xoiprk,kxprcw->xoicw", row_mats, window, preferred_element_type=jnp.float32
        )
        power = jnp.sum(image * image, axis=(1, 3))
        return jnp.sum(source_weight[:, None, None] * power, axis=0)

    blocks = lax.map(one_block, jnp.arange(tile_rows // block_rows, dtype=jnp.int32))
    own_image = blocks.reshape(tile_rows, width)
    pieces = own_image.reshape(count, local_rows, width)
    summed = jnp.sum(lax.all_to_all(pieces, "src", 0, 0), axis=0)
    return summed.reshape(1, local_rows, width)


def solution(mesh):
    placed = (
        P(("group", "tile"), "src", None, None, None),
        P("src", None, None, None),
        P("src", None, None, None),
        P("src"),
    )
    return jax.shard_map(
        per_device,
        mesh=mesh,
        in_specs=placed,
        out_specs=P(("group", "tile"), "src", None),
        check_vma=False,
    )
```

```python
import functools

import jax
import jax.numpy as jnp
from jax import lax
from jax.experimental import pallas as pl
from jax.experimental.pallas import tpu as pltpu
from jax.sharding import PartitionSpec as P

LANES = 128
F32 = jnp.float32
BF16 = jnp.bfloat16


def send_kernel(rim, field_ref, send_ref):
    _, rows, _, comps, width = field_ref.shape
    sources, halves = send_ref.shape[:2]
    per_half = width // LANES // halves
    field = field_ref[0].astype(F32)
    edge = jnp.zeros((rows, rim), F32)
    planes = [[field[:, part, comp, :] for part in range(2)] for comp in range(comps)]
    for half in range(halves):
        groups = []
        for block in range(half * per_half, (half + 1) * per_half):
            first, last = block * LANES, (block + 1) * LANES
            for comp in range(comps):
                mains, rims = [], []
                for plane in planes[comp]:
                    mains.append(plane[:, first:last])
                    rims.append(plane[:, first - rim : first] if first > 0 else edge)
                    rims.append(plane[:, last : last + rim] if last < width else edge)
                groups.append(jnp.concatenate(mains + rims, axis=1))
        packed = jnp.concatenate(groups, axis=0).astype(BF16)
        for source in range(sources):
            send_ref[source, half] = packed


def rolled(line):
    return pltpu.roll(jnp.broadcast_to(line, (LANES, LANES)), 0, 1, stride=1, stride_axis=0)


def band_kernel(rim, x_taps_ref, y_taps_ref, column_ref, row_ref):
    _, _, ranks, taps = x_taps_ref.shape
    tap = lax.broadcasted_iota(jnp.int32, (taps, LANES), 0)
    lane = lax.broadcasted_iota(jnp.int32, (taps, LANES), 1)
    x_place = (lane == (rim - tap) % LANES).astype(BF16)
    y_place = (lane == (tap - rim) % LANES).astype(BF16)
    i = lax.broadcasted_iota(jnp.int32, (LANES, LANES), 0)
    j = lax.broadcasted_iota(jnp.int32, (LANES, LANES), 1)
    near = jnp.abs(i - j) < LANES // 2
    x_lines = [jnp.dot(x_taps_ref[0, part], x_place, preferred_element_type=F32) for part in range(2)]
    y_lines = [jnp.dot(y_taps_ref[0, part], y_place, preferred_element_type=F32) for part in range(2)]
    half_lanes = LANES // 2
    for r in range(ranks):
        re, im = (rolled(lines[r : r + 1]) for lines in x_lines)

        def columns(of_re, of_im):
            parts = [jnp.where(near, of_re, 0.0), jnp.where(near, of_im, 0.0)]
            for ring in (of_re, of_im):
                parts.append(jnp.where(j[LANES - rim :] < half_lanes, ring[LANES - rim :], 0.0))
                parts.append(jnp.where(j[:rim] >= half_lanes, ring[:rim], 0.0))
            return jnp.concatenate(parts, axis=0).astype(BF16)

        column_ref[r, :, :LANES] = columns(re, -im)
        column_ref[r, :, LANES:] = columns(im, re)

        re, im = (rolled(lines[r : r + 1]) for lines in y_lines)
        masks = [near] if row_ref.shape[0] == 1 else [j - i > half_lanes, near, j - i < -half_lanes]
        for w, mask in enumerate(masks):
            re_w, im_w = (jnp.where(mask, re, 0.0), jnp.where(mask, im, 0.0))
            at = 2 * r * LANES
            row_ref[w, :LANES, at : at + LANES] = re_w.astype(BF16)
            row_ref[w, :LANES, at + LANES : at + 2 * LANES] = (-im_w).astype(BF16)
            row_ref[w, LANES:, at : at + LANES] = im_w.astype(BF16)
            row_ref[w, LANES:, at + LANES : at + 2 * LANES] = re_w.astype(BF16)


def image_kernel(comps, got_ref, column_ref, row_ref, weight_ref, out_ref, lines_ref, passed_ref):
    sources, tiles, per_device, depth = got_ref.shape
    rows = out_ref.shape[2]
    ranks = column_ref.shape[0]
    groups = per_device // rows
    per_half = groups // comps
    tile_rows = sources * rows
    slab_rows = tiles * tile_rows
    chunks = slab_rows // LANES
    width = per_half * LANES
    for tile in range(tiles):
        mine = got_ref[:, tile].astype(F32)
        for group in range(groups):
            cells = mine[:, group * rows : (group + 1) * rows].reshape(tile_rows, depth).astype(BF16)
            lines_ref[group, tile * tile_rows : (tile + 1) * tile_rows] = cells
    for chunk in range(chunks):
        lhs = lines_ref[:, chunk * LANES : (chunk + 1) * LANES].reshape(groups * LANES, depth)
        for r in range(ranks):
            got = jnp.dot(lhs, column_ref[r], preferred_element_type=F32).astype(BF16)
            for group in range(groups):
                block, comp = divmod(group, comps)
                at = comp * width + block * LANES
                for part in range(2):
                    passed_ref[chunk, (2 * r + part) * LANES : (2 * r + part + 1) * LANES, at : at + LANES] = (
                        got[group * LANES : (group + 1) * LANES, part * LANES : (part + 1) * LANES]
                    )
    for chunk in range(chunks):
        total = None
        for w in range(row_ref.shape[0]):
            other = chunk + w - row_ref.shape[0] // 2
            if 0 <= other < chunks:
                term = jnp.dot(row_ref[w], passed_ref[other], preferred_element_type=F32)
                total = term if total is None else total + term
        square = total * total
        square = square[:LANES] + square[LANES:]
        power = square[:, :width]
        for comp in range(1, comps):
            power = power + square[:, comp * width : (comp + 1) * width]
        power = power * weight_ref[0]
        for piece in range(LANES // rows):
            tile, source = divmod((chunk * LANES) // rows + piece, sources)
            out_ref[source, tile] = power[piece * rows : (piece + 1) * rows]


def per_device(near_field, x_taps, y_taps, source_weight):
    sources, tiles = lax.axis_size("src"), lax.axis_size("tile")
    _, rows, _, comps, width = near_field.shape
    ranks, taps = x_taps.shape[-2:]
    rim = (taps - 1) // 2
    half_width = width // tiles
    groups = half_width // LANES * comps
    depth = 2 * LANES + 4 * rim
    chunks = sources * tiles * rows // LANES
    windows = 1 if chunks == 1 else 3
    params = pltpu.CompilerParams(vmem_limit_bytes=48 * 1024 * 1024)
    whole = pl.BlockSpec(memory_space=pltpu.VMEM)

    send = pl.pallas_call(
        functools.partial(send_kernel, rim),
        out_shape=jax.ShapeDtypeStruct((sources, tiles, groups * rows, depth), BF16),
        in_specs=[whole],
        out_specs=whole,
        compiler_params=params,
        name="send_layout",
    )(near_field)
    got = lax.all_to_all(
        send.reshape(sources * tiles, groups * rows, depth), ("src", "tile"), 0, 0
    ).reshape(send.shape)

    column_mats, row_mats = pl.pallas_call(
        functools.partial(band_kernel, rim),
        out_shape=(
            jax.ShapeDtypeStruct((ranks, depth, 2 * LANES), BF16),
            jax.ShapeDtypeStruct((windows, 2 * LANES, 2 * ranks * LANES), BF16),
        ),
        in_specs=[whole, whole],
        out_specs=(whole, whole),
        compiler_params=params,
        name="band_matrices",
    )(x_taps, y_taps)

    power = pl.pallas_call(
        functools.partial(image_kernel, comps),
        out_shape=jax.ShapeDtypeStruct((sources, tiles, rows, half_width), F32),
        in_specs=[whole, whole, whole, pl.BlockSpec(memory_space=pltpu.SMEM)],
        out_specs=whole,
        scratch_shapes=[
            pltpu.VMEM((groups, chunks * LANES, depth), BF16),
            pltpu.VMEM((chunks, 2 * ranks * LANES, comps * half_width), BF16),
        ],
        compiler_params=params,
        name="image",
    )(got, column_mats, row_mats, source_weight)
    parts = lax.all_to_all(
        power.reshape(sources * tiles, rows, half_width), ("src", "tile"), 0, 0
    ).reshape(power.shape)
    summed = jnp.sum(parts, axis=0)
    return summed.transpose(1, 0, 2).reshape(1, rows, width)


def solution(mesh):
    placed = (
        P(("group", "tile"), "src", None, None, None),
        P("src", None, None, None),
        P("src", None, None, None),
        P("src"),
    )
    return jax.shard_map(
        per_device,
        mesh=mesh,
        in_specs=placed,
        out_specs=P(("group", "tile"), "src", None),
        check_vma=False,
    )
```

```python
import functools

import jax
import jax.numpy as jnp
from jax import lax
from jax.experimental import pallas as pl
from jax.experimental.pallas import tpu as pltpu
from jax.sharding import PartitionSpec as P

LANES = 128
F32 = jnp.float32
BF16 = jnp.bfloat16


def half_kernel(rim, tiles, field_ref, mine_ref, theirs_ref):
    _, _, comps, _, width = field_ref.shape
    rows = field_ref.shape[1]
    half_width = width // tiles
    field = field_ref[0].astype(F32)
    edge = jnp.zeros((rows, rim), F32)
    halves = []
    for half in range(tiles):
        first, last = half * half_width, (half + 1) * half_width
        groups = []
        for comp in range(comps):
            mains, rims = [], []
            for part in range(2):
                plane = field[:, comp, part, :]
                mains.append(plane[:, first:last])
                rims.append(plane[:, first - rim : first] if first > 0 else edge)
                rims.append(plane[:, last : last + rim] if last < width else edge)
            groups.append(jnp.concatenate(mains + rims, axis=1))
        halves.append(jnp.concatenate(groups, axis=0))
    lower = lax.axis_index("tile") == 0
    mine_ref[...] = jnp.where(lower, halves[0], halves[1]).astype(BF16)
    theirs_ref[...] = jnp.where(lower, halves[1], halves[0]).astype(BF16)


def rolled(line):
    return pltpu.roll(jnp.broadcast_to(line, (LANES, LANES)), 0, 1, stride=1, stride_axis=0)


def band_kernel(rim, x_taps_ref, y_taps_ref, column_ref, row_ref):
    _, _, ranks, taps = x_taps_ref.shape
    tap = lax.broadcasted_iota(jnp.int32, (taps, LANES), 0)
    lane = lax.broadcasted_iota(jnp.int32, (taps, LANES), 1)
    x_place = (lane == (rim - tap) % LANES).astype(BF16)
    y_place = (lane == (tap - rim) % LANES).astype(BF16)
    i = lax.broadcasted_iota(jnp.int32, (LANES, LANES), 0)
    j = lax.broadcasted_iota(jnp.int32, (LANES, LANES), 1)
    near = jnp.abs(i - j) < LANES // 2
    x_lines = [jnp.dot(x_taps_ref[0, part], x_place, preferred_element_type=F32) for part in range(2)]
    y_lines = [jnp.dot(y_taps_ref[0, part], y_place, preferred_element_type=F32) for part in range(2)]
    half_lanes = LANES // 2
    for r in range(ranks):
        re, im = (rolled(lines[r : r + 1]) for lines in x_lines)

        def columns(of_re, of_im):
            parts = [jnp.where(near, of_re, 0.0), jnp.where(near, of_im, 0.0)]
            for ring in (of_re, of_im):
                parts.append(jnp.where(j[LANES - rim :] < half_lanes, ring[LANES - rim :], 0.0))
                parts.append(jnp.where(j[:rim] >= half_lanes, ring[:rim], 0.0))
            return jnp.concatenate(parts, axis=0).astype(BF16)

        column_ref[r, :, :LANES] = columns(re, -im)
        column_ref[r, :, LANES:] = columns(im, re)

        re, im = (rolled(lines[r : r + 1]) for lines in y_lines)
        masks = [near] if row_ref.shape[0] == 1 else [j - i > half_lanes, near, j - i < -half_lanes]
        for w, mask in enumerate(masks):
            re_w, im_w = (jnp.where(mask, re, 0.0), jnp.where(mask, im, 0.0))
            at = 2 * r * LANES
            row_ref[w, :LANES, at : at + LANES] = re_w.astype(BF16)
            row_ref[w, :LANES, at + LANES : at + 2 * LANES] = (-im_w).astype(BF16)
            row_ref[w, LANES:, at : at + LANES] = im_w.astype(BF16)
            row_ref[w, LANES:, at + LANES : at + 2 * LANES] = re_w.astype(BF16)


def image_kernel(rim, steps, comps, *refs):
    pieces = refs[: len(steps)]
    column_ref, row_ref, weight_ref, out_ref, lines_ref, passed_ref = refs[len(steps) :]
    sources, tiles, rows, width = out_ref.shape
    ranks = column_ref.shape[0]
    blocks = width // LANES
    tile_rows = sources * rows
    chunks = tiles * tile_rows // LANES
    me = lax.axis_index("src")
    for step, piece in zip(steps, pieces):
        source = jnp.bitwise_xor(me, step)
        for tile in range(tiles):
            cells = piece[tile].astype(F32)
            for comp in range(comps):
                at = pl.multiple_of(tile * tile_rows + source * rows, rows)
                lines_ref[comp, pl.ds(at, rows), :] = cells[comp * rows : (comp + 1) * rows]
    for chunk in range(chunks):
        windows = []
        for block in range(blocks):
            first, last = block * LANES, (block + 1) * LANES
            for comp in range(comps):
                cells = lines_ref[comp, chunk * LANES : (chunk + 1) * LANES, :]
                mains, rims = [], []
                for part in range(2):
                    plane = cells[:, part * width : (part + 1) * width]
                    halo = 2 * width + 2 * part * rim
                    mains.append(plane[:, first:last])
                    rims.append(plane[:, first - rim : first] if block > 0 else cells[:, halo : halo + rim])
                    rims.append(
                        plane[:, last : last + rim] if last < width else cells[:, halo + rim : halo + 2 * rim]
                    )
                windows.append(jnp.concatenate(mains + rims, axis=1).astype(BF16))
        lhs = jnp.concatenate(windows, axis=0)
        for r in range(ranks):
            got = jnp.dot(lhs, column_ref[r], preferred_element_type=F32).astype(BF16)
            for group in range(blocks * comps):
                block, comp = divmod(group, comps)
                at = comp * width + block * LANES
                for part in range(2):
                    passed_ref[chunk, (2 * r + part) * LANES : (2 * r + part + 1) * LANES, at : at + LANES] = (
                        got[group * LANES : (group + 1) * LANES, part * LANES : (part + 1) * LANES]
                    )
    for chunk in range(chunks):
        total = None
        for w in range(row_ref.shape[0]):
            other = chunk + w - row_ref.shape[0] // 2
            if 0 <= other < chunks:
                term = jnp.dot(row_ref[w], passed_ref[other], preferred_element_type=F32)
                total = term if total is None else total + term
        square = total * total
        square = square[:LANES] + square[LANES:]
        power = square[:, :width]
        for comp in range(1, comps):
            power = power + square[:, comp * width : (comp + 1) * width]
        power = power * weight_ref[0]
        for piece in range(LANES // rows):
            tile, source = divmod((chunk * LANES) // rows + piece, sources)
            out_ref[source, tile] = power[piece * rows : (piece + 1) * rows]


def per_device(near_field, x_taps, y_taps, source_weight):
    sources, tiles = lax.axis_size("src"), lax.axis_size("tile")
    _, rows, _, comps, width = near_field.shape
    ranks, taps = x_taps.shape[-2:]
    rim = (taps - 1) // 2
    half_width = width // tiles
    depth = 2 * LANES + 4 * rim
    held = 2 * half_width + 4 * rim
    chunks = sources * tiles * rows // LANES
    windows = 1 if chunks == 1 else 3
    params = pltpu.CompilerParams(vmem_limit_bytes=48 * 1024 * 1024)
    whole = pl.BlockSpec(memory_space=pltpu.VMEM)

    half = jax.ShapeDtypeStruct((comps * rows, held), BF16)
    mine, theirs = pl.pallas_call(
        functools.partial(half_kernel, rim, tiles),
        out_shape=(half, half),
        in_specs=[whole],
        out_specs=(whole, whole),
        compiler_params=params,
        name="column_halves",
    )(near_field.transpose(0, 1, 3, 2, 4))
    other = lax.ppermute(theirs, "tile", [(0, 1), (1, 0)])
    lower = lax.axis_index("tile") == 0
    own = jnp.stack([jnp.where(lower, mine, other), jnp.where(lower, other, mine)])
    steps = sorted(range(1, sources), key=lambda d: (-(d // 2 > 1), d % 2, d))
    pieces = [lax.ppermute(own, "src", [(i, i ^ d) for i in range(sources)]) for d in steps]

    column_mats, row_mats = pl.pallas_call(
        functools.partial(band_kernel, rim),
        out_shape=(
            jax.ShapeDtypeStruct((ranks, depth, 2 * LANES), BF16),
            jax.ShapeDtypeStruct((windows, 2 * LANES, 2 * ranks * LANES), BF16),
        ),
        in_specs=[whole, whole],
        out_specs=(whole, whole),
        compiler_params=params,
        name="band_matrices",
    )(x_taps, y_taps)

    power = pl.pallas_call(
        functools.partial(image_kernel, rim, [0] + steps, comps),
        out_shape=jax.ShapeDtypeStruct((sources, tiles, rows, half_width), F32),
        in_specs=[whole] * (sources + 2) + [pl.BlockSpec(memory_space=pltpu.SMEM)],
        out_specs=whole,
        scratch_shapes=[
            pltpu.VMEM((comps, chunks * LANES, held), F32),
            pltpu.VMEM((chunks, 2 * ranks * LANES, comps * half_width), BF16),
        ],
        compiler_params=params,
        name="image",
    )(own, *pieces, column_mats, row_mats, source_weight)
    parts = lax.all_to_all(
        power.reshape(sources * tiles, rows, half_width), ("src", "tile"), 0, 0
    ).reshape(power.shape)
    summed = jnp.sum(parts, axis=0)
    return summed.transpose(1, 0, 2).reshape(1, rows, width)


def solution(mesh):
    placed = (
        P(("group", "tile"), "src", None, None, None),
        P("src", None, None, None),
        P("src", None, None, None),
        P("src"),
    )
    return jax.shard_map(
        per_device,
        mesh=mesh,
        in_specs=placed,
        out_specs=P(("group", "tile"), "src", None),
        check_vma=False,
    )
```

```python
import functools

import jax
import jax.numpy as jnp
from jax import lax
from jax.experimental import pallas as pl
from jax.experimental.pallas import tpu as pltpu
from jax.sharding import PartitionSpec as P

LANES = 128
F32 = jnp.float32
BF16 = jnp.bfloat16


def half_kernel(rim, tiles, field_ref, x_taps_ref, y_taps_ref, mine_ref, theirs_ref, lines_ref):
    _, _, comps, _, width = field_ref.shape
    rows = field_ref.shape[1]
    half_width = width // tiles
    field = field_ref[0].astype(F32)
    edge = jnp.zeros((rows, rim), F32)
    halves = []
    for half in range(tiles):
        first, last = half * half_width, (half + 1) * half_width
        groups = []
        for comp in range(comps):
            mains, rims = [], []
            for part in range(2):
                plane = field[:, comp, part, :]
                mains.append(plane[:, first:last])
                rims.append(plane[:, first - rim : first] if first > 0 else edge)
                rims.append(plane[:, last : last + rim] if last < width else edge)
            groups.append(jnp.concatenate(mains + rims, axis=1))
        halves.append(jnp.concatenate(groups, axis=0))
    lower = lax.axis_index("tile") == 0
    mine_ref[...] = jnp.where(lower, halves[0], halves[1]).astype(BF16)
    theirs_ref[...] = jnp.where(lower, halves[1], halves[0]).astype(BF16)
    taps = x_taps_ref.shape[-1]
    tap = lax.broadcasted_iota(jnp.int32, (taps, LANES), 0)
    lane = lax.broadcasted_iota(jnp.int32, (taps, LANES), 1)
    x_place = (lane == (rim - tap) % LANES).astype(BF16)
    y_place = (lane == (tap - rim) % LANES).astype(BF16)
    for part in range(2):
        lines_ref[part] = jnp.dot(x_taps_ref[0, part], x_place, preferred_element_type=F32)
        lines_ref[2 + part] = jnp.dot(y_taps_ref[0, part], y_place, preferred_element_type=F32)


def rolled(line):
    return pltpu.roll(jnp.broadcast_to(line, (LANES, LANES)), 0, 1, stride=1, stride_axis=0)


def band_kernel(rim, lines_ref, column_ref, row_ref):
    ranks = lines_ref.shape[1]
    i = lax.broadcasted_iota(jnp.int32, (LANES, LANES), 0)
    j = lax.broadcasted_iota(jnp.int32, (LANES, LANES), 1)
    near = jnp.abs(i - j) < LANES // 2
    x_lines, y_lines = (lines_ref[0], lines_ref[1]), (lines_ref[2], lines_ref[3])
    half_lanes = LANES // 2
    for r in range(ranks):
        re, im = (rolled(lines[r : r + 1]) for lines in x_lines)

        def columns(of_re, of_im):
            parts = [jnp.where(near, of_re, 0.0), jnp.where(near, of_im, 0.0)]
            for ring in (of_re, of_im):
                parts.append(jnp.where(j[LANES - rim :] < half_lanes, ring[LANES - rim :], 0.0))
                parts.append(jnp.where(j[:rim] >= half_lanes, ring[:rim], 0.0))
            return jnp.concatenate(parts, axis=0).astype(BF16)

        column_ref[r, :, :LANES] = columns(re, -im)
        column_ref[r, :, LANES:] = columns(im, re)

        re, im = (rolled(lines[r : r + 1]) for lines in y_lines)
        masks = [near] if row_ref.shape[0] == 1 else [j - i > half_lanes, near, j - i < -half_lanes]
        for w, mask in enumerate(masks):
            re_w, im_w = (jnp.where(mask, re, 0.0), jnp.where(mask, im, 0.0))
            at = 2 * r * LANES
            row_ref[w, :LANES, at : at + LANES] = re_w.astype(BF16)
            row_ref[w, :LANES, at + LANES : at + 2 * LANES] = (-im_w).astype(BF16)
            row_ref[w, LANES:, at : at + LANES] = im_w.astype(BF16)
            row_ref[w, LANES:, at + LANES : at + 2 * LANES] = re_w.astype(BF16)


def image_kernel(rim, steps, comps, *refs):
    pieces = refs[: len(steps)]
    column_ref, row_ref, weight_ref, out_ref, lines_ref, passed_ref = refs[len(steps) :]
    sources, tiles, rows, width = out_ref.shape
    ranks = column_ref.shape[0]
    blocks = width // LANES
    tile_rows = sources * rows
    chunks = tiles * tile_rows // LANES
    me = lax.axis_index("src")
    for step, piece in zip(steps, pieces):
        source = jnp.bitwise_xor(me, step)
        for tile in range(tiles):
            cells = piece[tile].astype(F32)
            for comp in range(comps):
                at = pl.multiple_of(tile * tile_rows + source * rows, rows)
                lines_ref[comp, pl.ds(at, rows), :] = cells[comp * rows : (comp + 1) * rows]
    for chunk in range(chunks):
        windows = []
        for block in range(blocks):
            first, last = block * LANES, (block + 1) * LANES
            for comp in range(comps):
                cells = lines_ref[comp, chunk * LANES : (chunk + 1) * LANES, :]
                mains, rims = [], []
                for part in range(2):
                    plane = cells[:, part * width : (part + 1) * width]
                    halo = 2 * width + 2 * part * rim
                    mains.append(plane[:, first:last])
                    rims.append(plane[:, first - rim : first] if block > 0 else cells[:, halo : halo + rim])
                    rims.append(
                        plane[:, last : last + rim] if last < width else cells[:, halo + rim : halo + 2 * rim]
                    )
                windows.append(jnp.concatenate(mains + rims, axis=1).astype(BF16))
        lhs = jnp.concatenate(windows, axis=0)
        for r in range(ranks):
            got = jnp.dot(lhs, column_ref[r], preferred_element_type=F32).astype(BF16)
            for group in range(blocks * comps):
                block, comp = divmod(group, comps)
                at = comp * width + block * LANES
                for part in range(2):
                    passed_ref[chunk, (2 * r + part) * LANES : (2 * r + part + 1) * LANES, at : at + LANES] = (
                        got[group * LANES : (group + 1) * LANES, part * LANES : (part + 1) * LANES]
                    )
    for chunk in range(chunks):
        total = None
        for w in range(row_ref.shape[0]):
            other = chunk + w - row_ref.shape[0] // 2
            if 0 <= other < chunks:
                term = jnp.dot(row_ref[w], passed_ref[other], preferred_element_type=F32)
                total = term if total is None else total + term
        square = total * total
        square = square[:LANES] + square[LANES:]
        power = square[:, :width]
        for comp in range(1, comps):
            power = power + square[:, comp * width : (comp + 1) * width]
        power = power * weight_ref[0]
        for piece in range(LANES // rows):
            tile, source = divmod((chunk * LANES) // rows + piece, sources)
            out_ref[source, tile] = power[piece * rows : (piece + 1) * rows]


def per_device(near_field, x_taps, y_taps, source_weight):
    sources, tiles = lax.axis_size("src"), lax.axis_size("tile")
    _, rows, _, comps, width = near_field.shape
    ranks, taps = x_taps.shape[-2:]
    rim = (taps - 1) // 2
    half_width = width // tiles
    depth = 2 * LANES + 4 * rim
    held = 2 * half_width + 4 * rim
    chunks = sources * tiles * rows // LANES
    windows = 1 if chunks == 1 else 3
    params = pltpu.CompilerParams(vmem_limit_bytes=48 * 1024 * 1024)
    whole = pl.BlockSpec(memory_space=pltpu.VMEM)

    half = jax.ShapeDtypeStruct((comps * rows, held), BF16)
    mine, theirs, lines = pl.pallas_call(
        functools.partial(half_kernel, rim, tiles),
        out_shape=(half, half, jax.ShapeDtypeStruct((4, ranks, LANES), F32)),
        in_specs=[whole] * 3,
        out_specs=(whole,) * 3,
        compiler_params=params,
        name="column_halves",
    )(near_field.transpose(0, 1, 3, 2, 4), x_taps, y_taps)
    other = lax.ppermute(theirs, "tile", [(0, 1), (1, 0)])
    column_mats, row_mats = pl.pallas_call(
        functools.partial(band_kernel, rim),
        out_shape=(
            jax.ShapeDtypeStruct((ranks, depth, 2 * LANES), BF16),
            jax.ShapeDtypeStruct((windows, 2 * LANES, 2 * ranks * LANES), BF16),
        ),
        in_specs=[whole],
        out_specs=(whole, whole),
        compiler_params=params,
        name="band_matrices",
    )(lines)
    other, column_mats, row_mats = lax.optimization_barrier((other, column_mats, row_mats))
    lower = lax.axis_index("tile") == 0
    own = jnp.stack([jnp.where(lower, mine, other), jnp.where(lower, other, mine)])

    def swapped(piece, step):
        return lax.ppermute(piece, "src", [(i, i ^ step) for i in range(sources)])

    far = [d for d in range(4, sources, 2)] + [2]
    held_by_step = {0: own}
    for step in far:
        held_by_step[step] = swapped(own, step)
    for step in [0] + far:
        held_by_step[step + 1] = swapped(held_by_step[step], 1)
    steps = sorted(held_by_step)
    pieces = [held_by_step[step] for step in steps]

    power = pl.pallas_call(
        functools.partial(image_kernel, rim, steps, comps),
        out_shape=jax.ShapeDtypeStruct((sources, tiles, rows, half_width), F32),
        in_specs=[whole] * (sources + 2) + [pl.BlockSpec(memory_space=pltpu.SMEM)],
        out_specs=whole,
        scratch_shapes=[
            pltpu.VMEM((comps, chunks * LANES, held), F32),
            pltpu.VMEM((chunks, 2 * ranks * LANES, comps * half_width), BF16),
        ],
        compiler_params=params,
        name="image",
    )(*pieces, column_mats, row_mats, source_weight)
    parts = lax.all_to_all(
        power.reshape(sources * tiles, rows, half_width), ("src", "tile"), 0, 0
    ).reshape(power.shape)
    summed = jnp.sum(parts, axis=0)
    return summed.transpose(1, 0, 2).reshape(1, rows, width)


def solution(mesh):
    placed = (
        P(("group", "tile"), "src", None, None, None),
        P("src", None, None, None),
        P("src", None, None, None),
        P("src"),
    )
    return jax.shard_map(
        per_device,
        mesh=mesh,
        in_specs=placed,
        out_specs=P(("group", "tile"), "src", None),
        check_vma=False,
    )
```

```python
import functools

import jax
import jax.numpy as jnp
from jax import lax
from jax.experimental import pallas as pl
from jax.experimental.pallas import tpu as pltpu
from jax.sharding import PartitionSpec as P

LANES = 128
F32 = jnp.float32
BF16 = jnp.bfloat16


def half_kernel(
    rim, tiles, field_hbm, x_taps_hbm, y_taps_hbm, mine_ref, theirs_ref, lines_ref, field_ref, x_taps_ref, y_taps_ref, sems
):
    copies = [
        pltpu.make_async_copy(source, target, sems.at[k])
        for k, (source, target) in enumerate(
            ((field_hbm, field_ref), (x_taps_hbm, x_taps_ref), (y_taps_hbm, y_taps_ref))
        )
    ]
    for copy in copies:
        copy.start()
    copies[0].wait()
    comps, width = field_ref.shape[2], field_ref.shape[4]
    half_width = width // tiles
    field = field_ref[0].astype(F32)
    halves = []
    for half in range(tiles):
        first, last = half * half_width, (half + 1) * half_width
        inner = last if half == 0 else first - rim
        groups = []
        for comp in range(comps):
            planes = [field[:, comp, part, :] for part in range(2)]
            cells = [plane[:, first:last] for plane in planes] + [plane[:, inner : inner + rim] for plane in planes]
            groups.append(jnp.concatenate(cells, axis=1))
        halves.append(jnp.concatenate(groups, axis=0))
    lower = lax.axis_index("tile") == 0
    mine_ref[...] = jnp.where(lower, halves[0], halves[1]).astype(BF16)
    theirs_ref[...] = jnp.where(lower, halves[1], halves[0]).astype(BF16)
    copies[1].wait()
    copies[2].wait()
    taps = x_taps_ref.shape[-1]
    tap = lax.broadcasted_iota(jnp.int32, (taps, LANES), 0)
    lane = lax.broadcasted_iota(jnp.int32, (taps, LANES), 1)
    x_place = (lane == (rim - tap) % LANES).astype(BF16)
    y_place = (lane == (tap - rim) % LANES).astype(BF16)
    for part in range(2):
        lines_ref[part] = jnp.dot(x_taps_ref[0, part], x_place, preferred_element_type=F32)
        lines_ref[2 + part] = jnp.dot(y_taps_ref[0, part], y_place, preferred_element_type=F32)


def join_kernel(inner, mine_ref, other_ref, own_ref):
    lower = lax.axis_index("tile") == 0
    mine, other = mine_ref[...].astype(F32), other_ref[...].astype(F32)
    cells = [jnp.where(lower, mine, other), jnp.where(lower, other, mine)]
    main = mine.shape[1] - inner
    own_ref[...] = jnp.concatenate([c[:, :main] for c in cells] + [c[:, main:] for c in cells], axis=1).astype(BF16)


def rolled(line):
    return pltpu.roll(jnp.broadcast_to(line, (LANES, LANES)), 0, 1, stride=1, stride_axis=0)


def band_kernel(rim, lines_ref, column_ref, row_ref):
    ranks = lines_ref.shape[1]
    i = lax.broadcasted_iota(jnp.int32, (LANES, LANES), 0)
    j = lax.broadcasted_iota(jnp.int32, (LANES, LANES), 1)
    near = jnp.abs(i - j) < LANES // 2
    x_lines, y_lines = (lines_ref[0], lines_ref[1]), (lines_ref[2], lines_ref[3])
    half_lanes = LANES // 2
    for r in range(ranks):
        re, im = (rolled(lines[r : r + 1]) for lines in x_lines)

        def columns(of_re, of_im):
            parts = [jnp.where(near, of_re, 0.0), jnp.where(near, of_im, 0.0)]
            for ring in (of_re, of_im):
                parts.append(jnp.where(j[LANES - rim :] < half_lanes, ring[LANES - rim :], 0.0))
                parts.append(jnp.where(j[:rim] >= half_lanes, ring[:rim], 0.0))
            return jnp.concatenate(parts, axis=0).astype(BF16)

        column_ref[r, :, :LANES] = columns(re, -im)
        column_ref[r, :, LANES:] = columns(im, re)

        re, im = (rolled(lines[r : r + 1]) for lines in y_lines)
        masks = [near] if row_ref.shape[0] == 1 else [j - i > half_lanes, near, j - i < -half_lanes]
        for w, mask in enumerate(masks):
            re_w, im_w = (jnp.where(mask, re, 0.0), jnp.where(mask, im, 0.0))
            at = 2 * r * LANES
            row_ref[w, :LANES, at : at + LANES] = re_w.astype(BF16)
            row_ref[w, :LANES, at + LANES : at + 2 * LANES] = (-im_w).astype(BF16)
            row_ref[w, LANES:, at : at + LANES] = im_w.astype(BF16)
            row_ref[w, LANES:, at + LANES : at + 2 * LANES] = re_w.astype(BF16)


def image_kernel(rim, steps, far, comps, tiles, rows, *refs):
    pieces = refs[: len(steps)]
    column_ref, row_ref, weight_ref = refs[len(steps) : len(steps) + 3]
    outs = refs[len(steps) + 3 : len(steps) + 3 + len(far)]
    lines_ref, passed_ref, power_ref = refs[len(steps) + 3 + len(far) :]
    width = power_ref.shape[1]
    ranks = column_ref.shape[0]
    blocks = width // LANES
    tile_rows = len(steps) * rows
    chunks = tiles * tile_rows // LANES
    me = lax.axis_index("src")
    lower = lax.axis_index("tile") == 0
    for step, piece in zip(steps, pieces):
        cells = piece[...].astype(F32)
        for tile in range(tiles):
            at = pl.multiple_of(tile * tile_rows + jnp.bitwise_xor(me, step) * rows, rows)
            main, halo = 2 * width * tile, 2 * (width * tiles + rim * tile)
            for comp in range(comps):
                some = cells[comp * rows : (comp + 1) * rows]
                lines_ref[comp, pl.ds(at, rows), : 2 * width] = some[:, main : main + 2 * width]
                lines_ref[comp, pl.ds(at, rows), 2 * width :] = some[:, halo : halo + 2 * rim]
    for chunk in range(chunks):
        windows = []
        for block in range(blocks):
            first, last = block * LANES, (block + 1) * LANES
            for comp in range(comps):
                cells = lines_ref[comp, chunk * LANES : (chunk + 1) * LANES, :]
                mains, rims = [], []
                for part in range(2):
                    plane = cells[:, part * width : (part + 1) * width]
                    halo = cells[:, 2 * width + part * rim : 2 * width + (part + 1) * rim]
                    mains.append(plane[:, first:last])
                    rims.append(plane[:, first - rim : first] if block > 0 else jnp.where(lower, 0.0, halo))
                    rims.append(plane[:, last : last + rim] if last < width else jnp.where(lower, halo, 0.0))
                windows.append(jnp.concatenate(mains + rims, axis=1).astype(BF16))
        lhs = jnp.concatenate(windows, axis=0)
        for r in range(ranks):
            got = jnp.dot(lhs, column_ref[r], preferred_element_type=F32).astype(BF16)
            for group in range(blocks * comps):
                block, comp = divmod(group, comps)
                at = comp * width + block * LANES
                for part in range(2):
                    passed_ref[chunk, (2 * r + part) * LANES : (2 * r + part + 1) * LANES, at : at + LANES] = (
                        got[group * LANES : (group + 1) * LANES, part * LANES : (part + 1) * LANES]
                    )
    for chunk in range(chunks):
        total = None
        for w in range(row_ref.shape[0]):
            other = chunk + w - row_ref.shape[0] // 2
            if 0 <= other < chunks:
                term = jnp.dot(row_ref[w], passed_ref[other], preferred_element_type=F32)
                total = term if total is None else total + term
        square = total * total
        square = square[:LANES] + square[LANES:]
        power = square[:, :width]
        for comp in range(1, comps):
            power = power + square[:, comp * width : (comp + 1) * width]
        power_ref[chunk * LANES : (chunk + 1) * LANES, :] = power * weight_ref[0]
    for step, out_ref in zip(far, outs):
        for side in range(2):
            owner = jnp.bitwise_xor(me, step + side)
            for tile in range(tiles):
                at = pl.multiple_of(tile * tile_rows + owner * rows, rows)
                out_ref[side, tile] = power_ref[pl.ds(at, rows), :]


def first_sum_kernel(*refs):
    terms, (keep_ref, pass_ref) = refs[:-2], refs[-2:]
    total = terms[0][...]
    for term in terms[1:]:
        total = total + term[...]
    keep_ref[...] = total[0]
    pass_ref[...] = total[1]


def second_sum_kernel(keep_ref, got_ref, mine_ref, theirs_ref):
    total = keep_ref[...] + got_ref[...]
    lower = lax.axis_index("tile") == 0
    mine_ref[...] = jnp.where(lower, total[0], total[1])
    theirs_ref[...] = jnp.where(lower, total[1], total[0])


def merge_kernel(mine_ref, other_ref, out_ref):
    width = mine_ref.shape[1]
    lower = lax.axis_index("tile") == 0
    mine, other = mine_ref[...], other_ref[...]
    out_ref[0, :, :width] = jnp.where(lower, mine, other)
    out_ref[0, :, width:] = jnp.where(lower, other, mine)


def per_device(near_field, x_taps, y_taps, source_weight):
    sources, tiles = lax.axis_size("src"), lax.axis_size("tile")
    _, rows, _, comps, width = near_field.shape
    ranks, taps = x_taps.shape[-2:]
    rim = (taps - 1) // 2
    half_width = width // tiles
    depth = 2 * LANES + 4 * rim
    held = 2 * half_width + 2 * rim
    chunks = sources * tiles * rows // LANES
    windows = 1 if chunks == 1 else 3
    params = pltpu.CompilerParams(vmem_limit_bytes=48 * 1024 * 1024)
    whole = pl.BlockSpec(memory_space=pltpu.VMEM)

    half = jax.ShapeDtypeStruct((comps * rows, held), BF16)
    mine, theirs, lines = pl.pallas_call(
        functools.partial(half_kernel, rim, tiles),
        out_shape=(half, half, jax.ShapeDtypeStruct((4, ranks, LANES), F32)),
        in_specs=[pl.BlockSpec(memory_space=pltpu.HBM)] * 3,
        out_specs=(whole,) * 3,
        scratch_shapes=[
            pltpu.VMEM((1, rows, comps, 2, width), BF16),
            pltpu.VMEM(x_taps.shape, BF16),
            pltpu.VMEM(y_taps.shape, BF16),
            pltpu.SemaphoreType.DMA((3,)),
        ],
        compiler_params=params,
        name="column_halves",
    )(near_field.transpose(0, 1, 3, 2, 4), x_taps, y_taps)
    other = lax.ppermute(theirs, "tile", [(0, 1), (1, 0)])
    column_mats, row_mats = pl.pallas_call(
        functools.partial(band_kernel, rim),
        out_shape=(
            jax.ShapeDtypeStruct((ranks, depth, 2 * LANES), BF16),
            jax.ShapeDtypeStruct((windows, 2 * LANES, 2 * ranks * LANES), BF16),
        ),
        in_specs=[whole],
        out_specs=(whole, whole),
        compiler_params=params,
        name="band_matrices",
    )(lines)
    other, column_mats, row_mats = lax.optimization_barrier((other, column_mats, row_mats))

    def call(kernel, name, out_shape, *operands):
        many = isinstance(out_shape, tuple)
        return pl.pallas_call(
            kernel,
            out_shape=out_shape,
            in_specs=[whole] * len(operands),
            out_specs=(whole,) * len(out_shape) if many else whole,
            compiler_params=params,
            name=name,
        )(*operands)

    own = call(
        functools.partial(join_kernel, 2 * rim),
        "join_cores",
        jax.ShapeDtypeStruct((comps * rows, tiles * held), BF16),
        mine,
        other,
    )

    def swapped(piece, step):
        return lax.ppermute(piece, "src", [(i, i ^ step) for i in range(sources)])

    far = [d for d in range(4, sources, 2)] + [2]
    held_by_step = {0: own}
    for step in far:
        held_by_step[step] = swapped(own, step)
    for step in [0] + far:
        held_by_step[step + 1] = swapped(held_by_step[step], 1)
    steps = sorted(held_by_step)
    pieces = [held_by_step[step] for step in steps]

    targets = [0] + far
    block = jax.ShapeDtypeStruct((2, tiles, rows, half_width), F32)
    powers = pl.pallas_call(
        functools.partial(image_kernel, rim, steps, targets, comps, tiles, rows),
        out_shape=(block,) * len(targets),
        in_specs=[whole] * (sources + 2) + [pl.BlockSpec(memory_space=pltpu.SMEM)],
        out_specs=(whole,) * len(targets),
        scratch_shapes=[
            pltpu.VMEM((comps, chunks * LANES, held), F32),
            pltpu.VMEM((chunks, 2 * ranks * LANES, comps * half_width), BF16),
            pltpu.VMEM((chunks * LANES, half_width), F32),
        ],
        compiler_params=params,
        name="image",
    )(*pieces, column_mats, row_mats, source_weight)
    terms = [powers[0]] + [swapped(power, step) for power, step in zip(powers[1:], far)]
    pair = jax.ShapeDtypeStruct((tiles, rows, half_width), F32)
    keep, passed_on = call(first_sum_kernel, "sum_far", (pair, pair), *terms)
    single = jax.ShapeDtypeStruct((rows, half_width), F32)
    mine, theirs = call(second_sum_kernel, "sum_near", (single, single), keep, swapped(passed_on, 1))
    other = lax.ppermute(theirs, "tile", [(0, 1), (1, 0)])
    return call(merge_kernel, "merge_halves", jax.ShapeDtypeStruct((1, rows, width), F32), mine, other)


def solution(mesh):
    placed = (
        P(("group", "tile"), "src", None, None, None),
        P("src", None, None, None),
        P("src", None, None, None),
        P("src"),
    )
    return jax.shard_map(
        per_device,
        mesh=mesh,
        in_specs=placed,
        out_specs=P(("group", "tile"), "src", None),
        check_vma=False,
    )
```

```python
import functools

import jax
import jax.numpy as jnp
from jax import lax
from jax.experimental import pallas as pl
from jax.experimental.pallas import tpu as pltpu
from jax.sharding import PartitionSpec as P

LANES = 128
F32 = jnp.float32
BF16 = jnp.bfloat16


def halves_kernel(rim, tiles, *refs):
    pieces, (mine_ref, theirs_ref) = refs[:-2], refs[-2:]
    lower = lax.axis_index("tile") == 0
    for k, piece in enumerate(pieces):
        _, _, comps, _, width = piece.shape
        half_width = width // tiles
        field = piece[0].astype(F32)
        halves = []
        for half in range(tiles):
            first, last = half * half_width, (half + 1) * half_width
            inner = last if half == 0 else first - rim
            groups = []
            for comp in range(comps):
                planes = [field[:, comp, part, :] for part in range(2)]
                cells = [plane[:, first:last] for plane in planes] + [plane[:, inner : inner + rim] for plane in planes]
                groups.append(jnp.concatenate(cells, axis=1))
            halves.append(jnp.concatenate(groups, axis=0))
        mine_ref[k] = jnp.where(lower, halves[0], halves[1]).astype(BF16)
        theirs_ref[k] = jnp.where(lower, halves[1], halves[0]).astype(BF16)


def rolled(line):
    return pltpu.roll(jnp.broadcast_to(line, (LANES, LANES)), 0, 1, stride=1, stride_axis=0)


def band_kernel(rim, x_taps_ref, y_taps_ref, column_ref, row_ref):
    _, _, ranks, taps = x_taps_ref.shape
    tap = lax.broadcasted_iota(jnp.int32, (taps, LANES), 0)
    lane = lax.broadcasted_iota(jnp.int32, (taps, LANES), 1)
    x_place = (lane == (rim - tap) % LANES).astype(BF16)
    y_place = (lane == (tap - rim) % LANES).astype(BF16)
    i = lax.broadcasted_iota(jnp.int32, (LANES, LANES), 0)
    j = lax.broadcasted_iota(jnp.int32, (LANES, LANES), 1)
    near = jnp.abs(i - j) < LANES // 2
    x_lines = [jnp.dot(x_taps_ref[0, part], x_place, preferred_element_type=F32) for part in range(2)]
    y_lines = [jnp.dot(y_taps_ref[0, part], y_place, preferred_element_type=F32) for part in range(2)]
    half_lanes = LANES // 2
    for r in range(ranks):
        re, im = (rolled(lines[r : r + 1]) for lines in x_lines)

        def columns(of_re, of_im):
            parts = [jnp.where(near, of_re, 0.0), jnp.where(near, of_im, 0.0)]
            for ring in (of_re, of_im):
                parts.append(jnp.where(j[LANES - rim :] < half_lanes, ring[LANES - rim :], 0.0))
                parts.append(jnp.where(j[:rim] >= half_lanes, ring[:rim], 0.0))
            return jnp.concatenate(parts, axis=0).astype(BF16)

        column_ref[r, :, :LANES] = columns(re, -im)
        column_ref[r, :, LANES:] = columns(im, re)

        re, im = (rolled(lines[r : r + 1]) for lines in y_lines)
        masks = [near] if row_ref.shape[0] == 1 else [j - i > half_lanes, near, j - i < -half_lanes]
        for w, mask in enumerate(masks):
            re_w, im_w = (jnp.where(mask, re, 0.0), jnp.where(mask, im, 0.0))
            at = 2 * r * LANES
            row_ref[w, :LANES, at : at + LANES] = re_w.astype(BF16)
            row_ref[w, :LANES, at + LANES : at + 2 * LANES] = (-im_w).astype(BF16)
            row_ref[w, LANES:, at : at + LANES] = im_w.astype(BF16)
            row_ref[w, LANES:, at + LANES : at + 2 * LANES] = re_w.astype(BF16)


def image_kernel(rim, batches, comps, *refs):
    count = 2 * len(batches)
    column_ref, row_ref, weight_ref, out_ref, lines_ref, passed_ref = refs[count:]
    sources, tiles, rows, width = out_ref.shape
    ranks = column_ref.shape[0]
    blocks = width // LANES
    tile_rows = sources * rows
    chunks = tiles * tile_rows // LANES
    me = lax.axis_index("src")
    my_tile = lax.axis_index("tile")
    lower = my_tile == 0
    for k, piece in enumerate(refs[:count]):
        tile = my_tile if k % 2 == 0 else 1 - my_tile
        for place, step in enumerate(batches[k // 2]):
            cells = piece[place].astype(F32)
            at = pl.multiple_of(tile * tile_rows + jnp.bitwise_xor(me, step) * rows, rows)
            for comp in range(comps):
                lines_ref[comp, pl.ds(at, rows), :] = cells[comp * rows : (comp + 1) * rows]
    for chunk in range(chunks):
        windows = []
        for block in range(blocks):
            first, last = block * LANES, (block + 1) * LANES
            for comp in range(comps):
                cells = lines_ref[comp, chunk * LANES : (chunk + 1) * LANES, :]
                mains, rims = [], []
                for part in range(2):
                    plane = cells[:, part * width : (part + 1) * width]
                    halo = cells[:, 2 * width + part * rim : 2 * width + (part + 1) * rim]
                    mains.append(plane[:, first:last])
                    rims.append(plane[:, first - rim : first] if block > 0 else jnp.where(lower, 0.0, halo))
                    rims.append(plane[:, last : last + rim] if last < width else jnp.where(lower, halo, 0.0))
                windows.append(jnp.concatenate(mains + rims, axis=1).astype(BF16))
        lhs = jnp.concatenate(windows, axis=0)
        for r in range(ranks):
            got = jnp.dot(lhs, column_ref[r], preferred_element_type=F32).astype(BF16)
            for group in range(blocks * comps):
                block, comp = divmod(group, comps)
                at = comp * width + block * LANES
                for part in range(2):
                    passed_ref[chunk, (2 * r + part) * LANES : (2 * r + part + 1) * LANES, at : at + LANES] = (
                        got[group * LANES : (group + 1) * LANES, part * LANES : (part + 1) * LANES]
                    )
    for chunk in range(chunks):
        total = None
        for w in range(row_ref.shape[0]):
            other = chunk + w - row_ref.shape[0] // 2
            if 0 <= other < chunks:
                term = jnp.dot(row_ref[w], passed_ref[other], preferred_element_type=F32)
                total = term if total is None else total + term
        square = total * total
        square = square[:LANES] + square[LANES:]
        power = square[:, :width]
        for comp in range(1, comps):
            power = power + square[:, comp * width : (comp + 1) * width]
        power = power * weight_ref[0]
        for piece in range(LANES // rows):
            tile, source = divmod((chunk * LANES) // rows + piece, sources)
            out_ref[source, tile] = power[piece * rows : (piece + 1) * rows]


def per_device(near_field, x_taps, y_taps, source_weight):
    sources, tiles = lax.axis_size("src"), lax.axis_size("tile")
    _, rows, _, comps, width = near_field.shape
    ranks, taps = x_taps.shape[-2:]
    rim = (taps - 1) // 2
    half_width = width // tiles
    depth = 2 * LANES + 4 * rim
    held = 2 * half_width + 2 * rim
    chunks = sources * tiles * rows // LANES
    windows = 1 if chunks == 1 else 3
    params = pltpu.CompilerParams(vmem_limit_bytes=48 * 1024 * 1024)
    whole = pl.BlockSpec(memory_space=pltpu.VMEM)

    raw = near_field.transpose(0, 1, 3, 2, 4)

    def swapped(piece, step):
        return lax.ppermute(piece, "src", [(i, i ^ step) for i in range(sources)])

    far = [d for d in range(4, sources, 2)][::-1] + [2]
    pieces = {0: raw}
    for step in far:
        pieces[step] = swapped(raw, step)
    for step in [0] + far:
        pieces[step + 1] = swapped(pieces[step], 1)
    batches = [[0] + far + [1], [step + 1 for step in far]]

    column_mats, row_mats = pl.pallas_call(
        functools.partial(band_kernel, rim),
        out_shape=(
            jax.ShapeDtypeStruct((ranks, depth, 2 * LANES), BF16),
            jax.ShapeDtypeStruct((windows, 2 * LANES, 2 * ranks * LANES), BF16),
        ),
        in_specs=[whole, whole],
        out_specs=(whole, whole),
        compiler_params=params,
        name="band_matrices",
    )(x_taps, y_taps)

    halves = []
    for batch in batches:
        half = jax.ShapeDtypeStruct((len(batch), comps * rows, held), BF16)
        mine, theirs = pl.pallas_call(
            functools.partial(halves_kernel, rim, tiles),
            out_shape=(half, half),
            in_specs=[whole] * len(batch),
            out_specs=(whole, whole),
            compiler_params=params,
            name="column_halves",
        )(*[pieces[step] for step in batch])
        halves += [mine, lax.ppermute(theirs, "tile", [(0, 1), (1, 0)])]

    power = pl.pallas_call(
        functools.partial(image_kernel, rim, batches, comps),
        out_shape=jax.ShapeDtypeStruct((sources, tiles, rows, half_width), F32),
        in_specs=[whole] * (len(halves) + 2) + [pl.BlockSpec(memory_space=pltpu.SMEM)],
        out_specs=whole,
        scratch_shapes=[
            pltpu.VMEM((comps, chunks * LANES, held), F32),
            pltpu.VMEM((chunks, 2 * ranks * LANES, comps * half_width), BF16),
        ],
        compiler_params=params,
        name="image",
    )(*halves, column_mats, row_mats, source_weight)
    parts = lax.all_to_all(
        power.reshape(sources * tiles, rows, half_width), ("src", "tile"), 0, 0
    ).reshape(power.shape)
    summed = jnp.sum(parts, axis=0)
    return summed.transpose(1, 0, 2).reshape(1, rows, width)


def solution(mesh):
    placed = (
        P(("group", "tile"), "src", None, None, None),
        P("src", None, None, None),
        P("src", None, None, None),
        P("src"),
    )
    return jax.shard_map(
        per_device,
        mesh=mesh,
        in_specs=placed,
        out_specs=P(("group", "tile"), "src", None),
        check_vma=False,
    )
```

```python
import functools

import jax
import jax.numpy as jnp
from jax import lax
from jax.experimental import pallas as pl
from jax.experimental.pallas import tpu as pltpu
from jax.sharding import PartitionSpec as P

LANES = 128
F32 = jnp.float32
BF16 = jnp.bfloat16


def half_kernel(rim, tiles, field_ref, mine_ref, theirs_ref):
    comps, width = field_ref.shape[2], field_ref.shape[4]
    half_width = width // tiles
    field = field_ref[0].astype(F32)
    halves = []
    for half in range(tiles):
        first, last = half * half_width, (half + 1) * half_width
        inner = last if half == 0 else first - rim
        groups = []
        for comp in range(comps):
            planes = [field[:, comp, part, :] for part in range(2)]
            cells = [plane[:, first:last] for plane in planes] + [plane[:, inner : inner + rim] for plane in planes]
            groups.append(jnp.concatenate(cells, axis=1))
        halves.append(jnp.concatenate(groups, axis=0))
    lower = lax.axis_index("tile") == 0
    mine_ref[...] = jnp.where(lower, halves[0], halves[1]).astype(BF16)
    theirs_ref[...] = jnp.where(lower, halves[1], halves[0]).astype(BF16)


def join_kernel(inner, mine_ref, other_ref, own_ref):
    lower = lax.axis_index("tile") == 0
    mine, other = mine_ref[...].astype(F32), other_ref[...].astype(F32)
    cells = [jnp.where(lower, mine, other), jnp.where(lower, other, mine)]
    main = mine.shape[1] - inner
    own_ref[...] = jnp.concatenate([c[:, :main] for c in cells] + [c[:, main:] for c in cells], axis=1).astype(BF16)


def rolled(line):
    return pltpu.roll(jnp.broadcast_to(line, (LANES, LANES)), 0, 1, stride=1, stride_axis=0)


def band_kernel(rim, x_taps_ref, y_taps_ref, column_ref, row_ref):
    _, _, ranks, taps = x_taps_ref.shape
    tap = lax.broadcasted_iota(jnp.int32, (taps, LANES), 0)
    lane = lax.broadcasted_iota(jnp.int32, (taps, LANES), 1)
    x_place = (lane == (rim - tap) % LANES).astype(BF16)
    y_place = (lane == (tap - rim) % LANES).astype(BF16)
    i = lax.broadcasted_iota(jnp.int32, (LANES, LANES), 0)
    j = lax.broadcasted_iota(jnp.int32, (LANES, LANES), 1)
    near = jnp.abs(i - j) < LANES // 2
    x_lines = [jnp.dot(x_taps_ref[0, part], x_place, preferred_element_type=F32) for part in range(2)]
    y_lines = [jnp.dot(y_taps_ref[0, part], y_place, preferred_element_type=F32) for part in range(2)]
    half_lanes = LANES // 2
    for r in range(ranks):
        re, im = (rolled(lines[r : r + 1]) for lines in x_lines)

        def columns(of_re, of_im):
            parts = [jnp.where(near, of_re, 0.0), jnp.where(near, of_im, 0.0)]
            for ring in (of_re, of_im):
                parts.append(jnp.where(j[LANES - rim :] < half_lanes, ring[LANES - rim :], 0.0))
                parts.append(jnp.where(j[:rim] >= half_lanes, ring[:rim], 0.0))
            return jnp.concatenate(parts, axis=0).astype(BF16)

        column_ref[r, :, :LANES] = columns(re, -im)
        column_ref[r, :, LANES:] = columns(im, re)

        re, im = (rolled(lines[r : r + 1]) for lines in y_lines)
        masks = [near] if row_ref.shape[0] == 1 else [j - i > half_lanes, near, j - i < -half_lanes]
        for w, mask in enumerate(masks):
            re_w, im_w = (jnp.where(mask, re, 0.0), jnp.where(mask, im, 0.0))
            at = 2 * r * LANES
            row_ref[w, :LANES, at : at + LANES] = re_w.astype(BF16)
            row_ref[w, :LANES, at + LANES : at + 2 * LANES] = (-im_w).astype(BF16)
            row_ref[w, LANES:, at : at + LANES] = im_w.astype(BF16)
            row_ref[w, LANES:, at + LANES : at + 2 * LANES] = re_w.astype(BF16)


def image_kernel(rim, steps, comps, *refs):
    pieces = refs[: len(steps)]
    column_ref, row_ref, weight_ref, out_ref, lines_ref, passed_ref = refs[len(steps) :]
    sources, tiles, rows, width = out_ref.shape
    ranks = column_ref.shape[0]
    blocks = width // LANES
    tile_rows = len(steps) * rows
    chunks = tiles * tile_rows // LANES
    me = lax.axis_index("src")
    lower = lax.axis_index("tile") == 0
    for step, piece in zip(steps, pieces):
        cells = piece[...].astype(F32)
        for tile in range(tiles):
            at = pl.multiple_of(tile * tile_rows + jnp.bitwise_xor(me, step) * rows, rows)
            main, halo = 2 * width * tile, 2 * (width * tiles + rim * tile)
            for comp in range(comps):
                some = cells[comp * rows : (comp + 1) * rows]
                lines_ref[comp, pl.ds(at, rows), : 2 * width] = some[:, main : main + 2 * width]
                lines_ref[comp, pl.ds(at, rows), 2 * width :] = some[:, halo : halo + 2 * rim]
    for chunk in range(chunks):
        windows = []
        for block in range(blocks):
            first, last = block * LANES, (block + 1) * LANES
            for comp in range(comps):
                cells = lines_ref[comp, chunk * LANES : (chunk + 1) * LANES, :]
                mains, rims = [], []
                for part in range(2):
                    plane = cells[:, part * width : (part + 1) * width]
                    halo = cells[:, 2 * width + part * rim : 2 * width + (part + 1) * rim]
                    mains.append(plane[:, first:last])
                    rims.append(plane[:, first - rim : first] if block > 0 else jnp.where(lower, 0.0, halo))
                    rims.append(plane[:, last : last + rim] if last < width else jnp.where(lower, halo, 0.0))
                windows.append(jnp.concatenate(mains + rims, axis=1).astype(BF16))
        lhs = jnp.concatenate(windows, axis=0)
        for r in range(ranks):
            got = jnp.dot(lhs, column_ref[r], preferred_element_type=F32).astype(BF16)
            for group in range(blocks * comps):
                block, comp = divmod(group, comps)
                at = comp * width + block * LANES
                for part in range(2):
                    passed_ref[chunk, (2 * r + part) * LANES : (2 * r + part + 1) * LANES, at : at + LANES] = (
                        got[group * LANES : (group + 1) * LANES, part * LANES : (part + 1) * LANES]
                    )
    for chunk in range(chunks):
        total = None
        for w in range(row_ref.shape[0]):
            other = chunk + w - row_ref.shape[0] // 2
            if 0 <= other < chunks:
                term = jnp.dot(row_ref[w], passed_ref[other], preferred_element_type=F32)
                total = term if total is None else total + term
        square = total * total
        square = square[:LANES] + square[LANES:]
        power = square[:, :width]
        for comp in range(1, comps):
            power = power + square[:, comp * width : (comp + 1) * width]
        power = power * weight_ref[0]
        for piece in range(LANES // rows):
            tile, source = divmod((chunk * LANES) // rows + piece, sources)
            out_ref[source, tile] = power[piece * rows : (piece + 1) * rows]


def per_device(near_field, x_taps, y_taps, source_weight):
    sources, tiles = lax.axis_size("src"), lax.axis_size("tile")
    _, rows, _, comps, width = near_field.shape
    ranks, taps = x_taps.shape[-2:]
    rim = (taps - 1) // 2
    half_width = width // tiles
    depth = 2 * LANES + 4 * rim
    held = 2 * half_width + 2 * rim
    chunks = sources * tiles * rows // LANES
    windows = 1 if chunks == 1 else 3
    params = pltpu.CompilerParams(vmem_limit_bytes=48 * 1024 * 1024)
    whole = pl.BlockSpec(memory_space=pltpu.VMEM)

    half = jax.ShapeDtypeStruct((comps * rows, held), BF16)
    def call(kernel, name, out_shape, *operands):
        many = isinstance(out_shape, tuple)
        return pl.pallas_call(
            kernel,
            out_shape=out_shape,
            in_specs=[whole] * len(operands),
            out_specs=(whole,) * len(out_shape) if many else whole,
            compiler_params=params,
            name=name,
        )(*operands)

    def swapped(piece, step):
        return lax.ppermute(piece, "src", [(i, i ^ step) for i in range(sources)])

    mine, theirs = call(
        functools.partial(half_kernel, rim, tiles), "column_halves", (half, half), near_field.transpose(0, 1, 3, 2, 4)
    )
    other = lax.ppermute(theirs, "tile", [(0, 1), (1, 0)])
    own = call(
        functools.partial(join_kernel, 2 * rim),
        "join_cores",
        jax.ShapeDtypeStruct((comps * rows, tiles * held), BF16),
        mine,
        other,
    )
    mats = call(
        functools.partial(band_kernel, rim),
        "band_matrices",
        (
            jax.ShapeDtypeStruct((ranks, depth, 2 * LANES), BF16),
            jax.ShapeDtypeStruct((windows, 2 * LANES, 2 * ranks * LANES), BF16),
        ),
        x_taps,
        y_taps,
    )
    far = [d for d in range(4, sources, 2)][::-1] + [2]
    by_step = {0: own}
    for step in far:
        by_step[step] = swapped(own, step)
    by_step[1] = swapped(own, 1)
    by_step[1], by_step[2], mats = lax.optimization_barrier((by_step[1], by_step[2], mats))
    for step in far:
        by_step[step + 1] = swapped(by_step[step], 1)
    steps = sorted(by_step)
    pieces = [by_step[step] for step in steps]

    power = pl.pallas_call(
        functools.partial(image_kernel, rim, steps, comps),
        out_shape=jax.ShapeDtypeStruct((sources, tiles, rows, half_width), F32),
        in_specs=[whole] * (sources + 2) + [pl.BlockSpec(memory_space=pltpu.SMEM)],
        out_specs=whole,
        scratch_shapes=[
            pltpu.VMEM((comps, chunks * LANES, held), F32),
            pltpu.VMEM((chunks, 2 * ranks * LANES, comps * half_width), BF16),
        ],
        compiler_params=params,
        name="image",
    )(*pieces, *mats, source_weight)
    parts = lax.all_to_all(
        power.reshape(sources * tiles, rows, half_width), ("src", "tile"), 0, 0
    ).reshape(power.shape)
    summed = jnp.sum(parts, axis=0)
    return summed.transpose(1, 0, 2).reshape(1, rows, width)


def solution(mesh):
    placed = (
        P(("group", "tile"), "src", None, None, None),
        P("src", None, None, None),
        P("src", None, None, None),
        P("src"),
    )
    return jax.shard_map(
        per_device,
        mesh=mesh,
        in_specs=placed,
        out_specs=P(("group", "tile"), "src", None),
        check_vma=False,
    )
```

```python
import functools

import jax
import jax.numpy as jnp
from jax import lax
from jax.experimental import pallas as pl
from jax.experimental.pallas import tpu as pltpu
from jax.sharding import PartitionSpec as P

LANES = 128
F32 = jnp.float32
BF16 = jnp.bfloat16


def send_kernel(rim, field_ref, x_taps_ref, y_taps_ref, weight_ref, send_ref):
    _, rows, comps, _, width = field_ref.shape
    sources, tiles, height, lanes = send_ref.shape
    ranks, taps = x_taps_ref.shape[2:]
    mine = width // (sources * tiles)
    window = mine + 2 * rim
    edge = jnp.zeros((rows, rim), F32)
    field = field_ref[0].astype(F32)
    padded = [
        [jnp.concatenate([edge, field[:, comp, part, :], edge], axis=1) for part in range(2)] for comp in range(comps)
    ]
    lines = [ref[0, part].astype(F32) for ref in (x_taps_ref, y_taps_ref) for part in range(2)]
    weight = jnp.full((ranks, 1), weight_ref[0], F32)
    high = weight.astype(BF16).astype(F32)
    middle = (weight - high).astype(BF16).astype(F32)
    low = weight - high - middle
    spare = [line[:, taps - 1 :] for line in lines] + [high, middle, low]
    spare.append(jnp.zeros((ranks, lanes - 2 * window - len(spare)), F32))
    spare = jnp.concatenate(spare, axis=1)
    spare = jnp.concatenate([spare, jnp.zeros((comps * rows - ranks, spare.shape[1]), F32)], axis=0)
    held = jnp.concatenate([line[:, : taps - 1] for line in lines], axis=1)
    for device in range(sources * tiles):
        at = device * mine
        cells = [jnp.concatenate([plane[:, at : at + window] for plane in padded[comp]], axis=1) for comp in range(comps)]
        cells = jnp.concatenate([jnp.concatenate(cells, axis=0), spare], axis=1)
        source, tile = divmod(device, tiles)
        send_ref[source, tile] = jnp.concatenate([cells, held], axis=0).astype(BF16)


def rolled(line, count):
    return pltpu.roll(jnp.broadcast_to(line, (count, line.shape[1])), 0, 1, stride=1, stride_axis=0)


def image_kernel(rim, comps, rows, ranks, got_ref, out_ref, field_ref, lhs_ref, row_ref, total_ref):
    sources, tiles, _, lanes = got_ref.shape
    mine, slab_rows = total_ref.shape
    window = mine + 2 * rim
    tile_rows = sources * rows
    chunks = slab_rows // LANES
    windows = row_ref.shape[1]
    half_lanes = LANES // 2
    for tile in range(tiles):
        cells = got_ref[:, tile].astype(F32)
        for comp in range(comps):
            some = cells[:, comp * rows : (comp + 1) * rows, :].reshape(tile_rows, lanes).astype(BF16)
            at = comp * slab_rows + tile * tile_rows
            field_ref[at : at + tile_rows, :] = some

    tap = lax.broadcasted_iota(jnp.int32, (2 * rim, lanes), 0)
    lane = lax.broadcasted_iota(jnp.int32, (2 * rim, lanes), 1)
    re_place = (lane == tap).astype(BF16)
    im_place = (lane == tap + window).astype(BF16)
    y_place = (lane == (rim - tap) % LANES).astype(BF16)[:, :LANES]
    one = lane[:1]
    re_last = (one == 2 * rim).astype(F32)
    im_last = (one == 2 * rim + window).astype(F32)
    y_last = (one == LANES - rim).astype(F32)[:, :LANES]
    k = lax.broadcasted_iota(jnp.int32, (LANES, LANES), 0)
    i = lax.broadcasted_iota(jnp.int32, (LANES, LANES), 1)
    near = jnp.abs(i - k) < half_lanes
    masks = [near] if windows == 1 else [k - i > half_lanes, near, k - i < -half_lanes]
    total_ref[...] = jnp.zeros_like(total_ref)

    def placed(first, last, place, last_place):
        return jnp.dot(first, place, preferred_element_type=F32) + last * last_place

    def one_source(source, slot):
        block = got_ref[source, 0].astype(F32)
        held = block[comps * rows : comps * rows + ranks]
        firsts = [held[:, 2 * rim * n : 2 * rim * (n + 1)].astype(BF16) for n in range(4)]
        spare = block[:ranks, 2 * window :]
        lasts = [spare[:, n : n + 1] for n in range(4)]
        weight = spare[:1, 4:5] + spare[:1, 5:6] + spare[:1, 6:7]
        at_re = [placed(firsts[n], lasts[n], re_place, re_last) for n in range(2)]
        at_im = [placed(firsts[n], lasts[n], im_place, im_last) for n in range(2)]
        x_lines = [at_re[0] - at_im[1], at_re[1] + at_im[0]]
        y_lines = [placed(firsts[n], lasts[n], y_place, y_last) for n in range(2, 4)]
        column_mat = jnp.concatenate(
            [rolled(x_lines[out][r : r + 1], mine) for r in range(ranks) for out in range(2)], axis=0
        ).astype(BF16)
        passed = lax.dot_general(column_mat, field_ref[...], (((1,), (1,)), ((), ())), preferred_element_type=F32)
        for chunk in range(chunks):
            for n in range(2 * ranks):
                cells = [
                    passed[n * mine : (n + 1) * mine, comp * slab_rows + chunk * LANES : comp * slab_rows + (chunk + 1) * LANES]
                    for comp in range(comps)
                ]
                lhs_ref[slot, chunk, :, n * LANES : (n + 1) * LANES] = jnp.concatenate(cells, axis=0).astype(BF16)
        for r in range(ranks):
            re, im = (rolled(lines[r : r + 1], LANES) for lines in y_lines)
            at = 2 * r * LANES
            for n, mask in enumerate(masks):
                re_n, im_n = jnp.where(mask, re, 0.0), jnp.where(mask, im, 0.0)
                row_ref[slot, n, at : at + LANES, :LANES] = re_n.astype(BF16)
                row_ref[slot, n, at : at + LANES, LANES:] = im_n.astype(BF16)
                row_ref[slot, n, at + LANES : at + 2 * LANES, :LANES] = (-im_n).astype(BF16)
                row_ref[slot, n, at + LANES : at + 2 * LANES, LANES:] = re_n.astype(BF16)
        for chunk in range(chunks):
            image = None
            for n in range(windows):
                other = chunk + n - windows // 2
                if 0 <= other < chunks:
                    term = jnp.dot(lhs_ref[slot, other], row_ref[slot, n], preferred_element_type=F32)
                    image = term if image is None else image + term
            square = image * image
            square = square[:, :LANES] + square[:, LANES:]
            power = square[:mine]
            for comp in range(1, comps):
                power = power + square[comp * mine : (comp + 1) * mine]
            total_ref[:, chunk * LANES : (chunk + 1) * LANES] += weight * power

    if sources <= 8:
        for source in range(sources):
            one_source(source, source % 2)
    else:
        lax.fori_loop(0, sources, lambda source, _: one_source(source, 0), None)
    for chunk in range(chunks):
        lines = total_ref[:, chunk * LANES : (chunk + 1) * LANES].T
        for piece in range(LANES // rows):
            tile, source = divmod((chunk * LANES) // rows + piece, sources)
            out_ref[source, tile] = lines[piece * rows : (piece + 1) * rows]


def merge_kernel(parts_ref, out_ref):
    out_ref[0] = jnp.concatenate([parts_ref[n] for n in range(parts_ref.shape[0])], axis=1)


def per_device(near_field, x_taps, y_taps, source_weight):
    sources, tiles = lax.axis_size("src"), lax.axis_size("tile")
    _, rows, _, comps, width = near_field.shape
    ranks, taps = x_taps.shape[-2:]
    rim = (taps - 1) // 2
    devices = sources * tiles
    mine = width // devices
    lanes = 2 * LANES
    slab_rows = devices * rows
    chunks = slab_rows // LANES
    windows = 1 if chunks == 1 else 3
    height = comps * rows + ranks
    params = pltpu.CompilerParams(vmem_limit_bytes=48 * 1024 * 1024)
    whole = pl.BlockSpec(memory_space=pltpu.VMEM)
    send = pl.pallas_call(
        functools.partial(send_kernel, rim),
        out_shape=jax.ShapeDtypeStruct((sources, tiles, height, lanes), BF16),
        in_specs=[whole] * 3 + [pl.BlockSpec(memory_space=pltpu.SMEM)],
        out_specs=whole,
        compiler_params=params,
        name="send_columns",
    )(near_field.transpose(0, 1, 3, 2, 4), x_taps, y_taps, source_weight)
    got = lax.all_to_all(send.reshape(devices, height, lanes), ("src", "tile"), 0, 0).reshape(send.shape)
    slots = 2 if sources <= 8 else 1
    image = pl.pallas_call(
        functools.partial(image_kernel, rim, comps, rows, ranks),
        out_shape=jax.ShapeDtypeStruct((sources, tiles, rows, mine), F32),
        in_specs=[whole],
        out_specs=whole,
        scratch_shapes=[
            pltpu.VMEM((comps * slab_rows, lanes), BF16),
            pltpu.VMEM((slots, chunks, comps * mine, 2 * ranks * LANES), BF16),
            pltpu.VMEM((slots, windows, 2 * ranks * LANES, 2 * LANES), BF16),
            pltpu.VMEM((mine, slab_rows), F32),
        ],
        compiler_params=params,
        name="image",
    )(got)
    parts = lax.all_to_all(image.reshape(devices, rows, mine), ("src", "tile"), 0, 0)
    return pl.pallas_call(
        merge_kernel,
        out_shape=jax.ShapeDtypeStruct((1, rows, width), F32),
        in_specs=[whole],
        out_specs=whole,
        compiler_params=params,
        name="merge_columns",
    )(parts)


def solution(mesh):
    placed = (
        P(("group", "tile"), "src", None, None, None),
        P("src", None, None, None),
        P("src", None, None, None),
        P("src"),
    )
    return jax.shard_map(
        per_device,
        mesh=mesh,
        in_specs=placed,
        out_specs=P(("group", "tile"), "src", None),
        check_vma=False,
    )
```

```python
import functools

import jax
import jax.numpy as jnp
from jax import lax
from jax.experimental import pallas as pl
from jax.experimental.pallas import tpu as pltpu
from jax.sharding import PartitionSpec as P

LANES = 128
F32 = jnp.float32
BF16 = jnp.bfloat16


def send_kernel(
    rim, field_hbm, x_taps_hbm, y_taps_hbm, weight_ref, send_ref, field_ref, x_taps_ref, y_taps_ref, sems
):
    pairs = ((field_hbm, field_ref), (x_taps_hbm, x_taps_ref), (y_taps_hbm, y_taps_ref))
    copies = [pltpu.make_async_copy(source, target, sems.at[n]) for n, (source, target) in enumerate(pairs)]
    for copy in copies:
        copy.start()
    for copy in copies:
        copy.wait()
    _, rows, comps, _, width = field_ref.shape
    sources, tiles, height, lanes = send_ref.shape
    ranks, taps = x_taps_ref.shape[2:]
    mine = width // (sources * tiles)
    window = mine + 2 * rim
    edge = jnp.zeros((rows, rim), F32)
    field = field_ref[0].astype(F32)
    padded = [
        [jnp.concatenate([edge, field[:, comp, part, :], edge], axis=1) for part in range(2)] for comp in range(comps)
    ]
    lower = lax.axis_index("tile") == 0
    lines = [
        jnp.where(lower, x_taps_ref[0, part].astype(F32), y_taps_ref[0, part].astype(F32)) for part in range(2)
    ]
    weight = jnp.full((ranks, 1), weight_ref[0], F32)
    high = weight.astype(BF16).astype(F32)
    middle = (weight - high).astype(BF16).astype(F32)
    low = weight - high - middle
    last = [line[:, taps - 1 :] for line in lines] + [high, middle, low]
    last.append(jnp.zeros((ranks, taps - 1 - len(last)), F32))
    spare = jnp.concatenate([line[:, : taps - 1] for line in lines] + [jnp.concatenate(last, axis=1)], axis=0)
    unused = lanes - 2 * window - (taps - 1)
    if unused > 0:
        spare = jnp.concatenate([spare, jnp.zeros((height, unused), F32)], axis=1)
    for device in range(sources * tiles):
        at = device * mine
        cells = [jnp.concatenate([plane[:, at : at + window] for plane in padded[comp]], axis=1) for comp in range(comps)]
        source, tile = divmod(device, tiles)
        send_ref[source, tile] = jnp.concatenate([jnp.concatenate(cells, axis=0), spare], axis=1).astype(BF16)


def rolled(line, count):
    return pltpu.roll(jnp.broadcast_to(line, (count, line.shape[1])), 0, 1, stride=1, stride_axis=0)


def image_kernel(rim, comps, rows, ranks, got_ref, out_ref, field_ref, lhs_ref, row_ref, total_ref):
    sources, tiles, _, lanes = got_ref.shape
    mine, slab_rows = total_ref.shape
    window = mine + 2 * rim
    tile_rows = sources * rows
    chunks = slab_rows // LANES
    windows = row_ref.shape[1]
    half_lanes = LANES // 2
    for tile in range(tiles):
        cells = got_ref[:, tile].astype(F32)
        for comp in range(comps):
            some = cells[:, comp * rows : (comp + 1) * rows, :].reshape(tile_rows, lanes).astype(BF16)
            at = comp * slab_rows + tile * tile_rows
            field_ref[at : at + tile_rows, :] = some

    tap = lax.broadcasted_iota(jnp.int32, (2 * rim, lanes), 0)
    lane = lax.broadcasted_iota(jnp.int32, (2 * rim, lanes), 1)
    re_place = (lane == tap).astype(BF16)
    im_place = (lane == tap + window).astype(BF16)
    y_place = (lane == (rim - tap) % LANES).astype(BF16)[:, :LANES]
    one = lane[:1]
    re_last = (one == 2 * rim).astype(F32)
    im_last = (one == 2 * rim + window).astype(F32)
    y_last = (one == LANES - rim).astype(F32)[:, :LANES]
    k = lax.broadcasted_iota(jnp.int32, (LANES, LANES), 0)
    i = lax.broadcasted_iota(jnp.int32, (LANES, LANES), 1)
    near = jnp.abs(i - k) < half_lanes
    masks = [near] if windows == 1 else [k - i > half_lanes, near, k - i < -half_lanes]
    total_ref[...] = jnp.zeros_like(total_ref)

    def placed(first, last, place, last_place):
        return jnp.dot(first, place, preferred_element_type=F32) + last * last_place

    def one_source(source, slot):
        blocks = [got_ref[source, tile].astype(F32)[:, 2 * window : 2 * window + 2 * rim] for tile in range(2)]
        firsts = [block[part * ranks : (part + 1) * ranks].astype(BF16) for block in blocks for part in range(2)]
        lasts = [block[2 * ranks : 3 * ranks, part : part + 1] for block in blocks for part in range(2)]
        weight = blocks[0][2 * ranks : 2 * ranks + 1]
        weight = weight[:, 2:3] + weight[:, 3:4] + weight[:, 4:5]
        at_re = [placed(firsts[n], lasts[n], re_place, re_last) for n in range(2)]
        at_im = [placed(firsts[n], lasts[n], im_place, im_last) for n in range(2)]
        x_lines = [at_re[0] - at_im[1], at_re[1] + at_im[0]]
        y_lines = [placed(firsts[n], lasts[n], y_place, y_last) for n in range(2, 4)]
        column_mat = jnp.concatenate(
            [rolled(x_lines[out][r : r + 1], mine) for r in range(ranks) for out in range(2)], axis=0
        ).astype(BF16)
        passed = lax.dot_general(column_mat, field_ref[...], (((1,), (1,)), ((), ())), preferred_element_type=F32)
        for chunk in range(chunks):
            for n in range(2 * ranks):
                cells = [
                    passed[n * mine : (n + 1) * mine, comp * slab_rows + chunk * LANES : comp * slab_rows + (chunk + 1) * LANES]
                    for comp in range(comps)
                ]
                lhs_ref[slot, chunk, :, n * LANES : (n + 1) * LANES] = jnp.concatenate(cells, axis=0).astype(BF16)
        for r in range(ranks):
            re, im = (rolled(lines[r : r + 1], LANES) for lines in y_lines)
            at = 2 * r * LANES
            for n, mask in enumerate(masks):
                re_n, im_n = jnp.where(mask, re, 0.0), jnp.where(mask, im, 0.0)
                row_ref[slot, n, at : at + LANES, :LANES] = re_n.astype(BF16)
                row_ref[slot, n, at : at + LANES, LANES:] = im_n.astype(BF16)
                row_ref[slot, n, at + LANES : at + 2 * LANES, :LANES] = (-im_n).astype(BF16)
                row_ref[slot, n, at + LANES : at + 2 * LANES, LANES:] = re_n.astype(BF16)
        for chunk in range(chunks):
            image = None
            for n in range(windows):
                other = chunk + n - windows // 2
                if 0 <= other < chunks:
                    term = jnp.dot(lhs_ref[slot, other], row_ref[slot, n], preferred_element_type=F32)
                    image = term if image is None else image + term
            square = image * image
            square = square[:, :LANES] + square[:, LANES:]
            power = square[:mine]
            for comp in range(1, comps):
                power = power + square[comp * mine : (comp + 1) * mine]
            total_ref[:, chunk * LANES : (chunk + 1) * LANES] += weight * power

    if sources <= 8:
        for source in range(sources):
            one_source(source, source % 2)
    else:
        lax.fori_loop(0, sources, lambda source, _: one_source(source, 0), None)
    for chunk in range(chunks):
        lines = total_ref[:, chunk * LANES : (chunk + 1) * LANES].T
        for piece in range(LANES // rows):
            tile, source = divmod((chunk * LANES) // rows + piece, sources)
            block = lines[piece * rows : (piece + 1) * rows]
            step = out_ref.shape[2]
            groups = [block[n : n + step] for n in range(0, rows, step)]
            out_ref[source, tile] = jnp.concatenate(groups, axis=1)


def merge_kernel(parts_ref, out_ref):
    devices = parts_ref.shape[0]
    mine = out_ref.shape[2] // devices
    blocks = []
    for device in range(devices):
        part = parts_ref[device]
        groups = [part[:, at : at + mine] for at in range(0, part.shape[1], mine)]
        blocks.append(jnp.concatenate(groups, axis=0))
    out_ref[0] = jnp.concatenate(blocks, axis=1)


def per_device(near_field, x_taps, y_taps, source_weight):
    sources, tiles = lax.axis_size("src"), lax.axis_size("tile")
    _, rows, _, comps, width = near_field.shape
    ranks, taps = x_taps.shape[-2:]
    rim = (taps - 1) // 2
    devices = sources * tiles
    mine = width // devices
    lanes = 2 * LANES
    slab_rows = devices * rows
    chunks = slab_rows // LANES
    windows = 1 if chunks == 1 else 3
    height = comps * rows
    step = max(1, rows * mine // LANES)
    params = pltpu.CompilerParams(vmem_limit_bytes=48 * 1024 * 1024)
    whole = pl.BlockSpec(memory_space=pltpu.VMEM)

    def in_hbm(array):
        return pltpu.with_memory_space_constraint(array, pltpu.HBM)

    send = pl.pallas_call(
        functools.partial(send_kernel, rim),
        out_shape=jax.ShapeDtypeStruct((sources, tiles, height, lanes), BF16),
        in_specs=[pl.BlockSpec(memory_space=pltpu.HBM)] * 3 + [pl.BlockSpec(memory_space=pltpu.SMEM)],
        out_specs=whole,
        scratch_shapes=[
            pltpu.VMEM((1, rows, comps, 2, width), BF16),
            pltpu.VMEM(x_taps.shape, BF16),
            pltpu.VMEM(y_taps.shape, BF16),
            pltpu.SemaphoreType.DMA((3,)),
        ],
        compiler_params=params,
        name="send_columns",
    )(in_hbm(near_field.transpose(0, 1, 3, 2, 4)), in_hbm(x_taps), in_hbm(y_taps), source_weight)
    got = lax.all_to_all(send.reshape(devices, height, lanes), ("src", "tile"), 0, 0).reshape(send.shape)
    slots = 2 if sources <= 8 else 1
    image = pl.pallas_call(
        functools.partial(image_kernel, rim, comps, rows, ranks),
        out_shape=jax.ShapeDtypeStruct((sources, tiles, step, rows // step * mine), F32),
        in_specs=[whole],
        out_specs=whole,
        scratch_shapes=[
            pltpu.VMEM((comps * slab_rows, lanes), BF16),
            pltpu.VMEM((slots, chunks, comps * mine, 2 * ranks * LANES), BF16),
            pltpu.VMEM((slots, windows, 2 * ranks * LANES, 2 * LANES), BF16),
            pltpu.VMEM((mine, slab_rows), F32),
        ],
        compiler_params=params,
        name="image",
    )(got)
    parts = lax.all_to_all(image.reshape((devices,) + image.shape[2:]), ("src", "tile"), 0, 0)
    return pl.pallas_call(
        merge_kernel,
        out_shape=jax.ShapeDtypeStruct((1, rows, width), F32),
        in_specs=[whole],
        out_specs=whole,
        compiler_params=params,
        name="merge_columns",
    )(parts)


def solution(mesh):
    placed = (
        P(("group", "tile"), "src", None, None, None),
        P("src", None, None, None),
        P("src", None, None, None),
        P("src"),
    )
    return jax.shard_map(
        per_device,
        mesh=mesh,
        in_specs=placed,
        out_specs=P(("group", "tile"), "src", None),
        check_vma=False,
    )
```

```python
import functools

import jax
import jax.numpy as jnp
from jax import lax
from jax.experimental import pallas as pl
from jax.experimental.pallas import tpu as pltpu
from jax.sharding import PartitionSpec as P

LANES = 128
F32 = jnp.float32
BF16 = jnp.bfloat16


def send_kernel(
    rim, field_hbm, x_taps_hbm, y_taps_hbm, weight_ref, send_ref, field_ref, x_taps_ref, y_taps_ref, sems
):
    pairs = ((field_hbm, field_ref), (x_taps_hbm, x_taps_ref), (y_taps_hbm, y_taps_ref))
    copies = [pltpu.make_async_copy(source, target, sems.at[n]) for n, (source, target) in enumerate(pairs)]
    for copy in copies:
        copy.start()
    for copy in copies:
        copy.wait()
    _, rows, comps, _, width = field_ref.shape
    sources, tiles, height, lanes = send_ref.shape
    ranks, taps = x_taps_ref.shape[2:]
    mine = width // (sources * tiles)
    window = mine + 2 * rim
    edge = jnp.zeros((rows, rim), F32)
    field = field_ref[0].astype(F32)
    padded = [
        [jnp.concatenate([edge, field[:, comp, part, :], edge], axis=1) for part in range(2)] for comp in range(comps)
    ]
    lower = lax.axis_index("tile") == 0
    lines = [
        jnp.where(lower, x_taps_ref[0, part].astype(F32), y_taps_ref[0, part].astype(F32)) for part in range(2)
    ]
    weight = jnp.full((ranks, 1), weight_ref[0], F32)
    high = weight.astype(BF16).astype(F32)
    middle = (weight - high).astype(BF16).astype(F32)
    low = weight - high - middle
    last = [line[:, taps - 1 :] for line in lines] + [high, middle, low]
    last.append(jnp.zeros((ranks, taps - 1 - len(last)), F32))
    spare = jnp.concatenate([line[:, : taps - 1] for line in lines] + [jnp.concatenate(last, axis=1)], axis=0)
    unused = lanes - 2 * window - (taps - 1)
    if unused > 0:
        spare = jnp.concatenate([spare, jnp.zeros((height, unused), F32)], axis=1)
    for device in range(sources * tiles):
        at = device * mine
        cells = [jnp.concatenate([plane[:, at : at + window] for plane in padded[comp]], axis=1) for comp in range(comps)]
        source, tile = divmod(device, tiles)
        send_ref[source, tile] = jnp.concatenate([jnp.concatenate(cells, axis=0), spare], axis=1).astype(BF16)


def rolled(line, count):
    return pltpu.roll(jnp.broadcast_to(line, (count, line.shape[1])), 0, 1, stride=1, stride_axis=0)


def image_kernel(rim, comps, rows, ranks, got_ref, out_ref, field_ref, lhs_ref, row_ref, total_ref):
    sources, tiles, _, lanes = got_ref.shape
    mine, slab_rows = total_ref.shape
    window = mine + 2 * rim
    tile_rows = sources * rows
    chunks = slab_rows // LANES
    windows = row_ref.shape[1]
    half_lanes = LANES // 2
    for tile in range(tiles):
        cells = got_ref[:, tile].astype(F32)
        for comp in range(comps):
            some = cells[:, comp * rows : (comp + 1) * rows, :].reshape(tile_rows, lanes).astype(BF16)
            at = comp * slab_rows + tile * tile_rows
            field_ref[at : at + tile_rows, :] = some

    tap = lax.broadcasted_iota(jnp.int32, (2 * rim, lanes), 0)
    lane = lax.broadcasted_iota(jnp.int32, (2 * rim, lanes), 1)
    re_place = (lane == tap).astype(BF16)
    im_place = (lane == tap + window).astype(BF16)
    y_place = (lane == (rim - tap) % LANES).astype(BF16)[:, :LANES]
    one = lane[:1]
    re_last = (one == 2 * rim).astype(F32)
    im_last = (one == 2 * rim + window).astype(F32)
    y_last = (one == LANES - rim).astype(F32)[:, :LANES]
    k = lax.broadcasted_iota(jnp.int32, (LANES, LANES), 0)
    i = lax.broadcasted_iota(jnp.int32, (LANES, LANES), 1)
    near = jnp.abs(i - k) < half_lanes
    masks = [near] if windows == 1 else [k - i > half_lanes, near, k - i < -half_lanes]
    total_ref[...] = jnp.zeros_like(total_ref)

    def placed(first, last, place, last_place):
        return jnp.dot(first, place, preferred_element_type=F32) + last * last_place

    def one_source(source, slot):
        blocks = [got_ref[source, tile].astype(F32)[:, 2 * window : 2 * window + 2 * rim] for tile in range(2)]
        firsts = [block[part * ranks : (part + 1) * ranks].astype(BF16) for block in blocks for part in range(2)]
        lasts = [block[2 * ranks : 3 * ranks, part : part + 1] for block in blocks for part in range(2)]
        weight = blocks[0][2 * ranks : 2 * ranks + 1]
        weight = weight[:, 2:3] + weight[:, 3:4] + weight[:, 4:5]
        at_re = [placed(firsts[n], lasts[n], re_place, re_last) for n in range(2)]
        at_im = [placed(firsts[n], lasts[n], im_place, im_last) for n in range(2)]
        x_lines = [at_re[0] - at_im[1], at_re[1] + at_im[0]]
        y_lines = [placed(firsts[n], lasts[n], y_place, y_last) for n in range(2, 4)]
        column_mat = jnp.concatenate(
            [rolled(x_lines[out][r : r + 1], mine) for r in range(ranks) for out in range(2)], axis=0
        ).astype(BF16)
        passed = lax.dot_general(column_mat, field_ref[...], (((1,), (1,)), ((), ())), preferred_element_type=F32)
        for chunk in range(chunks):
            for r in range(ranks):
                cells = []
                for part in range(2):
                    for comp in range(comps):
                        top, left = (2 * r + part) * mine, comp * slab_rows + chunk * LANES
                        cells.append(passed[top : top + mine, left : left + LANES])
                lhs_ref[slot, chunk, :, r * LANES : (r + 1) * LANES] = jnp.concatenate(cells, axis=0).astype(BF16)
        for r in range(ranks):
            for part in range(2):
                ring = rolled(y_lines[part][r : r + 1], LANES)
                for n, mask in enumerate(masks):
                    row_ref[slot, n, r * LANES : (r + 1) * LANES, part * LANES : (part + 1) * LANES] = jnp.where(
                        mask, ring, 0.0
                    ).astype(BF16)
        for chunk in range(chunks):
            image = None
            for n in range(windows):
                other = chunk + n - windows // 2
                if 0 <= other < chunks:
                    term = jnp.dot(lhs_ref[slot, other], row_ref[slot, n], preferred_element_type=F32)
                    image = term if image is None else image + term
            of_re, of_im = image[: comps * mine], image[comps * mine :]
            image_re = of_re[:, :LANES] - of_im[:, LANES:]
            image_im = of_re[:, LANES:] + of_im[:, :LANES]
            square = image_re * image_re + image_im * image_im
            power = square[:mine]
            for comp in range(1, comps):
                power = power + square[comp * mine : (comp + 1) * mine]
            total_ref[:, chunk * LANES : (chunk + 1) * LANES] += weight * power

    if sources <= 8:
        for source in range(sources):
            one_source(source, source % 2)
    else:
        lax.fori_loop(0, sources, lambda source, _: one_source(source, 0), None)
    for chunk in range(chunks):
        lines = total_ref[:, chunk * LANES : (chunk + 1) * LANES].T
        for piece in range(LANES // rows):
            tile, source = divmod((chunk * LANES) // rows + piece, sources)
            block = lines[piece * rows : (piece + 1) * rows]
            step = out_ref.shape[2]
            groups = [block[n : n + step] for n in range(0, rows, step)]
            out_ref[source, tile] = jnp.concatenate(groups, axis=1)


def merge_kernel(parts_ref, out_ref):
    devices = parts_ref.shape[0]
    mine = out_ref.shape[2] // devices
    blocks = []
    for device in range(devices):
        part = parts_ref[device]
        groups = [part[:, at : at + mine] for at in range(0, part.shape[1], mine)]
        blocks.append(jnp.concatenate(groups, axis=0))
    out_ref[0] = jnp.concatenate(blocks, axis=1)


def per_device(near_field, x_taps, y_taps, source_weight):
    sources, tiles = lax.axis_size("src"), lax.axis_size("tile")
    _, rows, _, comps, width = near_field.shape
    ranks, taps = x_taps.shape[-2:]
    rim = (taps - 1) // 2
    devices = sources * tiles
    mine = width // devices
    lanes = 2 * LANES
    slab_rows = devices * rows
    chunks = slab_rows // LANES
    windows = 1 if chunks == 1 else 3
    height = comps * rows
    step = max(1, rows * mine // LANES)
    params = pltpu.CompilerParams(vmem_limit_bytes=48 * 1024 * 1024)
    whole = pl.BlockSpec(memory_space=pltpu.VMEM)

    def in_hbm(array):
        return pltpu.with_memory_space_constraint(array, pltpu.HBM)

    send = pl.pallas_call(
        functools.partial(send_kernel, rim),
        out_shape=jax.ShapeDtypeStruct((sources, tiles, height, lanes), BF16),
        in_specs=[pl.BlockSpec(memory_space=pltpu.HBM)] * 3 + [pl.BlockSpec(memory_space=pltpu.SMEM)],
        out_specs=whole,
        scratch_shapes=[
            pltpu.VMEM((1, rows, comps, 2, width), BF16),
            pltpu.VMEM(x_taps.shape, BF16),
            pltpu.VMEM(y_taps.shape, BF16),
            pltpu.SemaphoreType.DMA((3,)),
        ],
        compiler_params=params,
        name="send_columns",
    )(in_hbm(near_field.transpose(0, 1, 3, 2, 4)), in_hbm(x_taps), in_hbm(y_taps), source_weight)
    got = lax.all_to_all(send.reshape(devices, height, lanes), ("src", "tile"), 0, 0).reshape(send.shape)
    slots = 2 if sources <= 8 else 1
    image = pl.pallas_call(
        functools.partial(image_kernel, rim, comps, rows, ranks),
        out_shape=jax.ShapeDtypeStruct((sources, tiles, step, rows // step * mine), F32),
        in_specs=[whole],
        out_specs=whole,
        scratch_shapes=[
            pltpu.VMEM((comps * slab_rows, lanes), BF16),
            pltpu.VMEM((slots, chunks, 2 * comps * mine, ranks * LANES), BF16),
            pltpu.VMEM((slots, windows, ranks * LANES, 2 * LANES), BF16),
            pltpu.VMEM((mine, slab_rows), F32),
        ],
        compiler_params=params,
        name="image",
    )(got)
    parts = lax.all_to_all(image.reshape((devices,) + image.shape[2:]), ("src", "tile"), 0, 0)
    return pl.pallas_call(
        merge_kernel,
        out_shape=jax.ShapeDtypeStruct((1, rows, width), F32),
        in_specs=[whole],
        out_specs=whole,
        compiler_params=params,
        name="merge_columns",
    )(parts)


def solution(mesh):
    placed = (
        P(("group", "tile"), "src", None, None, None),
        P("src", None, None, None),
        P("src", None, None, None),
        P("src"),
    )
    return jax.shard_map(
        per_device,
        mesh=mesh,
        in_specs=placed,
        out_specs=P(("group", "tile"), "src", None),
        check_vma=False,
    )
```

```python
import functools

import jax
import jax.numpy as jnp
from jax import lax
from jax.experimental import pallas as pl
from jax.experimental.pallas import tpu as pltpu
from jax.sharding import PartitionSpec as P

LANES = 128
F32 = jnp.float32
BF16 = jnp.bfloat16


def send_kernel(
    rim, field_hbm, x_taps_hbm, y_taps_hbm, weight_ref, send_ref, field_ref, x_taps_ref, y_taps_ref, sems
):
    pairs = ((field_hbm, field_ref), (x_taps_hbm, x_taps_ref), (y_taps_hbm, y_taps_ref))
    copies = [pltpu.make_async_copy(source, target, sems.at[n]) for n, (source, target) in enumerate(pairs)]
    for copy in copies:
        copy.start()
    for copy in copies:
        copy.wait()
    _, rows, comps, _, width = field_ref.shape
    sources, tiles, height, lanes = send_ref.shape
    ranks, taps = x_taps_ref.shape[2:]
    mine = width // (sources * tiles)
    window = mine + 2 * rim
    edge = jnp.zeros((rows, rim), F32)
    field = field_ref[0].astype(F32)
    padded = [
        [jnp.concatenate([edge, field[:, comp, part, :], edge], axis=1) for part in range(2)] for comp in range(comps)
    ]
    lower = lax.axis_index("tile") == 0
    lines = [
        jnp.where(lower, x_taps_ref[0, part].astype(F32), y_taps_ref[0, part].astype(F32)) for part in range(2)
    ]
    weight = jnp.full((ranks, 1), weight_ref[0], F32)
    high = weight.astype(BF16).astype(F32)
    middle = (weight - high).astype(BF16).astype(F32)
    low = weight - high - middle
    last = [line[:, taps - 1 :] for line in lines] + [high, middle, low]
    last.append(jnp.zeros((ranks, taps - 1 - len(last)), F32))
    spare = jnp.concatenate([line[:, : taps - 1] for line in lines] + [jnp.concatenate(last, axis=1)], axis=0)
    unused = lanes - 2 * window - (taps - 1)
    if unused > 0:
        spare = jnp.concatenate([spare, jnp.zeros((height, unused), F32)], axis=1)
    for device in range(sources * tiles):
        at = device * mine
        cells = [jnp.concatenate([plane[:, at : at + window] for plane in padded[comp]], axis=1) for comp in range(comps)]
        source, tile = divmod(device, tiles)
        send_ref[source, tile] = jnp.concatenate([jnp.concatenate(cells, axis=0), spare], axis=1).astype(BF16)


def rolled(line, count):
    return pltpu.roll(jnp.broadcast_to(line, (count, line.shape[1])), 0, 1, stride=1, stride_axis=0)


def image_kernel(rim, comps, rows, ranks, got_ref, out_ref, field_ref, column_ref, lhs_ref, row_ref, total_ref):
    sources, tiles, _, lanes = got_ref.shape
    mine, slab_rows = total_ref.shape
    window = mine + 2 * rim
    tile_rows = sources * rows
    chunks = slab_rows // LANES
    windows = row_ref.shape[1]
    half_lanes = LANES // 2
    for tile in range(tiles):
        cells = got_ref[:, tile].astype(F32)
        for comp in range(comps):
            some = cells[:, comp * rows : (comp + 1) * rows, :].reshape(tile_rows, lanes).astype(BF16)
            at = comp * slab_rows + tile * tile_rows
            field_ref[at : at + tile_rows, :] = some

    tap = lax.broadcasted_iota(jnp.int32, (2 * rim, lanes), 0)
    lane = lax.broadcasted_iota(jnp.int32, (2 * rim, lanes), 1)
    re_place = (lane == tap).astype(BF16)
    im_place = (lane == tap + window).astype(BF16)
    y_place = (lane == (rim - tap) % LANES).astype(BF16)[:, :LANES]
    one = lane[:1]
    re_last = (one == 2 * rim).astype(F32)
    im_last = (one == 2 * rim + window).astype(F32)
    y_last = (one == LANES - rim).astype(F32)[:, :LANES]
    k = lax.broadcasted_iota(jnp.int32, (LANES, LANES), 0)
    i = lax.broadcasted_iota(jnp.int32, (LANES, LANES), 1)
    near = jnp.abs(i - k) < half_lanes
    masks = [near] if windows == 1 else [k - i > half_lanes, near, k - i < -half_lanes]
    total_ref[...] = jnp.zeros_like(total_ref)

    def placed(first, last, place, last_place):
        return jnp.dot(first, place, preferred_element_type=F32) + last * last_place

    def bands(source, slot):
        blocks = [got_ref[source, tile].astype(F32)[:, 2 * window : 2 * window + 2 * rim] for tile in range(2)]
        firsts = [block[part * ranks : (part + 1) * ranks].astype(BF16) for block in blocks for part in range(2)]
        lasts = [block[2 * ranks : 3 * ranks, part : part + 1] for block in blocks for part in range(2)]
        at_re = [placed(firsts[n], lasts[n], re_place, re_last) for n in range(2)]
        at_im = [placed(firsts[n], lasts[n], im_place, im_last) for n in range(2)]
        x_lines = [at_re[0] - at_im[1], at_re[1] + at_im[0]]
        y_lines = [placed(firsts[n], lasts[n], y_place, y_last) for n in range(2, 4)]
        column_ref[slot] = jnp.concatenate(
            [rolled(x_lines[out][r : r + 1], mine) for r in range(ranks) for out in range(2)], axis=0
        ).astype(BF16)
        for r in range(ranks):
            for part in range(2):
                ring = rolled(y_lines[part][r : r + 1], LANES)
                for n, mask in enumerate(masks):
                    row_ref[slot, n, r * LANES : (r + 1) * LANES, part * LANES : (part + 1) * LANES] = jnp.where(
                        mask, ring, 0.0
                    ).astype(BF16)

    def column_pass(slot):
        passed = lax.dot_general(
            column_ref[slot], field_ref[...], (((1,), (1,)), ((), ())), preferred_element_type=F32
        )
        for chunk in range(chunks):
            for r in range(ranks):
                cells = []
                for part in range(2):
                    for comp in range(comps):
                        top, left = (2 * r + part) * mine, comp * slab_rows + chunk * LANES
                        cells.append(passed[top : top + mine, left : left + LANES])
                lhs_ref[slot, chunk, :, r * LANES : (r + 1) * LANES] = jnp.concatenate(cells, axis=0).astype(BF16)

    def row_pass(source, slot):
        weight = got_ref[source, 0].astype(F32)[2 * ranks : 2 * ranks + 1, 2 * window : 2 * window + 2 * rim]
        weight = weight[:, 2:3] + weight[:, 3:4] + weight[:, 4:5]
        for chunk in range(chunks):
            image = None
            for n in range(windows):
                other = chunk + n - windows // 2
                if 0 <= other < chunks:
                    term = jnp.dot(lhs_ref[slot, other], row_ref[slot, n], preferred_element_type=F32)
                    image = term if image is None else image + term
            of_re, of_im = image[: comps * mine], image[comps * mine :]
            image_re = of_re[:, :LANES] - of_im[:, LANES:]
            image_im = of_re[:, LANES:] + of_im[:, :LANES]
            square = image_re * image_re + image_im * image_im
            power = square[:mine]
            for comp in range(1, comps):
                power = power + square[comp * mine : (comp + 1) * mine]
            total_ref[:, chunk * LANES : (chunk + 1) * LANES] += weight * power

    if sources <= 8:
        bands(0, 0)
        for source in range(sources):
            column_pass(source)
            if source + 1 < sources:
                bands(source + 1, source + 1)
            row_pass(source, source)
    else:

        def one_source(source, _):
            bands(source, 0)
            column_pass(0)
            row_pass(source, 0)

        lax.fori_loop(0, sources, one_source, None)
    for chunk in range(chunks):
        lines = total_ref[:, chunk * LANES : (chunk + 1) * LANES].T
        for piece in range(LANES // rows):
            tile, source = divmod((chunk * LANES) // rows + piece, sources)
            block = lines[piece * rows : (piece + 1) * rows]
            step = out_ref.shape[2]
            groups = [block[n : n + step] for n in range(0, rows, step)]
            out_ref[source, tile] = jnp.concatenate(groups, axis=1)


def merge_kernel(parts_ref, out_ref):
    devices = parts_ref.shape[0]
    mine = out_ref.shape[2] // devices
    blocks = []
    for device in range(devices):
        part = parts_ref[device]
        groups = [part[:, at : at + mine] for at in range(0, part.shape[1], mine)]
        blocks.append(jnp.concatenate(groups, axis=0))
    out_ref[0] = jnp.concatenate(blocks, axis=1)


def per_device(near_field, x_taps, y_taps, source_weight):
    sources, tiles = lax.axis_size("src"), lax.axis_size("tile")
    _, rows, _, comps, width = near_field.shape
    ranks, taps = x_taps.shape[-2:]
    rim = (taps - 1) // 2
    devices = sources * tiles
    mine = width // devices
    lanes = 2 * LANES
    slab_rows = devices * rows
    chunks = slab_rows // LANES
    windows = 1 if chunks == 1 else 3
    height = comps * rows
    step = max(1, rows * mine // LANES)
    params = pltpu.CompilerParams(vmem_limit_bytes=48 * 1024 * 1024)
    whole = pl.BlockSpec(memory_space=pltpu.VMEM)

    def in_hbm(array):
        return pltpu.with_memory_space_constraint(array, pltpu.HBM)

    send = pl.pallas_call(
        functools.partial(send_kernel, rim),
        out_shape=jax.ShapeDtypeStruct((sources, tiles, height, lanes), BF16),
        in_specs=[pl.BlockSpec(memory_space=pltpu.HBM)] * 3 + [pl.BlockSpec(memory_space=pltpu.SMEM)],
        out_specs=whole,
        scratch_shapes=[
            pltpu.VMEM((1, rows, comps, 2, width), BF16),
            pltpu.VMEM(x_taps.shape, BF16),
            pltpu.VMEM(y_taps.shape, BF16),
            pltpu.SemaphoreType.DMA((3,)),
        ],
        compiler_params=params,
        name="send_columns",
    )(in_hbm(near_field.transpose(0, 1, 3, 2, 4)), in_hbm(x_taps), in_hbm(y_taps), source_weight)
    got = lax.all_to_all(send.reshape(devices, height, lanes), ("src", "tile"), 0, 0).reshape(send.shape)
    slots = sources if sources <= 8 else 1
    image = pl.pallas_call(
        functools.partial(image_kernel, rim, comps, rows, ranks),
        out_shape=jax.ShapeDtypeStruct((sources, tiles, step, rows // step * mine), F32),
        in_specs=[whole],
        out_specs=whole,
        scratch_shapes=[
            pltpu.VMEM((comps * slab_rows, lanes), BF16),
            pltpu.VMEM((slots, 2 * ranks * mine, lanes), BF16),
            pltpu.VMEM((slots, chunks, 2 * comps * mine, ranks * LANES), BF16),
            pltpu.VMEM((slots, windows, ranks * LANES, 2 * LANES), BF16),
            pltpu.VMEM((mine, slab_rows), F32),
        ],
        compiler_params=params,
        name="image",
    )(got)
    parts = lax.all_to_all(image.reshape((devices,) + image.shape[2:]), ("src", "tile"), 0, 0)
    return pl.pallas_call(
        merge_kernel,
        out_shape=jax.ShapeDtypeStruct((1, rows, width), F32),
        in_specs=[whole],
        out_specs=whole,
        compiler_params=params,
        name="merge_columns",
    )(parts)


def solution(mesh):
    placed = (
        P(("group", "tile"), "src", None, None, None),
        P("src", None, None, None),
        P("src", None, None, None),
        P("src"),
    )
    return jax.shard_map(
        per_device,
        mesh=mesh,
        in_specs=placed,
        out_specs=P(("group", "tile"), "src", None),
        check_vma=False,
    )
```

```python
import functools

import jax
import jax.numpy as jnp
from jax import lax
from jax.experimental import pallas as pl
from jax.experimental.pallas import tpu as pltpu
from jax.sharding import PartitionSpec as P

LANES = 128
F32 = jnp.float32
BF16 = jnp.bfloat16


def send_kernel(
    rim, field_hbm, x_taps_hbm, y_taps_hbm, weight_ref, send_ref, field_ref, x_taps_ref, y_taps_ref, sems
):
    pairs = ((field_hbm, field_ref), (x_taps_hbm, x_taps_ref), (y_taps_hbm, y_taps_ref))
    copies = [pltpu.make_async_copy(source, target, sems.at[n]) for n, (source, target) in enumerate(pairs)]
    for copy in copies:
        copy.start()
    for copy in copies:
        copy.wait()
    _, rows, comps, _, width = field_ref.shape
    sources, tiles, height, lanes = send_ref.shape
    ranks, taps = x_taps_ref.shape[2:]
    mine = width // (sources * tiles)
    window = mine + 2 * rim
    edge = jnp.zeros((rows, rim), F32)
    field = field_ref[0].astype(F32)
    padded = [
        [jnp.concatenate([edge, field[:, comp, part, :], edge], axis=1) for part in range(2)] for comp in range(comps)
    ]
    lower = lax.axis_index("tile") == 0
    lines = [
        jnp.where(lower, x_taps_ref[0, part].astype(F32), y_taps_ref[0, part].astype(F32)) for part in range(2)
    ]
    weight = jnp.full((ranks, 1), weight_ref[0], F32)
    high = weight.astype(BF16).astype(F32)
    middle = (weight - high).astype(BF16).astype(F32)
    low = weight - high - middle
    last = [line[:, taps - 1 :] for line in lines] + [high, middle, low]
    last.append(jnp.zeros((ranks, taps - 1 - len(last)), F32))
    spare = jnp.concatenate([line[:, : taps - 1] for line in lines] + [jnp.concatenate(last, axis=1)], axis=0)
    spares = [spare[:, :rim], spare[:, rim:]]
    if window < LANES - rim:
        gap = jnp.zeros((height, LANES - rim - window), F32)
        spares = [jnp.concatenate([gap, part], axis=1) for part in spares]
    for device in range(sources * tiles):
        at = device * mine
        cells = []
        for part in range(2):
            plane = [padded[comp][part][:, at : at + window] for comp in range(comps)]
            cells += [jnp.concatenate(plane, axis=0), spares[part]]
        source, tile = divmod(device, tiles)
        send_ref[source, tile] = jnp.concatenate(cells, axis=1).astype(BF16)


def rolled(line, count):
    return pltpu.roll(jnp.broadcast_to(line, (count, line.shape[1])), 0, 1, stride=1, stride_axis=0)


def image_kernel(rim, comps, rows, ranks, got_ref, out_ref, field_ref, taps_ref, column_ref, lhs_ref, row_ref, total_ref):
    sources, tiles, _, lanes = got_ref.shape
    mine, slab_rows = total_ref.shape
    window = mine + 2 * rim
    tile_rows = sources * rows
    chunks = slab_rows // LANES
    windows = row_ref.shape[1]
    half_lanes = LANES // 2
    for tile in range(tiles):
        cells = got_ref[:, tile].astype(F32)
        for comp in range(comps):
            some = cells[:, comp * rows : (comp + 1) * rows, :].reshape(tile_rows, lanes).astype(BF16)
            at = comp * slab_rows + tile * tile_rows
            field_ref[at : at + tile_rows, :] = some

    tap = lax.broadcasted_iota(jnp.int32, (2 * rim, LANES), 0)
    lane = lax.broadcasted_iota(jnp.int32, (2 * rim, LANES), 1)
    x_place = (lane == tap).astype(BF16)
    y_place = (lane == (rim - tap) % LANES).astype(BF16)
    x_last = (lane[:1] == 2 * rim).astype(F32)
    y_last = (lane[:1] == LANES - rim).astype(F32)
    for n, (place, last_place) in enumerate(((x_place, x_last), (y_place, y_last))):
        block = got_ref[:, n].astype(F32)
        taps = jnp.concatenate([block[:, :, LANES - rim : LANES], block[:, :, 2 * LANES - rim :]], axis=2)
        for part in range(2):
            first = taps[:, part * ranks : (part + 1) * ranks].reshape(sources * ranks, 2 * rim)
            last = taps[:, 2 * ranks : 3 * ranks].reshape(sources * ranks, 2 * rim)[:, part : part + 1]
            line = jnp.dot(first.astype(BF16), place, preferred_element_type=F32) + last * last_place
            taps_ref[2 * n + part] = line
    k = lax.broadcasted_iota(jnp.int32, (LANES, LANES), 0)
    i = lax.broadcasted_iota(jnp.int32, (LANES, LANES), 1)
    near = jnp.abs(i - k) < half_lanes
    masks = [near] if windows == 1 else [k - i > half_lanes, near, k - i < -half_lanes]
    total_ref[...] = jnp.zeros_like(total_ref)

    def bands(source, slot):
        at = source * ranks if isinstance(source, int) else pl.multiple_of(source * ranks, ranks)
        lines = [taps_ref[n, pl.ds(at, ranks), :] for n in range(4)]
        y_lines = lines[2:]
        for r in range(ranks):
            re, im = (rolled(line[r : r + 1], mine) for line in lines[:2])
            top = 2 * r * mine
            column_ref[slot, top : top + mine, :LANES] = re.astype(column_ref.dtype)
            column_ref[slot, top : top + mine, LANES:] = (-im).astype(column_ref.dtype)
            column_ref[slot, top + mine : top + 2 * mine, :LANES] = im.astype(column_ref.dtype)
            column_ref[slot, top + mine : top + 2 * mine, LANES:] = re.astype(column_ref.dtype)
        for r in range(ranks):
            for part in range(2):
                ring = rolled(y_lines[part][r : r + 1], LANES)
                for n, mask in enumerate(masks):
                    row_ref[slot, n, r * LANES : (r + 1) * LANES, part * LANES : (part + 1) * LANES] = jnp.where(
                        mask, ring, 0.0
                    ).astype(BF16)

    def column_pass(slot):
        passed = lax.dot_general(
            column_ref[slot].astype(BF16), field_ref[...], (((1,), (1,)), ((), ())), preferred_element_type=F32
        )
        for chunk in range(chunks):
            for r in range(ranks):
                cells = []
                for part in range(2):
                    for comp in range(comps):
                        top, left = (2 * r + part) * mine, comp * slab_rows + chunk * LANES
                        cells.append(passed[top : top + mine, left : left + LANES])
                lhs_ref[slot, chunk, :, r * LANES : (r + 1) * LANES] = jnp.concatenate(cells, axis=0).astype(BF16)

    def row_pass(source, slot):
        weight = got_ref[source, 0].astype(F32)[2 * ranks : 2 * ranks + 1, LANES - rim : LANES]
        weight = weight[:, 2:3] + weight[:, 3:4] + weight[:, 4:5]
        for chunk in range(chunks):
            image = None
            for n in range(windows):
                other = chunk + n - windows // 2
                if 0 <= other < chunks:
                    term = jnp.dot(lhs_ref[slot, other], row_ref[slot, n], preferred_element_type=F32)
                    image = term if image is None else image + term
            of_re, of_im = image[: comps * mine], image[comps * mine :]
            image_re = of_re[:, :LANES] - of_im[:, LANES:]
            image_im = of_re[:, LANES:] + of_im[:, :LANES]
            square = image_re * image_re + image_im * image_im
            power = square[:mine]
            for comp in range(1, comps):
                power = power + square[comp * mine : (comp + 1) * mine]
            total_ref[:, chunk * LANES : (chunk + 1) * LANES] += weight * power

    if sources <= 8:
        bands(0, 0)
        column_pass(0)
        bands(1, 1)
        for source in range(sources):
            if source + 1 < sources:
                column_pass(source + 1)
            row_pass(source, source)
            if source + 2 < sources:
                bands(source + 2, source + 2)
    else:

        def one_source(source, _):
            bands(source, 0)
            column_pass(0)
            row_pass(source, 0)

        lax.fori_loop(0, sources, one_source, None)
    for chunk in range(chunks):
        lines = total_ref[:, chunk * LANES : (chunk + 1) * LANES].T
        for piece in range(LANES // rows):
            tile, source = divmod((chunk * LANES) // rows + piece, sources)
            block = lines[piece * rows : (piece + 1) * rows]
            step = out_ref.shape[2]
            groups = [block[n : n + step] for n in range(0, rows, step)]
            out_ref[source, tile] = jnp.concatenate(groups, axis=1)


def merge_kernel(parts_ref, out_ref):
    devices = parts_ref.shape[0]
    mine = out_ref.shape[2] // devices
    blocks = []
    for device in range(devices):
        part = parts_ref[device]
        groups = [part[:, at : at + mine] for at in range(0, part.shape[1], mine)]
        blocks.append(jnp.concatenate(groups, axis=0))
    out_ref[0] = jnp.concatenate(blocks, axis=1)


def per_device(near_field, x_taps, y_taps, source_weight):
    sources, tiles = lax.axis_size("src"), lax.axis_size("tile")
    _, rows, _, comps, width = near_field.shape
    ranks, taps = x_taps.shape[-2:]
    rim = (taps - 1) // 2
    devices = sources * tiles
    mine = width // devices
    lanes = 2 * LANES
    slab_rows = devices * rows
    chunks = slab_rows // LANES
    windows = 1 if chunks == 1 else 3
    height = comps * rows
    step = max(1, rows * mine // LANES)
    params = pltpu.CompilerParams(vmem_limit_bytes=48 * 1024 * 1024)
    whole = pl.BlockSpec(memory_space=pltpu.VMEM)

    def in_hbm(array):
        return pltpu.with_memory_space_constraint(array, pltpu.HBM)

    send = pl.pallas_call(
        functools.partial(send_kernel, rim),
        out_shape=jax.ShapeDtypeStruct((sources, tiles, height, lanes), BF16),
        in_specs=[pl.BlockSpec(memory_space=pltpu.HBM)] * 3 + [pl.BlockSpec(memory_space=pltpu.SMEM)],
        out_specs=whole,
        scratch_shapes=[
            pltpu.VMEM((1, rows, comps, 2, width), BF16),
            pltpu.VMEM(x_taps.shape, BF16),
            pltpu.VMEM(y_taps.shape, BF16),
            pltpu.SemaphoreType.DMA((3,)),
        ],
        compiler_params=params,
        name="send_columns",
    )(in_hbm(near_field.transpose(0, 1, 3, 2, 4)), in_hbm(x_taps), in_hbm(y_taps), source_weight)
    got = lax.all_to_all(send.reshape(devices, height, lanes), ("src", "tile"), 0, 0).reshape(send.shape)
    slots = sources if sources <= 8 else 1
    image = pl.pallas_call(
        functools.partial(image_kernel, rim, comps, rows, ranks),
        out_shape=jax.ShapeDtypeStruct((sources, tiles, step, rows // step * mine), F32),
        in_specs=[whole],
        out_specs=whole,
        scratch_shapes=[
            pltpu.VMEM((comps * slab_rows, lanes), BF16),
            pltpu.VMEM((4, sources * ranks, LANES), F32),
            pltpu.VMEM((slots, 2 * ranks * mine, lanes), BF16 if mine % 16 == 0 else F32),
            pltpu.VMEM((slots, chunks, 2 * comps * mine, ranks * LANES), BF16),
            pltpu.VMEM((slots, windows, ranks * LANES, 2 * LANES), BF16),
            pltpu.VMEM((mine, slab_rows), F32),
        ],
        compiler_params=params,
        name="image",
    )(got)
    parts = lax.all_to_all(image.reshape((devices,) + image.shape[2:]), ("src", "tile"), 0, 0)
    return pl.pallas_call(
        merge_kernel,
        out_shape=jax.ShapeDtypeStruct((1, rows, width), F32),
        in_specs=[whole],
        out_specs=whole,
        compiler_params=params,
        name="merge_columns",
    )(parts)


def solution(mesh):
    placed = (
        P(("group", "tile"), "src", None, None, None),
        P("src", None, None, None),
        P("src", None, None, None),
        P("src"),
    )
    return jax.shard_map(
        per_device,
        mesh=mesh,
        in_specs=placed,
        out_specs=P(("group", "tile"), "src", None),
        check_vma=False,
    )
```

```python
import functools

import jax
import jax.numpy as jnp
from jax import lax
from jax.experimental import pallas as pl
from jax.experimental.pallas import tpu as pltpu
from jax.sharding import PartitionSpec as P

LANES = 128
F32 = jnp.float32
BF16 = jnp.bfloat16


def send_kernel(
    rim, field_hbm, x_taps_hbm, y_taps_hbm, weight_ref, send_ref, field_ref, x_taps_ref, y_taps_ref, sems
):
    pairs = ((field_hbm, field_ref), (x_taps_hbm, x_taps_ref), (y_taps_hbm, y_taps_ref))
    copies = [pltpu.make_async_copy(source, target, sems.at[n]) for n, (source, target) in enumerate(pairs)]
    for copy in copies:
        copy.start()
    for copy in copies:
        copy.wait()
    _, rows, comps, _, width = field_ref.shape
    sources, tiles, height, lanes = send_ref.shape
    ranks, taps = x_taps_ref.shape[2:]
    mine = width // (sources * tiles)
    window = mine + 2 * rim
    edge = jnp.zeros((rows, rim), F32)
    field = field_ref[0].astype(F32)
    padded = [
        [jnp.concatenate([edge, field[:, comp, part, :], edge], axis=1) for part in range(2)] for comp in range(comps)
    ]
    lower = lax.axis_index("tile") == 0
    lines = [
        jnp.where(lower, x_taps_ref[0, part].astype(F32), y_taps_ref[0, part].astype(F32)) for part in range(2)
    ]
    weight = jnp.full((ranks, 1), weight_ref[0], F32)
    high = weight.astype(BF16).astype(F32)
    middle = (weight - high).astype(BF16).astype(F32)
    low = weight - high - middle
    last = [line[:, taps - 1 :] for line in lines] + [high, middle, low]
    last.append(jnp.zeros((ranks, taps - 1 - len(last)), F32))
    spare = jnp.concatenate([line[:, : taps - 1] for line in lines] + [jnp.concatenate(last, axis=1)], axis=0)
    spares = [spare[:, :rim], spare[:, rim:]]
    if window < LANES - rim:
        gap = jnp.zeros((height, LANES - rim - window), F32)
        spares = [jnp.concatenate([gap, part], axis=1) for part in spares]
    for device in range(sources * tiles):
        at = device * mine
        cells = []
        for part in range(2):
            plane = [padded[comp][part][:, at : at + window] for comp in range(comps)]
            cells += [jnp.concatenate(plane, axis=0), spares[part]]
        source, tile = divmod(device, tiles)
        send_ref[source, tile] = jnp.concatenate(cells, axis=1).astype(BF16)


def rolled(line, count):
    return pltpu.roll(jnp.broadcast_to(line, (count, line.shape[1])), 0, 1, stride=1, stride_axis=0)


def image_kernel(rim, comps, rows, ranks, got_ref, out_ref, field_ref, taps_ref, column_ref, lhs_ref, row_ref, total_ref):
    sources, tiles, _, lanes = got_ref.shape
    mine, slab_rows = total_ref.shape
    window = mine + 2 * rim
    tile_rows = sources * rows
    chunks = slab_rows // LANES
    windows = row_ref.shape[1]
    half_lanes = LANES // 2
    for tile in range(tiles):
        cells = got_ref[:, tile].astype(F32)
        for comp in range(comps):
            some = cells[:, comp * rows : (comp + 1) * rows, :].reshape(tile_rows, lanes).astype(BF16)
            at = comp * slab_rows + tile * tile_rows
            field_ref[at : at + tile_rows, :] = some

    tap = lax.broadcasted_iota(jnp.int32, (2 * rim, LANES), 0)
    lane = lax.broadcasted_iota(jnp.int32, (2 * rim, LANES), 1)
    x_place = (lane == tap).astype(BF16)
    y_place = (lane == (rim - tap) % LANES).astype(BF16)
    x_last = (lane[:1] == 2 * rim).astype(F32)
    y_last = (lane[:1] == LANES - rim).astype(F32)
    for n, (place, last_place) in enumerate(((x_place, x_last), (y_place, y_last))):
        block = got_ref[:, n].astype(F32)
        taps = jnp.concatenate([block[:, :, LANES - rim : LANES], block[:, :, 2 * LANES - rim :]], axis=2)
        for part in range(2):
            first = taps[:, part * ranks : (part + 1) * ranks].reshape(sources * ranks, 2 * rim)
            last = taps[:, 2 * ranks : 3 * ranks].reshape(sources * ranks, 2 * rim)[:, part : part + 1]
            line = jnp.dot(first.astype(BF16), place, preferred_element_type=F32) + last * last_place
            taps_ref[2 * n + part] = line
    k = lax.broadcasted_iota(jnp.int32, (LANES, LANES), 0)
    i = lax.broadcasted_iota(jnp.int32, (LANES, LANES), 1)
    near = jnp.abs(i - k) < half_lanes
    masks = [near] if windows == 1 else [k - i > half_lanes, near, k - i < -half_lanes]
    total_ref[...] = jnp.zeros_like(total_ref)

    def bands(source, slot):
        at = source * ranks if isinstance(source, int) else pl.multiple_of(source * ranks, ranks)
        lines = [taps_ref[n, pl.ds(at, ranks), :] for n in range(4)]
        y_lines = lines[2:]
        for r in range(ranks):
            re, im = (rolled(line[r : r + 1], mine) for line in lines[:2])
            top = 2 * r * mine
            column_ref[slot, top : top + mine, :LANES] = re.astype(column_ref.dtype)
            column_ref[slot, top : top + mine, LANES:] = (-im).astype(column_ref.dtype)
            column_ref[slot, top + mine : top + 2 * mine, :LANES] = im.astype(column_ref.dtype)
            column_ref[slot, top + mine : top + 2 * mine, LANES:] = re.astype(column_ref.dtype)
        for r in range(ranks):
            for part in range(2):
                ring = rolled(y_lines[part][r : r + 1], LANES)
                for n, mask in enumerate(masks):
                    band = [
                        jnp.where(mask[:rim], ring[:rim], 0.0),
                        ring[rim : LANES - rim] if n == windows // 2 else jnp.zeros((LANES - 2 * rim, LANES), F32),
                        jnp.where(mask[LANES - rim :], ring[LANES - rim :], 0.0),
                    ]
                    row_ref[slot, n, r * LANES : (r + 1) * LANES, part * LANES : (part + 1) * LANES] = jnp.concatenate(
                        band, axis=0
                    ).astype(BF16)

    def column_pass(slot):
        passed = lax.dot_general(
            column_ref[slot].astype(BF16), field_ref[...], (((1,), (1,)), ((), ())), preferred_element_type=F32
        )
        for chunk in range(chunks):
            for r in range(ranks):
                cells = []
                for part in range(2):
                    for comp in range(comps):
                        top, left = (2 * r + part) * mine, comp * slab_rows + chunk * LANES
                        cells.append(passed[top : top + mine, left : left + LANES])
                lhs_ref[slot, chunk, :, r * LANES : (r + 1) * LANES] = jnp.concatenate(cells, axis=0).astype(BF16)

    def row_pass(source, slot):
        weight = got_ref[source, 0].astype(F32)[2 * ranks : 2 * ranks + 1, LANES - rim : LANES]
        weight = weight[:, 2:3] + weight[:, 3:4] + weight[:, 4:5]
        for chunk in range(chunks):
            image = None
            for n in range(windows):
                other = chunk + n - windows // 2
                if 0 <= other < chunks:
                    term = jnp.dot(lhs_ref[slot, other], row_ref[slot, n], preferred_element_type=F32)
                    image = term if image is None else image + term
            of_re, of_im = image[: comps * mine], image[comps * mine :]
            image_re = of_re[:, :LANES] - of_im[:, LANES:]
            image_im = of_re[:, LANES:] + of_im[:, :LANES]
            square = image_re * image_re + image_im * image_im
            power = square[:mine]
            for comp in range(1, comps):
                power = power + square[comp * mine : (comp + 1) * mine]
            total_ref[:, chunk * LANES : (chunk + 1) * LANES] += weight * power

    if sources <= 8:
        bands(0, 0)
        column_pass(0)
        bands(1, 1)
        for source in range(sources):
            if source + 1 < sources:
                column_pass(source + 1)
            if source + 2 < sources:
                bands(source + 2, source + 2)
            row_pass(source, source)
    else:

        def one_source(source, _):
            bands(source, 0)
            column_pass(0)
            row_pass(source, 0)

        lax.fori_loop(0, sources, one_source, None)
    for chunk in range(chunks):
        lines = total_ref[:, chunk * LANES : (chunk + 1) * LANES].T
        for piece in range(LANES // rows):
            tile, source = divmod((chunk * LANES) // rows + piece, sources)
            block = lines[piece * rows : (piece + 1) * rows]
            step = out_ref.shape[2]
            groups = [block[n : n + step] for n in range(0, rows, step)]
            out_ref[source, tile] = jnp.concatenate(groups, axis=1)


def merge_kernel(parts_ref, out_ref):
    devices = parts_ref.shape[0]
    mine = out_ref.shape[2] // devices
    blocks = []
    for device in range(devices):
        part = parts_ref[device]
        groups = [part[:, at : at + mine] for at in range(0, part.shape[1], mine)]
        blocks.append(jnp.concatenate(groups, axis=0))
    out_ref[0] = jnp.concatenate(blocks, axis=1)


def per_device(near_field, x_taps, y_taps, source_weight):
    sources, tiles = lax.axis_size("src"), lax.axis_size("tile")
    _, rows, _, comps, width = near_field.shape
    ranks, taps = x_taps.shape[-2:]
    rim = (taps - 1) // 2
    devices = sources * tiles
    mine = width // devices
    lanes = 2 * LANES
    slab_rows = devices * rows
    chunks = slab_rows // LANES
    windows = 1 if chunks == 1 else 3
    height = comps * rows
    step = max(1, rows * mine // LANES)
    params = pltpu.CompilerParams(vmem_limit_bytes=48 * 1024 * 1024)
    whole = pl.BlockSpec(memory_space=pltpu.VMEM)

    def in_hbm(array):
        return pltpu.with_memory_space_constraint(array, pltpu.HBM)

    send = pl.pallas_call(
        functools.partial(send_kernel, rim),
        out_shape=jax.ShapeDtypeStruct((sources, tiles, height, lanes), BF16),
        in_specs=[pl.BlockSpec(memory_space=pltpu.HBM)] * 3 + [pl.BlockSpec(memory_space=pltpu.SMEM)],
        out_specs=whole,
        scratch_shapes=[
            pltpu.VMEM((1, rows, comps, 2, width), BF16),
            pltpu.VMEM(x_taps.shape, BF16),
            pltpu.VMEM(y_taps.shape, BF16),
            pltpu.SemaphoreType.DMA((3,)),
        ],
        compiler_params=params,
        name="send_columns",
    )(in_hbm(near_field.transpose(0, 1, 3, 2, 4)), in_hbm(x_taps), in_hbm(y_taps), source_weight)
    got = lax.all_to_all(send.reshape(devices, height, lanes), ("src", "tile"), 0, 0).reshape(send.shape)
    slots = sources if sources <= 8 else 1
    image = pl.pallas_call(
        functools.partial(image_kernel, rim, comps, rows, ranks),
        out_shape=jax.ShapeDtypeStruct((sources, tiles, step, rows // step * mine), F32),
        in_specs=[whole],
        out_specs=whole,
        scratch_shapes=[
            pltpu.VMEM((comps * slab_rows, lanes), BF16),
            pltpu.VMEM((4, sources * ranks, LANES), F32),
            pltpu.VMEM((slots, 2 * ranks * mine, lanes), BF16 if mine % 16 == 0 else F32),
            pltpu.VMEM((slots, chunks, 2 * comps * mine, ranks * LANES), BF16),
            pltpu.VMEM((slots, windows, ranks * LANES, 2 * LANES), BF16),
            pltpu.VMEM((mine, slab_rows), F32),
        ],
        compiler_params=params,
        name="image",
    )(got)
    parts = lax.all_to_all(image.reshape((devices,) + image.shape[2:]), ("src", "tile"), 0, 0)
    return pl.pallas_call(
        merge_kernel,
        out_shape=jax.ShapeDtypeStruct((1, rows, width), F32),
        in_specs=[whole],
        out_specs=whole,
        compiler_params=params,
        name="merge_columns",
    )(parts)


def solution(mesh):
    placed = (
        P(("group", "tile"), "src", None, None, None),
        P("src", None, None, None),
        P("src", None, None, None),
        P("src"),
    )
    return jax.shard_map(
        per_device,
        mesh=mesh,
        in_specs=placed,
        out_specs=P(("group", "tile"), "src", None),
        check_vma=False,
    )
```

```python
import functools

import jax
import jax.numpy as jnp
from jax import lax
from jax.experimental import pallas as pl
from jax.experimental.pallas import tpu as pltpu
from jax.sharding import PartitionSpec as P

LANES = 128
F32 = jnp.float32
BF16 = jnp.bfloat16


def send_kernel(
    rim, field_hbm, x_taps_hbm, y_taps_hbm, weight_ref, send_ref, field_ref, x_taps_ref, y_taps_ref, sems
):
    pairs = ((field_hbm, field_ref), (x_taps_hbm, x_taps_ref), (y_taps_hbm, y_taps_ref))
    copies = [pltpu.make_async_copy(source, target, sems.at[n]) for n, (source, target) in enumerate(pairs)]
    for copy in copies:
        copy.start()
    for copy in copies:
        copy.wait()
    _, rows, comps, _, width = field_ref.shape
    sources, tiles, height, lanes = send_ref.shape
    ranks, taps = x_taps_ref.shape[2:]
    mine = width // (sources * tiles)
    window = mine + 2 * rim
    edge = jnp.zeros((rows, rim), F32)
    field = field_ref[0].astype(F32)
    padded = [
        [jnp.concatenate([edge, field[:, comp, part, :], edge], axis=1) for part in range(2)] for comp in range(comps)
    ]
    lower = lax.axis_index("tile") == 0
    lines = [
        jnp.where(lower, x_taps_ref[0, part].astype(F32), y_taps_ref[0, part].astype(F32)) for part in range(2)
    ]
    weight = jnp.full((ranks, 1), weight_ref[0], F32)
    high = weight.astype(BF16).astype(F32)
    middle = (weight - high).astype(BF16).astype(F32)
    low = weight - high - middle
    last = [line[:, taps - 1 :] for line in lines] + [high, middle, low]
    last.append(jnp.zeros((ranks, taps - 1 - len(last)), F32))
    spare = jnp.concatenate([line[:, : taps - 1] for line in lines] + [jnp.concatenate(last, axis=1)], axis=0)
    spares = [spare[:, :rim], spare[:, rim:]]
    if window < LANES - rim:
        gap = jnp.zeros((height, LANES - rim - window), F32)
        spares = [jnp.concatenate([gap, part], axis=1) for part in spares]
    for device in range(sources * tiles):
        at = device * mine
        cells = []
        for part in range(2):
            plane = [padded[comp][part][:, at : at + window] for comp in range(comps)]
            cells += [jnp.concatenate(plane, axis=0), spares[part]]
        source, tile = divmod(device, tiles)
        send_ref[source, tile] = jnp.concatenate(cells, axis=1).astype(BF16)


def rolled(line, count):
    return pltpu.roll(jnp.broadcast_to(line, (count, line.shape[1])), 0, 1, stride=1, stride_axis=0)


def image_kernel(rim, comps, rows, ranks, got_ref, out_ref, field_ref, taps_ref, column_ref, lhs_ref, row_ref, total_ref):
    sources, tiles, _, lanes = got_ref.shape
    mine, slab_rows = total_ref.shape
    window = mine + 2 * rim
    tile_rows = sources * rows
    chunks = slab_rows // LANES
    windows = row_ref.shape[1]
    half_lanes = LANES // 2
    tile_cells = [got_ref[:, tile].astype(F32) for tile in range(tiles)]
    for comp in range(comps):
        lines = [cells[:, comp * rows : (comp + 1) * rows, :].reshape(tile_rows, lanes) for cells in tile_cells]
        lines = jnp.concatenate(lines, axis=0)
        field_ref[:, comp * slab_rows : (comp + 1) * slab_rows] = lines.T.astype(BF16)

    tap = lax.broadcasted_iota(jnp.int32, (2 * rim, LANES), 0)
    lane = lax.broadcasted_iota(jnp.int32, (2 * rim, LANES), 1)
    x_place = (lane == tap).astype(BF16)
    y_place = (lane == (rim - tap) % LANES).astype(BF16)
    x_last = (lane[:1] == 2 * rim).astype(F32)
    y_last = (lane[:1] == LANES - rim).astype(F32)
    for n, (place, last_place) in enumerate(((x_place, x_last), (y_place, y_last))):
        block = got_ref[:, n].astype(F32)
        taps = jnp.concatenate([block[:, :, LANES - rim : LANES], block[:, :, 2 * LANES - rim :]], axis=2)
        for part in range(2):
            first = taps[:, part * ranks : (part + 1) * ranks].reshape(sources * ranks, 2 * rim)
            last = taps[:, 2 * ranks : 3 * ranks].reshape(sources * ranks, 2 * rim)[:, part : part + 1]
            line = jnp.dot(first.astype(BF16), place, preferred_element_type=F32) + last * last_place
            taps_ref[2 * n + part] = line
    k = lax.broadcasted_iota(jnp.int32, (LANES, LANES), 0)
    i = lax.broadcasted_iota(jnp.int32, (LANES, LANES), 1)
    near = jnp.abs(i - k) < half_lanes
    masks = [near] if windows == 1 else [k - i > half_lanes, near, k - i < -half_lanes]
    total_ref[...] = jnp.zeros_like(total_ref)

    def bands(source, slot):
        at = source * ranks if isinstance(source, int) else pl.multiple_of(source * ranks, ranks)
        lines = [taps_ref[n, pl.ds(at, ranks), :] for n in range(4)]
        y_lines = lines[2:]
        for r in range(ranks):
            re, im = (rolled(line[r : r + 1], mine) for line in lines[:2])
            top = 2 * r * mine
            column_ref[slot, top : top + mine, :LANES] = re.astype(column_ref.dtype)
            column_ref[slot, top : top + mine, LANES:] = (-im).astype(column_ref.dtype)
            column_ref[slot, top + mine : top + 2 * mine, :LANES] = im.astype(column_ref.dtype)
            column_ref[slot, top + mine : top + 2 * mine, LANES:] = re.astype(column_ref.dtype)
        for r in range(ranks):
            for part in range(2):
                ring = rolled(y_lines[part][r : r + 1], LANES)
                for n, mask in enumerate(masks):
                    band = [
                        jnp.where(mask[:rim], ring[:rim], 0.0),
                        ring[rim : LANES - rim] if n == windows // 2 else jnp.zeros((LANES - 2 * rim, LANES), F32),
                        jnp.where(mask[LANES - rim :], ring[LANES - rim :], 0.0),
                    ]
                    row_ref[slot, n, r * LANES : (r + 1) * LANES, part * LANES : (part + 1) * LANES] = jnp.concatenate(
                        band, axis=0
                    ).astype(BF16)

    def column_pass(slot):
        passed = jnp.dot(column_ref[slot].astype(BF16), field_ref[...], preferred_element_type=F32)
        for chunk in range(chunks):
            for r in range(ranks):
                cells = []
                for part in range(2):
                    for comp in range(comps):
                        top, left = (2 * r + part) * mine, comp * slab_rows + chunk * LANES
                        cells.append(passed[top : top + mine, left : left + LANES])
                lhs_ref[slot, chunk, :, r * LANES : (r + 1) * LANES] = jnp.concatenate(cells, axis=0).astype(BF16)

    def row_pass(source, slot):
        weight = got_ref[source, 0].astype(F32)[2 * ranks : 2 * ranks + 1, LANES - rim : LANES]
        weight = weight[:, 2:3] + weight[:, 3:4] + weight[:, 4:5]
        for chunk in range(chunks):
            image = None
            for n in range(windows):
                other = chunk + n - windows // 2
                if 0 <= other < chunks:
                    term = jnp.dot(lhs_ref[slot, other], row_ref[slot, n], preferred_element_type=F32)
                    image = term if image is None else image + term
            of_re, of_im = image[: comps * mine], image[comps * mine :]
            image_re = of_re[:, :LANES] - of_im[:, LANES:]
            image_im = of_re[:, LANES:] + of_im[:, :LANES]
            square = image_re * image_re + image_im * image_im
            power = square[:mine]
            for comp in range(1, comps):
                power = power + square[comp * mine : (comp + 1) * mine]
            total_ref[:, chunk * LANES : (chunk + 1) * LANES] += weight * power

    if sources <= 8:
        bands(0, 0)
        column_pass(0)
        bands(1, 1)
        for source in range(sources):
            if source + 1 < sources:
                column_pass(source + 1)
            if source + 2 < sources:
                bands(source + 2, source + 2)
            row_pass(source, source)
    else:

        def one_source(source, _):
            bands(source, 0)
            column_pass(0)
            row_pass(source, 0)

        lax.fori_loop(0, sources, one_source, None)
    for chunk in range(chunks):
        lines = total_ref[:, chunk * LANES : (chunk + 1) * LANES].T
        for piece in range(LANES // rows):
            tile, source = divmod((chunk * LANES) // rows + piece, sources)
            block = lines[piece * rows : (piece + 1) * rows]
            step = out_ref.shape[2]
            groups = [block[n : n + step] for n in range(0, rows, step)]
            out_ref[source, tile] = jnp.concatenate(groups, axis=1)


def merge_kernel(parts_ref, out_ref):
    devices = parts_ref.shape[0]
    mine = out_ref.shape[2] // devices
    blocks = []
    for device in range(devices):
        part = parts_ref[device]
        groups = [part[:, at : at + mine] for at in range(0, part.shape[1], mine)]
        blocks.append(jnp.concatenate(groups, axis=0))
    out_ref[0] = jnp.concatenate(blocks, axis=1)


def per_device(near_field, x_taps, y_taps, source_weight):
    sources, tiles = lax.axis_size("src"), lax.axis_size("tile")
    _, rows, _, comps, width = near_field.shape
    ranks, taps = x_taps.shape[-2:]
    rim = (taps - 1) // 2
    devices = sources * tiles
    mine = width // devices
    lanes = 2 * LANES
    slab_rows = devices * rows
    chunks = slab_rows // LANES
    windows = 1 if chunks == 1 else 3
    height = comps * rows
    step = max(1, rows * mine // LANES)
    params = pltpu.CompilerParams(vmem_limit_bytes=48 * 1024 * 1024)
    whole = pl.BlockSpec(memory_space=pltpu.VMEM)

    def in_hbm(array):
        return pltpu.with_memory_space_constraint(array, pltpu.HBM)

    send = pl.pallas_call(
        functools.partial(send_kernel, rim),
        out_shape=jax.ShapeDtypeStruct((sources, tiles, height, lanes), BF16),
        in_specs=[pl.BlockSpec(memory_space=pltpu.HBM)] * 3 + [pl.BlockSpec(memory_space=pltpu.SMEM)],
        out_specs=whole,
        scratch_shapes=[
            pltpu.VMEM((1, rows, comps, 2, width), BF16),
            pltpu.VMEM(x_taps.shape, BF16),
            pltpu.VMEM(y_taps.shape, BF16),
            pltpu.SemaphoreType.DMA((3,)),
        ],
        compiler_params=params,
        name="send_columns",
    )(in_hbm(near_field.transpose(0, 1, 3, 2, 4)), in_hbm(x_taps), in_hbm(y_taps), source_weight)
    got = lax.all_to_all(send.reshape(devices, height, lanes), ("src", "tile"), 0, 0).reshape(send.shape)
    slots = sources if sources <= 8 else 1
    image = pl.pallas_call(
        functools.partial(image_kernel, rim, comps, rows, ranks),
        out_shape=jax.ShapeDtypeStruct((sources, tiles, step, rows // step * mine), F32),
        in_specs=[whole],
        out_specs=whole,
        scratch_shapes=[
            pltpu.VMEM((lanes, comps * slab_rows), BF16),
            pltpu.VMEM((4, sources * ranks, LANES), F32),
            pltpu.VMEM((slots, 2 * ranks * mine, lanes), BF16 if mine % 16 == 0 else F32),
            pltpu.VMEM((slots, chunks, 2 * comps * mine, ranks * LANES), BF16),
            pltpu.VMEM((slots, windows, ranks * LANES, 2 * LANES), BF16),
            pltpu.VMEM((mine, slab_rows), F32),
        ],
        compiler_params=params,
        name="image",
    )(got)
    parts = lax.all_to_all(image.reshape((devices,) + image.shape[2:]), ("src", "tile"), 0, 0)
    return pl.pallas_call(
        merge_kernel,
        out_shape=jax.ShapeDtypeStruct((1, rows, width), F32),
        in_specs=[whole],
        out_specs=whole,
        compiler_params=params,
        name="merge_columns",
    )(parts)


def solution(mesh):
    placed = (
        P(("group", "tile"), "src", None, None, None),
        P("src", None, None, None),
        P("src", None, None, None),
        P("src"),
    )
    return jax.shard_map(
        per_device,
        mesh=mesh,
        in_specs=placed,
        out_specs=P(("group", "tile"), "src", None),
        check_vma=False,
    )
```

```python
import functools

import jax
import jax.numpy as jnp
from jax import lax
from jax.experimental import pallas as pl
from jax.experimental.pallas import tpu as pltpu
from jax.sharding import PartitionSpec as P

LANES = 128
F32 = jnp.float32
BF16 = jnp.bfloat16


def send_kernel(
    rim, field_hbm, x_taps_hbm, y_taps_hbm, weight_ref, send_ref, field_ref, x_taps_ref, y_taps_ref, sems
):
    pairs = ((field_hbm, field_ref), (x_taps_hbm, x_taps_ref), (y_taps_hbm, y_taps_ref))
    copies = [pltpu.make_async_copy(source, target, sems.at[n]) for n, (source, target) in enumerate(pairs)]
    for copy in copies:
        copy.start()
    for copy in copies:
        copy.wait()
    _, rows, comps, _, width = field_ref.shape
    tiles, sources, height, lanes = send_ref.shape
    ranks, taps = x_taps_ref.shape[2:]
    mine = width // (sources * tiles)
    window = mine + 2 * rim
    edge = jnp.zeros((rows, rim), F32)
    field = field_ref[0].astype(F32)
    padded = [
        [jnp.concatenate([edge, field[:, comp, part, :], edge], axis=1) for part in range(2)] for comp in range(comps)
    ]
    lower = lax.axis_index("tile") == 0
    lines = [
        jnp.where(lower, x_taps_ref[0, part].astype(F32), y_taps_ref[0, part].astype(F32)) for part in range(2)
    ]
    weight = jnp.full((ranks, 1), weight_ref[0], F32)
    high = weight.astype(BF16).astype(F32)
    middle = (weight - high).astype(BF16).astype(F32)
    low = weight - high - middle
    last = [line[:, taps - 1 :] for line in lines] + [high, middle, low]
    last.append(jnp.zeros((ranks, taps - 1 - len(last)), F32))
    spare = jnp.concatenate([line[:, : taps - 1] for line in lines] + [jnp.concatenate(last, axis=1)], axis=0)
    spares = [spare[:, :rim], spare[:, rim:]]
    if window < LANES - rim:
        gap = jnp.zeros((height, LANES - rim - window), F32)
        spares = [jnp.concatenate([gap, part], axis=1) for part in spares]
    for device in range(sources * tiles):
        at = device * mine
        cells = []
        for part in range(2):
            plane = [padded[comp][part][:, at : at + window] for comp in range(comps)]
            cells += [jnp.concatenate(plane, axis=0), spares[part]]
        tile, source = divmod(device, sources)
        send_ref[tile, source] = jnp.concatenate(cells, axis=1).astype(BF16)


def rolled(line, count):
    return pltpu.roll(jnp.broadcast_to(line, (count, line.shape[1])), 0, 1, stride=1, stride_axis=0)


def image_kernel(rim, comps, rows, ranks, got_ref, out_ref, field_ref, taps_ref, column_ref, lhs_ref, row_ref, total_ref):
    tiles, sources, _, lanes = got_ref.shape
    mine, slab_rows = total_ref.shape
    window = mine + 2 * rim
    tile_rows = sources * rows
    chunks = slab_rows // LANES
    windows = row_ref.shape[1]
    half_lanes = LANES // 2
    for tile in range(tiles):
        cells = got_ref[tile].astype(F32)
        for comp in range(comps):
            some = cells[:, comp * rows : (comp + 1) * rows, :].reshape(tile_rows, lanes).astype(BF16)
            at = comp * slab_rows + tile * tile_rows
            field_ref[at : at + tile_rows, :] = some

    tap = lax.broadcasted_iota(jnp.int32, (2 * rim, LANES), 0)
    lane = lax.broadcasted_iota(jnp.int32, (2 * rim, LANES), 1)
    x_place = (lane == tap).astype(BF16)
    y_place = (lane == (rim - tap) % LANES).astype(BF16)
    x_last = (lane[:1] == 2 * rim).astype(F32)
    y_last = (lane[:1] == LANES - rim).astype(F32)
    for n, (place, last_place) in enumerate(((x_place, x_last), (y_place, y_last))):
        block = got_ref[n].astype(F32)
        taps = jnp.concatenate([block[:, :, LANES - rim : LANES], block[:, :, 2 * LANES - rim :]], axis=2)
        for part in range(2):
            first = taps[:, part * ranks : (part + 1) * ranks].reshape(sources * ranks, 2 * rim)
            last = taps[:, 2 * ranks : 3 * ranks].reshape(sources * ranks, 2 * rim)[:, part : part + 1]
            line = jnp.dot(first.astype(BF16), place, preferred_element_type=F32) + last * last_place
            taps_ref[2 * n + part] = line
    k = lax.broadcasted_iota(jnp.int32, (LANES, LANES), 0)
    i = lax.broadcasted_iota(jnp.int32, (LANES, LANES), 1)
    near = jnp.abs(i - k) < half_lanes
    masks = [near] if windows == 1 else [k - i > half_lanes, near, k - i < -half_lanes]
    total_ref[...] = jnp.zeros_like(total_ref)

    def bands(source, slot):
        at = source * ranks if isinstance(source, int) else pl.multiple_of(source * ranks, ranks)
        lines = [taps_ref[n, pl.ds(at, ranks), :] for n in range(4)]
        y_lines = lines[2:]
        for r in range(ranks):
            re, im = (rolled(line[r : r + 1], mine) for line in lines[:2])
            top = 2 * r * mine
            column_ref[slot, top : top + mine, :LANES] = re.astype(column_ref.dtype)
            column_ref[slot, top : top + mine, LANES:] = (-im).astype(column_ref.dtype)
            column_ref[slot, top + mine : top + 2 * mine, :LANES] = im.astype(column_ref.dtype)
            column_ref[slot, top + mine : top + 2 * mine, LANES:] = re.astype(column_ref.dtype)
        for r in range(ranks):
            for part in range(2):
                ring = rolled(y_lines[part][r : r + 1], LANES)
                for n, mask in enumerate(masks):
                    band = [
                        jnp.where(mask[:rim], ring[:rim], 0.0),
                        ring[rim : LANES - rim] if n == windows // 2 else jnp.zeros((LANES - 2 * rim, LANES), F32),
                        jnp.where(mask[LANES - rim :], ring[LANES - rim :], 0.0),
                    ]
                    row_ref[slot, n, r * LANES : (r + 1) * LANES, part * LANES : (part + 1) * LANES] = jnp.concatenate(
                        band, axis=0
                    ).astype(BF16)

    def column_pass(slot):
        passed = lax.dot_general(
            column_ref[slot].astype(BF16), field_ref[...], (((1,), (1,)), ((), ())), preferred_element_type=F32
        )
        for chunk in range(chunks):
            for r in range(ranks):
                cells = []
                for part in range(2):
                    for comp in range(comps):
                        top, left = (2 * r + part) * mine, comp * slab_rows + chunk * LANES
                        cells.append(passed[top : top + mine, left : left + LANES])
                lhs_ref[slot, chunk, :, r * LANES : (r + 1) * LANES] = jnp.concatenate(cells, axis=0).astype(BF16)

    def row_pass(source, slot):
        weight = got_ref[0, source].astype(F32)[2 * ranks : 2 * ranks + 1, LANES - rim : LANES]
        weight = weight[:, 2:3] + weight[:, 3:4] + weight[:, 4:5]
        for chunk in range(chunks):
            image = None
            for n in range(windows):
                other = chunk + n - windows // 2
                if 0 <= other < chunks:
                    term = jnp.dot(lhs_ref[slot, other], row_ref[slot, n], preferred_element_type=F32)
                    image = term if image is None else image + term
            of_re, of_im = image[: comps * mine], image[comps * mine :]
            image_re = of_re[:, :LANES] - of_im[:, LANES:]
            image_im = of_re[:, LANES:] + of_im[:, :LANES]
            square = image_re * image_re + image_im * image_im
            power = square[:mine]
            for comp in range(1, comps):
                power = power + square[comp * mine : (comp + 1) * mine]
            total_ref[:, chunk * LANES : (chunk + 1) * LANES] += weight * power

    if sources <= 8:
        bands(0, 0)
        column_pass(0)
        bands(1, 1)
        for source in range(sources):
            if source + 1 < sources:
                column_pass(source + 1)
            if source + 2 < sources:
                bands(source + 2, source + 2)
            row_pass(source, source)
    else:

        def one_source(source, _):
            bands(source, 0)
            column_pass(0)
            row_pass(source, 0)

        lax.fori_loop(0, sources, one_source, None)
    for chunk in range(chunks):
        lines = total_ref[:, chunk * LANES : (chunk + 1) * LANES].T
        for piece in range(LANES // rows):
            tile, source = divmod((chunk * LANES) // rows + piece, sources)
            block = lines[piece * rows : (piece + 1) * rows]
            step = out_ref.shape[2]
            groups = [block[n : n + step] for n in range(0, rows, step)]
            out_ref[tile, source] = jnp.concatenate(groups, axis=1)


def merge_kernel(parts_ref, out_ref):
    devices = parts_ref.shape[0]
    mine = out_ref.shape[2] // devices
    blocks = []
    for device in range(devices):
        part = parts_ref[device]
        groups = [part[:, at : at + mine] for at in range(0, part.shape[1], mine)]
        blocks.append(jnp.concatenate(groups, axis=0))
    out_ref[0] = jnp.concatenate(blocks, axis=1)


def per_device(near_field, x_taps, y_taps, source_weight):
    sources, tiles = lax.axis_size("src"), lax.axis_size("tile")
    _, rows, _, comps, width = near_field.shape
    ranks, taps = x_taps.shape[-2:]
    rim = (taps - 1) // 2
    devices = sources * tiles
    mine = width // devices
    lanes = 2 * LANES
    slab_rows = devices * rows
    chunks = slab_rows // LANES
    windows = 1 if chunks == 1 else 3
    height = comps * rows
    step = max(1, rows * mine // LANES)
    params = pltpu.CompilerParams(vmem_limit_bytes=48 * 1024 * 1024)
    whole = pl.BlockSpec(memory_space=pltpu.VMEM)

    def in_hbm(array):
        return pltpu.with_memory_space_constraint(array, pltpu.HBM)

    send = pl.pallas_call(
        functools.partial(send_kernel, rim),
        out_shape=jax.ShapeDtypeStruct((tiles, sources, height, lanes), BF16),
        in_specs=[pl.BlockSpec(memory_space=pltpu.HBM)] * 3 + [pl.BlockSpec(memory_space=pltpu.SMEM)],
        out_specs=whole,
        scratch_shapes=[
            pltpu.VMEM((1, rows, comps, 2, width), BF16),
            pltpu.VMEM(x_taps.shape, BF16),
            pltpu.VMEM(y_taps.shape, BF16),
            pltpu.SemaphoreType.DMA((3,)),
        ],
        compiler_params=params,
        name="send_columns",
    )(in_hbm(near_field.transpose(0, 1, 3, 2, 4)), in_hbm(x_taps), in_hbm(y_taps), source_weight)
    got = lax.all_to_all(send.reshape(devices, height, lanes), ("tile", "src"), 0, 0).reshape(send.shape)
    slots = sources if sources <= 8 else 1
    image = pl.pallas_call(
        functools.partial(image_kernel, rim, comps, rows, ranks),
        out_shape=jax.ShapeDtypeStruct((tiles, sources, step, rows // step * mine), F32),
        in_specs=[whole],
        out_specs=whole,
        scratch_shapes=[
            pltpu.VMEM((comps * slab_rows, lanes), BF16),
            pltpu.VMEM((4, sources * ranks, LANES), F32),
            pltpu.VMEM((slots, 2 * ranks * mine, lanes), BF16 if mine % 16 == 0 else F32),
            pltpu.VMEM((slots, chunks, 2 * comps * mine, ranks * LANES), BF16),
            pltpu.VMEM((slots, windows, ranks * LANES, 2 * LANES), BF16),
            pltpu.VMEM((mine, slab_rows), F32),
        ],
        compiler_params=params,
        name="image",
    )(got)
    parts = lax.all_to_all(image.reshape((devices,) + image.shape[2:]), ("tile", "src"), 0, 0)
    return pl.pallas_call(
        merge_kernel,
        out_shape=jax.ShapeDtypeStruct((1, rows, width), F32),
        in_specs=[whole],
        out_specs=whole,
        compiler_params=params,
        name="merge_columns",
    )(parts)


def solution(mesh):
    placed = (
        P(("group", "tile"), "src", None, None, None),
        P("src", None, None, None),
        P("src", None, None, None),
        P("src"),
    )
    return jax.shard_map(
        per_device,
        mesh=mesh,
        in_specs=placed,
        out_specs=P(("group", "tile"), "src", None),
        check_vma=False,
    )
```

```python
import functools

import jax
import jax.numpy as jnp
from jax import lax
from jax.experimental import pallas as pl
from jax.experimental.pallas import tpu as pltpu
from jax.sharding import PartitionSpec as P

LANES = 128
F32 = jnp.float32
BF16 = jnp.bfloat16


def send_kernel(
    rim, field_hbm, x_taps_hbm, y_taps_hbm, weight_ref, send_ref, field_ref, x_taps_ref, y_taps_ref, sems
):
    pairs = ((field_hbm, field_ref), (x_taps_hbm, x_taps_ref), (y_taps_hbm, y_taps_ref))
    copies = [pltpu.make_async_copy(source, target, sems.at[n]) for n, (source, target) in enumerate(pairs)]
    for copy in copies:
        copy.start()
    for copy in copies:
        copy.wait()
    _, rows, comps, _, width = field_ref.shape
    sources, tiles, height, lanes = send_ref.shape
    ranks, taps = x_taps_ref.shape[2:]
    mine = width // (sources * tiles)
    window = mine + 2 * rim
    edge = jnp.zeros((rows, rim), F32)
    field = field_ref[0].astype(F32)
    padded = [
        [jnp.concatenate([edge, field[:, comp, part, :], edge], axis=1) for part in range(2)] for comp in range(comps)
    ]
    lower = lax.axis_index("tile") == 0
    lines = [
        jnp.where(lower, x_taps_ref[0, part].astype(F32), y_taps_ref[0, part].astype(F32)) for part in range(2)
    ]
    weight = jnp.full((ranks, 1), weight_ref[0], F32)
    high = weight.astype(BF16).astype(F32)
    middle = (weight - high).astype(BF16).astype(F32)
    low = weight - high - middle
    last = [line[:, taps - 1 :] for line in lines] + [high, middle, low]
    last.append(jnp.zeros((ranks, taps - 1 - len(last)), F32))
    spare = jnp.concatenate([line[:, : taps - 1] for line in lines] + [jnp.concatenate(last, axis=1)], axis=0)
    spares = [spare[:, :rim], spare[:, rim:]]
    if window < LANES - rim:
        gap = jnp.zeros((height, LANES - rim - window), F32)
        spares = [jnp.concatenate([gap, part], axis=1) for part in spares]
    for device in range(sources * tiles):
        at = device * mine
        cells = []
        for part in range(2):
            plane = [padded[comp][part][:, at : at + window] for comp in range(comps)]
            cells += [jnp.concatenate(plane, axis=0), spares[part]]
        source, tile = divmod(device, tiles)
        send_ref[source, tile] = jnp.concatenate(cells, axis=1).astype(BF16)


def rolled(line, count):
    return pltpu.roll(jnp.broadcast_to(line, (count, line.shape[1])), 0, 1, stride=1, stride_axis=0)


def image_kernel(rim, comps, rows, ranks, got_ref, out_ref, field_ref, taps_ref, column_ref, lhs_ref, row_ref, total_ref):
    sources, tiles, _, lanes = got_ref.shape
    mine, slab_rows = total_ref.shape
    window = mine + 2 * rim
    tile_rows = sources * rows
    chunks = slab_rows // LANES
    windows = row_ref.shape[1]
    half_lanes = LANES // 2
    for tile in range(tiles):
        cells = got_ref[:, tile].astype(F32)
        for comp in range(comps):
            some = cells[:, comp * rows : (comp + 1) * rows, :].reshape(tile_rows, lanes).astype(BF16)
            at = comp * slab_rows + tile * tile_rows
            field_ref[at : at + tile_rows, :] = some

    tap = lax.broadcasted_iota(jnp.int32, (2 * rim, LANES), 0)
    lane = lax.broadcasted_iota(jnp.int32, (2 * rim, LANES), 1)
    x_place = (lane == tap).astype(BF16)
    y_place = (lane == (rim - tap) % LANES).astype(BF16)
    x_last = (lane[:1] == 2 * rim).astype(F32)
    y_last = (lane[:1] == LANES - rim).astype(F32)
    for n, (place, last_place) in enumerate(((x_place, x_last), (y_place, y_last))):
        block = got_ref[:, n].astype(F32)
        taps = jnp.concatenate([block[:, :, LANES - rim : LANES], block[:, :, 2 * LANES - rim :]], axis=2)
        for part in range(2):
            first = taps[:, part * ranks : (part + 1) * ranks].reshape(sources * ranks, 2 * rim)
            last = taps[:, 2 * ranks : 3 * ranks].reshape(sources * ranks, 2 * rim)[:, part : part + 1]
            line = jnp.dot(first.astype(BF16), place, preferred_element_type=F32) + last * last_place
            taps_ref[2 * n + part] = line
    k = lax.broadcasted_iota(jnp.int32, (LANES, LANES), 0)
    i = lax.broadcasted_iota(jnp.int32, (LANES, LANES), 1)
    near = jnp.abs(i - k) < half_lanes
    masks = [near] if windows == 1 else [k - i > half_lanes, near, k - i < -half_lanes]
    total_ref[...] = jnp.zeros_like(total_ref)

    def bands(source, slot):
        at = source * ranks if isinstance(source, int) else pl.multiple_of(source * ranks, ranks)
        lines = [taps_ref[n, pl.ds(at, ranks), :] for n in range(4)]
        y_lines = lines[2:]
        for r in range(ranks):
            re, im = (rolled(line[r : r + 1], mine) for line in lines[:2])
            top = 2 * r * mine
            column_ref[slot, top : top + mine, :LANES] = re.astype(column_ref.dtype)
            column_ref[slot, top : top + mine, LANES:] = (-im).astype(column_ref.dtype)
            column_ref[slot, top + mine : top + 2 * mine, :LANES] = im.astype(column_ref.dtype)
            column_ref[slot, top + mine : top + 2 * mine, LANES:] = re.astype(column_ref.dtype)
        for r in range(ranks):
            for part in range(2):
                ring = rolled(y_lines[part][r : r + 1], LANES)
                for n, mask in enumerate(masks):
                    band = [
                        jnp.where(mask[:rim], ring[:rim], 0.0),
                        ring[rim : LANES - rim] if n == windows // 2 else jnp.zeros((LANES - 2 * rim, LANES), F32),
                        jnp.where(mask[LANES - rim :], ring[LANES - rim :], 0.0),
                    ]
                    row_ref[slot, n, r * LANES : (r + 1) * LANES, part * LANES : (part + 1) * LANES] = jnp.concatenate(
                        band, axis=0
                    ).astype(BF16)

    def column_pass(slot, count):
        height = 2 * ranks * mine
        passed = lax.dot_general(
            column_ref[slot : slot + count].reshape(count * height, lanes).astype(BF16),
            field_ref[...],
            (((1,), (1,)), ((), ())),
            preferred_element_type=F32,
        )
        for n in range(count):
            for chunk in range(chunks):
                for r in range(ranks):
                    cells = []
                    for part in range(2):
                        for comp in range(comps):
                            top, left = n * height + (2 * r + part) * mine, comp * slab_rows + chunk * LANES
                            cells.append(passed[top : top + mine, left : left + LANES])
                    cells = jnp.concatenate(cells, axis=0).astype(BF16)
                    lhs_ref[slot + n, chunk, :, r * LANES : (r + 1) * LANES] = cells

    def row_pass(source, slot):
        weight = got_ref[source, 0].astype(F32)[2 * ranks : 2 * ranks + 1, LANES - rim : LANES]
        weight = weight[:, 2:3] + weight[:, 3:4] + weight[:, 4:5]
        for chunk in range(chunks):
            image = None
            for n in range(windows):
                other = chunk + n - windows // 2
                if 0 <= other < chunks:
                    term = jnp.dot(lhs_ref[slot, other], row_ref[slot, n], preferred_element_type=F32)
                    image = term if image is None else image + term
            of_re, of_im = image[: comps * mine], image[comps * mine :]
            image_re = of_re[:, :LANES] - of_im[:, LANES:]
            image_im = of_re[:, LANES:] + of_im[:, :LANES]
            square = image_re * image_re + image_im * image_im
            power = square[:mine]
            for comp in range(1, comps):
                power = power + square[comp * mine : (comp + 1) * mine]
            total_ref[:, chunk * LANES : (chunk + 1) * LANES] += weight * power

    if sources <= 8:
        count = 2 if sources % 2 == 0 else 1
        steps = list(range(0, sources, count))

        def prepare(step):
            for source in range(step, min(step + count, sources)):
                bands(source, source)

        prepare(0)
        column_pass(0, count)
        prepare(count)
        for step in steps:
            if step + count < sources:
                column_pass(step + count, count)
            prepare(step + 2 * count)
            for source in range(step, step + count):
                row_pass(source, source)
    else:

        def one_source(source, _):
            bands(source, 0)
            column_pass(0, 1)
            row_pass(source, 0)

        lax.fori_loop(0, sources, one_source, None)
    for chunk in range(chunks):
        lines = total_ref[:, chunk * LANES : (chunk + 1) * LANES].T
        for piece in range(LANES // rows):
            tile, source = divmod((chunk * LANES) // rows + piece, sources)
            block = lines[piece * rows : (piece + 1) * rows]
            step = out_ref.shape[2]
            groups = [block[n : n + step] for n in range(0, rows, step)]
            out_ref[source, tile] = jnp.concatenate(groups, axis=1)


def merge_kernel(parts_ref, out_ref):
    devices = parts_ref.shape[0]
    mine = out_ref.shape[2] // devices
    blocks = []
    for device in range(devices):
        part = parts_ref[device]
        groups = [part[:, at : at + mine] for at in range(0, part.shape[1], mine)]
        blocks.append(jnp.concatenate(groups, axis=0))
    out_ref[0] = jnp.concatenate(blocks, axis=1)


def per_device(near_field, x_taps, y_taps, source_weight):
    sources, tiles = lax.axis_size("src"), lax.axis_size("tile")
    _, rows, _, comps, width = near_field.shape
    ranks, taps = x_taps.shape[-2:]
    rim = (taps - 1) // 2
    devices = sources * tiles
    mine = width // devices
    lanes = 2 * LANES
    slab_rows = devices * rows
    chunks = slab_rows // LANES
    windows = 1 if chunks == 1 else 3
    height = comps * rows
    step = max(1, rows * mine // LANES)
    params = pltpu.CompilerParams(vmem_limit_bytes=48 * 1024 * 1024)
    whole = pl.BlockSpec(memory_space=pltpu.VMEM)

    def in_hbm(array):
        return pltpu.with_memory_space_constraint(array, pltpu.HBM)

    send = pl.pallas_call(
        functools.partial(send_kernel, rim),
        out_shape=jax.ShapeDtypeStruct((sources, tiles, height, lanes), BF16),
        in_specs=[pl.BlockSpec(memory_space=pltpu.HBM)] * 3 + [pl.BlockSpec(memory_space=pltpu.SMEM)],
        out_specs=whole,
        scratch_shapes=[
            pltpu.VMEM((1, rows, comps, 2, width), BF16),
            pltpu.VMEM(x_taps.shape, BF16),
            pltpu.VMEM(y_taps.shape, BF16),
            pltpu.SemaphoreType.DMA((3,)),
        ],
        compiler_params=params,
        name="send_columns",
    )(in_hbm(near_field.transpose(0, 1, 3, 2, 4)), in_hbm(x_taps), in_hbm(y_taps), source_weight)
    got = lax.all_to_all(send.reshape(devices, height, lanes), ("src", "tile"), 0, 0).reshape(send.shape)
    slots = sources if sources <= 8 else 1
    image = pl.pallas_call(
        functools.partial(image_kernel, rim, comps, rows, ranks),
        out_shape=jax.ShapeDtypeStruct((sources, tiles, step, rows // step * mine), F32),
        in_specs=[whole],
        out_specs=whole,
        scratch_shapes=[
            pltpu.VMEM((comps * slab_rows, lanes), BF16),
            pltpu.VMEM((4, sources * ranks, LANES), F32),
            pltpu.VMEM((slots, 2 * ranks * mine, lanes), BF16 if mine % 16 == 0 else F32),
            pltpu.VMEM((slots, chunks, 2 * comps * mine, ranks * LANES), BF16),
            pltpu.VMEM((slots, windows, ranks * LANES, 2 * LANES), BF16),
            pltpu.VMEM((mine, slab_rows), F32),
        ],
        compiler_params=params,
        name="image",
    )(got)
    parts = lax.all_to_all(image.reshape((devices,) + image.shape[2:]), ("src", "tile"), 0, 0)
    return pl.pallas_call(
        merge_kernel,
        out_shape=jax.ShapeDtypeStruct((1, rows, width), F32),
        in_specs=[whole],
        out_specs=whole,
        compiler_params=params,
        name="merge_columns",
    )(parts)


def solution(mesh):
    placed = (
        P(("group", "tile"), "src", None, None, None),
        P("src", None, None, None),
        P("src", None, None, None),
        P("src"),
    )
    return jax.shard_map(
        per_device,
        mesh=mesh,
        in_specs=placed,
        out_specs=P(("group", "tile"), "src", None),
        check_vma=False,
    )
```

```python
import functools

import jax
import jax.numpy as jnp
from jax import lax
from jax.experimental import pallas as pl
from jax.experimental.pallas import tpu as pltpu
from jax.sharding import PartitionSpec as P

LANES = 128
F32 = jnp.float32
BF16 = jnp.bfloat16


def send_kernel(
    rim, field_hbm, x_taps_hbm, y_taps_hbm, weight_ref, send_ref, field_ref, x_taps_ref, y_taps_ref, sems
):
    pairs = ((field_hbm, field_ref), (x_taps_hbm, x_taps_ref), (y_taps_hbm, y_taps_ref))
    copies = [pltpu.make_async_copy(source, target, sems.at[n]) for n, (source, target) in enumerate(pairs)]
    for copy in copies:
        copy.start()
    for copy in copies:
        copy.wait()
    _, rows, comps, _, width = field_ref.shape
    sources, tiles, height, lanes = send_ref.shape
    ranks, taps = x_taps_ref.shape[2:]
    mine = width // (sources * tiles)
    window = mine + 2 * rim
    edge = jnp.zeros((rows, rim), F32)
    field = field_ref[0].astype(F32)
    padded = [
        [jnp.concatenate([edge, field[:, comp, part, :], edge], axis=1) for part in range(2)] for comp in range(comps)
    ]
    lower = lax.axis_index("tile") == 0
    lines = [
        jnp.where(lower, x_taps_ref[0, part].astype(F32), y_taps_ref[0, part].astype(F32)) for part in range(2)
    ]
    weight = jnp.full((ranks, 1), weight_ref[0], F32)
    high = weight.astype(BF16).astype(F32)
    middle = (weight - high).astype(BF16).astype(F32)
    low = weight - high - middle
    last = [line[:, taps - 1 :] for line in lines] + [high, middle, low]
    last.append(jnp.zeros((ranks, taps - 1 - len(last)), F32))
    spare = jnp.concatenate([line[:, : taps - 1] for line in lines] + [jnp.concatenate(last, axis=1)], axis=0)
    spares = [spare[:, :rim], spare[:, rim:]]
    if window < LANES - rim:
        gap = jnp.zeros((height, LANES - rim - window), F32)
        spares = [jnp.concatenate([gap, part], axis=1) for part in spares]
    for device in range(sources * tiles):
        at = device * mine
        cells = []
        for part in range(2):
            plane = [padded[comp][part][:, at : at + window] for comp in range(comps)]
            cells += [jnp.concatenate(plane, axis=0), spares[part]]
        source, tile = divmod(device, tiles)
        send_ref[source, tile] = jnp.concatenate(cells, axis=1).astype(BF16)


def rolled(line, count):
    return pltpu.roll(jnp.broadcast_to(line, (count, line.shape[1])), 0, 1, stride=1, stride_axis=0)


def image_kernel(rim, comps, rows, ranks, got_ref, out_ref, field_ref, taps_ref, column_ref, lhs_ref, row_ref, total_ref):
    sources, tiles, _, lanes = got_ref.shape
    mine, slab_rows = total_ref.shape
    window = mine + 2 * rim
    tile_rows = sources * rows
    chunks = slab_rows // LANES
    windows = row_ref.shape[1]
    half_lanes = LANES // 2
    for tile in range(tiles):
        cells = got_ref[:, tile].astype(F32)
        for comp in range(comps):
            some = cells[:, comp * rows : (comp + 1) * rows, :].reshape(tile_rows, lanes).astype(BF16)
            at = comp * slab_rows + tile * tile_rows
            field_ref[at : at + tile_rows, :] = some

    tap = lax.broadcasted_iota(jnp.int32, (2 * rim, LANES), 0)
    lane = lax.broadcasted_iota(jnp.int32, (2 * rim, LANES), 1)
    x_place = (lane == tap).astype(BF16)
    y_place = (lane == (rim - tap) % LANES).astype(BF16)
    x_last = (lane[:1] == 2 * rim).astype(F32)
    y_last = (lane[:1] == LANES - rim).astype(F32)
    for n, (place, last_place) in enumerate(((x_place, x_last), (y_place, y_last))):
        block = got_ref[:, n].astype(F32)
        taps = jnp.concatenate([block[:, :, LANES - rim : LANES], block[:, :, 2 * LANES - rim :]], axis=2)
        for part in range(2):
            first = taps[:, part * ranks : (part + 1) * ranks].reshape(sources * ranks, 2 * rim)
            last = taps[:, 2 * ranks : 3 * ranks].reshape(sources * ranks, 2 * rim)[:, part : part + 1]
            line = jnp.dot(first.astype(BF16), place, preferred_element_type=F32) + last * last_place
            taps_ref[2 * n + part] = line
    k = lax.broadcasted_iota(jnp.int32, (LANES, LANES), 0)
    i = lax.broadcasted_iota(jnp.int32, (LANES, LANES), 1)
    near = jnp.abs(i - k) < half_lanes
    masks = [near] if windows == 1 else [k - i > half_lanes, near, k - i < -half_lanes]
    masks = [jnp.where(mask, 1.0, 0.0).astype(BF16) for mask in masks]
    total_ref[...] = jnp.zeros_like(total_ref)

    def bands(source, slot):
        at = source * ranks if isinstance(source, int) else pl.multiple_of(source * ranks, ranks)
        lines = [taps_ref[n, pl.ds(at, ranks), :] for n in range(4)]
        y_lines = lines[2:]
        for r in range(ranks):
            re, im = (rolled(line[r : r + 1], mine) for line in lines[:2])
            top = 2 * r * mine
            column_ref[slot, top : top + mine, :LANES] = re.astype(column_ref.dtype)
            column_ref[slot, top : top + mine, LANES:] = (-im).astype(column_ref.dtype)
            column_ref[slot, top + mine : top + 2 * mine, :LANES] = im.astype(column_ref.dtype)
            column_ref[slot, top + mine : top + 2 * mine, LANES:] = re.astype(column_ref.dtype)
        for r in range(ranks):
            for part in range(2):
                base = rolled(y_lines[part][r : r + 1], 16).astype(BF16)
                for top in range(0, LANES, 16):
                    block = pltpu.roll(base, top, 1) if top > 0 else base
                    inner = rim <= top < LANES - rim
                    for n, mask in enumerate(masks):
                        if not inner:
                            cells = block * mask[top : top + 16]
                        else:
                            cells = block if n == windows // 2 else jnp.zeros_like(block)
                        at = r * LANES + top
                        row_ref[slot, n, at : at + 16, part * LANES : (part + 1) * LANES] = cells

    def column_pass(slot):
        passed = lax.dot_general(
            column_ref[slot].astype(BF16), field_ref[...], (((1,), (1,)), ((), ())), preferred_element_type=F32
        )
        for chunk in range(chunks):
            for r in range(ranks):
                cells = []
                for part in range(2):
                    for comp in range(comps):
                        top, left = (2 * r + part) * mine, comp * slab_rows + chunk * LANES
                        cells.append(passed[top : top + mine, left : left + LANES])
                lhs_ref[slot, chunk, :, r * LANES : (r + 1) * LANES] = jnp.concatenate(cells, axis=0).astype(BF16)

    def row_pass(source, slot):
        weight = got_ref[source, 0].astype(F32)[2 * ranks : 2 * ranks + 1, LANES - rim : LANES]
        weight = weight[:, 2:3] + weight[:, 3:4] + weight[:, 4:5]
        for chunk in range(chunks):
            image = None
            for n in range(windows):
                other = chunk + n - windows // 2
                if 0 <= other < chunks:
                    term = jnp.dot(lhs_ref[slot, other], row_ref[slot, n], preferred_element_type=F32)
                    image = term if image is None else image + term
            of_re, of_im = image[: comps * mine], image[comps * mine :]
            image_re = of_re[:, :LANES] - of_im[:, LANES:]
            image_im = of_re[:, LANES:] + of_im[:, :LANES]
            square = image_re * image_re + image_im * image_im
            power = square[:mine]
            for comp in range(1, comps):
                power = power + square[comp * mine : (comp + 1) * mine]
            total_ref[:, chunk * LANES : (chunk + 1) * LANES] += weight * power

    if sources <= 8:
        bands(0, 0)
        column_pass(0)
        bands(1, 1)
        for source in range(sources):
            if source + 1 < sources:
                column_pass(source + 1)
            if source + 2 < sources:
                bands(source + 2, source + 2)
            row_pass(source, source)
    else:

        def one_source(source, _):
            bands(source, 0)
            column_pass(0)
            row_pass(source, 0)

        lax.fori_loop(0, sources, one_source, None)
    for chunk in range(chunks):
        lines = total_ref[:, chunk * LANES : (chunk + 1) * LANES].T
        for piece in range(LANES // rows):
            tile, source = divmod((chunk * LANES) // rows + piece, sources)
            block = lines[piece * rows : (piece + 1) * rows]
            step = out_ref.shape[2]
            groups = [block[n : n + step] for n in range(0, rows, step)]
            out_ref[source, tile] = jnp.concatenate(groups, axis=1)


def merge_kernel(parts_ref, out_ref):
    devices = parts_ref.shape[0]
    mine = out_ref.shape[2] // devices
    blocks = []
    for device in range(devices):
        part = parts_ref[device]
        groups = [part[:, at : at + mine] for at in range(0, part.shape[1], mine)]
        blocks.append(jnp.concatenate(groups, axis=0))
    out_ref[0] = jnp.concatenate(blocks, axis=1)


def per_device(near_field, x_taps, y_taps, source_weight):
    sources, tiles = lax.axis_size("src"), lax.axis_size("tile")
    _, rows, _, comps, width = near_field.shape
    ranks, taps = x_taps.shape[-2:]
    rim = (taps - 1) // 2
    devices = sources * tiles
    mine = width // devices
    lanes = 2 * LANES
    slab_rows = devices * rows
    chunks = slab_rows // LANES
    windows = 1 if chunks == 1 else 3
    height = comps * rows
    step = max(1, rows * mine // LANES)
    params = pltpu.CompilerParams(vmem_limit_bytes=48 * 1024 * 1024)
    whole = pl.BlockSpec(memory_space=pltpu.VMEM)

    def in_hbm(array):
        return pltpu.with_memory_space_constraint(array, pltpu.HBM)

    send = pl.pallas_call(
        functools.partial(send_kernel, rim),
        out_shape=jax.ShapeDtypeStruct((sources, tiles, height, lanes), BF16),
        in_specs=[pl.BlockSpec(memory_space=pltpu.HBM)] * 3 + [pl.BlockSpec(memory_space=pltpu.SMEM)],
        out_specs=whole,
        scratch_shapes=[
            pltpu.VMEM((1, rows, comps, 2, width), BF16),
            pltpu.VMEM(x_taps.shape, BF16),
            pltpu.VMEM(y_taps.shape, BF16),
            pltpu.SemaphoreType.DMA((3,)),
        ],
        compiler_params=params,
        name="send_columns",
    )(in_hbm(near_field.transpose(0, 1, 3, 2, 4)), in_hbm(x_taps), in_hbm(y_taps), source_weight)
    got = lax.all_to_all(send.reshape(devices, height, lanes), ("src", "tile"), 0, 0).reshape(send.shape)
    slots = sources if sources <= 8 else 1
    image = pl.pallas_call(
        functools.partial(image_kernel, rim, comps, rows, ranks),
        out_shape=jax.ShapeDtypeStruct((sources, tiles, step, rows // step * mine), F32),
        in_specs=[whole],
        out_specs=whole,
        scratch_shapes=[
            pltpu.VMEM((comps * slab_rows, lanes), BF16),
            pltpu.VMEM((4, sources * ranks, LANES), F32),
            pltpu.VMEM((slots, 2 * ranks * mine, lanes), BF16 if mine % 16 == 0 else F32),
            pltpu.VMEM((slots, chunks, 2 * comps * mine, ranks * LANES), BF16),
            pltpu.VMEM((slots, windows, ranks * LANES, 2 * LANES), BF16),
            pltpu.VMEM((mine, slab_rows), F32),
        ],
        compiler_params=params,
        name="image",
    )(got)
    parts = lax.all_to_all(image.reshape((devices,) + image.shape[2:]), ("src", "tile"), 0, 0)
    return pl.pallas_call(
        merge_kernel,
        out_shape=jax.ShapeDtypeStruct((1, rows, width), F32),
        in_specs=[whole],
        out_specs=whole,
        compiler_params=params,
        name="merge_columns",
    )(parts)


def solution(mesh):
    placed = (
        P(("group", "tile"), "src", None, None, None),
        P("src", None, None, None),
        P("src", None, None, None),
        P("src"),
    )
    return jax.shard_map(
        per_device,
        mesh=mesh,
        in_specs=placed,
        out_specs=P(("group", "tile"), "src", None),
        check_vma=False,
    )
```

```python
import functools

import jax
import jax.numpy as jnp
from jax import lax
from jax.experimental import pallas as pl
from jax.experimental.pallas import tpu as pltpu
from jax.sharding import PartitionSpec as P

LANES = 128
F32 = jnp.float32
BF16 = jnp.bfloat16


def send_kernel(
    rim, field_hbm, x_taps_hbm, y_taps_hbm, weight_ref, send_ref, field_ref, x_taps_ref, y_taps_ref, sems
):
    pairs = ((field_hbm, field_ref), (x_taps_hbm, x_taps_ref), (y_taps_hbm, y_taps_ref))
    copies = [pltpu.make_async_copy(source, target, sems.at[n]) for n, (source, target) in enumerate(pairs)]
    for copy in copies:
        copy.start()
    for copy in copies:
        copy.wait()
    _, rows, comps, _, width = field_ref.shape
    sources, tiles, height, lanes = send_ref.shape
    ranks, taps = x_taps_ref.shape[2:]
    mine = width // (sources * tiles)
    window = mine + 2 * rim
    edge = jnp.zeros((rows, rim), F32)
    field = field_ref[0].astype(F32)
    padded = [
        [jnp.concatenate([edge, field[:, comp, part, :], edge], axis=1) for part in range(2)] for comp in range(comps)
    ]
    lower = lax.axis_index("tile") == 0
    lines = [
        jnp.where(lower, x_taps_ref[0, part].astype(F32), y_taps_ref[0, part].astype(F32)) for part in range(2)
    ]
    weight = jnp.full((ranks, 1), weight_ref[0], F32)
    high = weight.astype(BF16).astype(F32)
    middle = (weight - high).astype(BF16).astype(F32)
    low = weight - high - middle
    last = [line[:, taps - 1 :] for line in lines] + [high, middle, low]
    last.append(jnp.zeros((ranks, taps - 1 - len(last)), F32))
    spare = jnp.concatenate([line[:, : taps - 1] for line in lines] + [jnp.concatenate(last, axis=1)], axis=0)
    spares = [spare[:, :rim], spare[:, rim:]]
    if window < LANES - rim:
        gap = jnp.zeros((height, LANES - rim - window), F32)
        spares = [jnp.concatenate([gap, part], axis=1) for part in spares]
    for device in range(sources * tiles):
        at = device * mine
        cells = []
        for part in range(2):
            plane = [padded[comp][part][:, at : at + window] for comp in range(comps)]
            cells += [jnp.concatenate(plane, axis=0), spares[part]]
        source, tile = divmod(device, tiles)
        send_ref[source, tile] = jnp.concatenate(cells, axis=1).astype(BF16)


def rolled(line, count):
    return pltpu.roll(jnp.broadcast_to(line, (count, line.shape[1])), 0, 1, stride=1, stride_axis=0)


def image_kernel(rim, comps, rows, ranks, got_ref, out_ref, field_ref, taps_ref, column_ref, lhs_ref, row_ref, total_ref):
    sources, tiles, _, lanes = got_ref.shape
    mine, slab_rows = total_ref.shape
    window = mine + 2 * rim
    tile_rows = sources * rows
    chunks = slab_rows // LANES
    windows = row_ref.shape[1]
    half_lanes = LANES // 2
    for tile in range(tiles):
        cells = got_ref[:, tile].astype(F32)
        for comp in range(comps):
            some = cells[:, comp * rows : (comp + 1) * rows, :].reshape(tile_rows, lanes).astype(BF16)
            at = comp * slab_rows + tile * tile_rows
            field_ref[at : at + tile_rows, :] = some

    tap = lax.broadcasted_iota(jnp.int32, (2 * rim, LANES), 0)
    lane = lax.broadcasted_iota(jnp.int32, (2 * rim, LANES), 1)
    x_place = (lane == tap).astype(BF16)
    y_place = (lane == (rim - tap) % LANES).astype(BF16)
    x_last = (lane[:1] == 2 * rim).astype(F32)
    y_last = (lane[:1] == LANES - rim).astype(F32)
    for n, (place, last_place) in enumerate(((x_place, x_last), (y_place, y_last))):
        block = got_ref[:, n].astype(F32)
        taps = jnp.concatenate([block[:, :, LANES - rim : LANES], block[:, :, 2 * LANES - rim :]], axis=2)
        for part in range(2):
            first = taps[:, part * ranks : (part + 1) * ranks].reshape(sources * ranks, 2 * rim)
            last = taps[:, 2 * ranks : 3 * ranks].reshape(sources * ranks, 2 * rim)[:, part : part + 1]
            line = jnp.dot(first.astype(BF16), place, preferred_element_type=F32) + last * last_place
            taps_ref[2 * n + part] = line
    k = lax.broadcasted_iota(jnp.int32, (LANES, LANES), 0)
    i = lax.broadcasted_iota(jnp.int32, (LANES, LANES), 1)
    near = jnp.abs(i - k) < half_lanes
    masks = [near] if windows == 1 else [k - i > half_lanes, near, k - i < -half_lanes]
    total_ref[...] = jnp.zeros_like(total_ref)

    def bands(source, slot):
        at = source * ranks if isinstance(source, int) else pl.multiple_of(source * ranks, ranks)
        lines = [taps_ref[n, pl.ds(at, ranks), :] for n in range(4)]
        y_lines = lines[2:]
        for r in range(ranks):
            re, im = (rolled(line[r : r + 1], mine) for line in lines[:2])
            top = 2 * r * mine
            column_ref[slot, top : top + mine, :LANES] = re.astype(column_ref.dtype)
            column_ref[slot, top : top + mine, LANES:] = (-im).astype(column_ref.dtype)
            column_ref[slot, top + mine : top + 2 * mine, :LANES] = im.astype(column_ref.dtype)
            column_ref[slot, top + mine : top + 2 * mine, LANES:] = re.astype(column_ref.dtype)
        for part in range(2):
            wide = jnp.broadcast_to(y_lines[part][:, None, :], (ranks, LANES, LANES))
            rings = pltpu.roll(wide, 0, 2, stride=1, stride_axis=1)
            for n, mask in enumerate(masks):
                middle = rings[:, rim : LANES - rim] if n == windows // 2 else jnp.zeros((ranks, LANES - 2 * rim, LANES), F32)
                band = [
                    jnp.where(mask[None, :rim], rings[:, :rim], 0.0),
                    middle,
                    jnp.where(mask[None, LANES - rim :], rings[:, LANES - rim :], 0.0),
                ]
                band = jnp.concatenate(band, axis=1).reshape(ranks * LANES, LANES)
                row_ref[slot, n, :, part * LANES : (part + 1) * LANES] = band.astype(BF16)

    def column_pass(slot):
        passed = lax.dot_general(
            column_ref[slot].astype(BF16), field_ref[...], (((1,), (1,)), ((), ())), preferred_element_type=F32
        )
        for chunk in range(chunks):
            for r in range(ranks):
                cells = []
                for part in range(2):
                    for comp in range(comps):
                        top, left = (2 * r + part) * mine, comp * slab_rows + chunk * LANES
                        cells.append(passed[top : top + mine, left : left + LANES])
                lhs_ref[slot, chunk, :, r * LANES : (r + 1) * LANES] = jnp.concatenate(cells, axis=0).astype(BF16)

    def row_pass(source, slot):
        weight = got_ref[source, 0].astype(F32)[2 * ranks : 2 * ranks + 1, LANES - rim : LANES]
        weight = weight[:, 2:3] + weight[:, 3:4] + weight[:, 4:5]
        for chunk in range(chunks):
            image = None
            for n in range(windows):
                other = chunk + n - windows // 2
                if 0 <= other < chunks:
                    term = jnp.dot(lhs_ref[slot, other], row_ref[slot, n], preferred_element_type=F32)
                    image = term if image is None else image + term
            of_re, of_im = image[: comps * mine], image[comps * mine :]
            image_re = of_re[:, :LANES] - of_im[:, LANES:]
            image_im = of_re[:, LANES:] + of_im[:, :LANES]
            square = image_re * image_re + image_im * image_im
            power = square[:mine]
            for comp in range(1, comps):
                power = power + square[comp * mine : (comp + 1) * mine]
            total_ref[:, chunk * LANES : (chunk + 1) * LANES] += weight * power

    if sources <= 8:
        bands(0, 0)
        column_pass(0)
        bands(1, 1)
        for source in range(sources):
            if source + 1 < sources:
                column_pass(source + 1)
            if source + 2 < sources:
                bands(source + 2, source + 2)
            row_pass(source, source)
    else:

        def one_source(source, _):
            bands(source, 0)
            column_pass(0)
            row_pass(source, 0)

        lax.fori_loop(0, sources, one_source, None)
    for chunk in range(chunks):
        lines = total_ref[:, chunk * LANES : (chunk + 1) * LANES].T
        for piece in range(LANES // rows):
            tile, source = divmod((chunk * LANES) // rows + piece, sources)
            block = lines[piece * rows : (piece + 1) * rows]
            step = out_ref.shape[2]
            groups = [block[n : n + step] for n in range(0, rows, step)]
            out_ref[source, tile] = jnp.concatenate(groups, axis=1)


def merge_kernel(parts_ref, out_ref):
    devices = parts_ref.shape[0]
    mine = out_ref.shape[2] // devices
    blocks = []
    for device in range(devices):
        part = parts_ref[device]
        groups = [part[:, at : at + mine] for at in range(0, part.shape[1], mine)]
        blocks.append(jnp.concatenate(groups, axis=0))
    out_ref[0] = jnp.concatenate(blocks, axis=1)


def per_device(near_field, x_taps, y_taps, source_weight):
    sources, tiles = lax.axis_size("src"), lax.axis_size("tile")
    _, rows, _, comps, width = near_field.shape
    ranks, taps = x_taps.shape[-2:]
    rim = (taps - 1) // 2
    devices = sources * tiles
    mine = width // devices
    lanes = 2 * LANES
    slab_rows = devices * rows
    chunks = slab_rows // LANES
    windows = 1 if chunks == 1 else 3
    height = comps * rows
    step = max(1, rows * mine // LANES)
    params = pltpu.CompilerParams(vmem_limit_bytes=48 * 1024 * 1024)
    whole = pl.BlockSpec(memory_space=pltpu.VMEM)

    def in_hbm(array):
        return pltpu.with_memory_space_constraint(array, pltpu.HBM)

    send = pl.pallas_call(
        functools.partial(send_kernel, rim),
        out_shape=jax.ShapeDtypeStruct((sources, tiles, height, lanes), BF16),
        in_specs=[pl.BlockSpec(memory_space=pltpu.HBM)] * 3 + [pl.BlockSpec(memory_space=pltpu.SMEM)],
        out_specs=whole,
        scratch_shapes=[
            pltpu.VMEM((1, rows, comps, 2, width), BF16),
            pltpu.VMEM(x_taps.shape, BF16),
            pltpu.VMEM(y_taps.shape, BF16),
            pltpu.SemaphoreType.DMA((3,)),
        ],
        compiler_params=params,
        name="send_columns",
    )(in_hbm(near_field.transpose(0, 1, 3, 2, 4)), in_hbm(x_taps), in_hbm(y_taps), source_weight)
    got = lax.all_to_all(send.reshape(devices, height, lanes), ("src", "tile"), 0, 0).reshape(send.shape)
    slots = sources if sources <= 8 else 1
    image = pl.pallas_call(
        functools.partial(image_kernel, rim, comps, rows, ranks),
        out_shape=jax.ShapeDtypeStruct((sources, tiles, step, rows // step * mine), F32),
        in_specs=[whole],
        out_specs=whole,
        scratch_shapes=[
            pltpu.VMEM((comps * slab_rows, lanes), BF16),
            pltpu.VMEM((4, sources * ranks, LANES), F32),
            pltpu.VMEM((slots, 2 * ranks * mine, lanes), BF16 if mine % 16 == 0 else F32),
            pltpu.VMEM((slots, chunks, 2 * comps * mine, ranks * LANES), BF16),
            pltpu.VMEM((slots, windows, ranks * LANES, 2 * LANES), BF16),
            pltpu.VMEM((mine, slab_rows), F32),
        ],
        compiler_params=params,
        name="image",
    )(got)
    parts = lax.all_to_all(image.reshape((devices,) + image.shape[2:]), ("src", "tile"), 0, 0)
    return pl.pallas_call(
        merge_kernel,
        out_shape=jax.ShapeDtypeStruct((1, rows, width), F32),
        in_specs=[whole],
        out_specs=whole,
        compiler_params=params,
        name="merge_columns",
    )(parts)


def solution(mesh):
    placed = (
        P(("group", "tile"), "src", None, None, None),
        P("src", None, None, None),
        P("src", None, None, None),
        P("src"),
    )
    return jax.shard_map(
        per_device,
        mesh=mesh,
        in_specs=placed,
        out_specs=P(("group", "tile"), "src", None),
        check_vma=False,
    )
```

```python
import functools

import jax
import jax.numpy as jnp
from jax import lax
from jax.experimental import pallas as pl
from jax.experimental.pallas import tpu as pltpu
from jax.sharding import PartitionSpec as P

LANES = 128
F32 = jnp.float32
BF16 = jnp.bfloat16


def send_kernel(
    rim, field_hbm, x_taps_hbm, y_taps_hbm, weight_ref, send_ref, field_ref, x_taps_ref, y_taps_ref, sems
):
    pairs = ((field_hbm, field_ref), (x_taps_hbm, x_taps_ref), (y_taps_hbm, y_taps_ref))
    copies = [pltpu.make_async_copy(source, target, sems.at[n]) for n, (source, target) in enumerate(pairs)]
    for copy in copies:
        copy.start()
    copies[1].wait()
    copies[2].wait()
    _, rows, comps, _, width = field_ref.shape
    sources, tiles, height, lanes = send_ref.shape
    ranks, taps = x_taps_ref.shape[2:]
    mine = width // (sources * tiles)
    window = mine + 2 * rim
    lower = lax.axis_index("tile") == 0
    lines = [
        jnp.where(lower, x_taps_ref[0, part].astype(F32), y_taps_ref[0, part].astype(F32)) for part in range(2)
    ]
    weight = jnp.full((ranks, 1), weight_ref[0], F32)
    high = weight.astype(BF16).astype(F32)
    middle = (weight - high).astype(BF16).astype(F32)
    low = weight - high - middle
    last = [line[:, taps - 1 :] for line in lines] + [high, middle, low]
    last.append(jnp.zeros((ranks, taps - 1 - len(last)), F32))
    spare = jnp.concatenate([line[:, : taps - 1] for line in lines] + [jnp.concatenate(last, axis=1)], axis=0)
    spares = [spare[:, :rim], spare[:, rim:]]
    if window < LANES - rim:
        gap = jnp.zeros((height, LANES - rim - window), F32)
        spares = [jnp.concatenate([gap, part], axis=1) for part in spares]
    copies[0].wait()
    edge = jnp.zeros((rows, rim), F32)
    field = field_ref[0].astype(F32)
    padded = [
        [jnp.concatenate([edge, field[:, comp, part, :], edge], axis=1) for part in range(2)] for comp in range(comps)
    ]
    for device in range(sources * tiles):
        at = device * mine
        cells = []
        for part in range(2):
            plane = [padded[comp][part][:, at : at + window] for comp in range(comps)]
            cells += [jnp.concatenate(plane, axis=0), spares[part]]
        source, tile = divmod(device, tiles)
        send_ref[source, tile] = jnp.concatenate(cells, axis=1).astype(BF16)


def rolled(line, count):
    return pltpu.roll(jnp.broadcast_to(line, (count, line.shape[1])), 0, 1, stride=1, stride_axis=0)


def image_kernel(rim, comps, rows, ranks, got_ref, out_ref, field_ref, taps_ref, column_ref, lhs_ref, row_ref, total_ref):
    sources, tiles, _, lanes = got_ref.shape
    mine, slab_rows = total_ref.shape
    window = mine + 2 * rim
    tile_rows = sources * rows
    chunks = slab_rows // LANES
    windows = row_ref.shape[1]
    half_lanes = LANES // 2
    for tile in range(tiles):
        cells = got_ref[:, tile].astype(F32)
        for comp in range(comps):
            some = cells[:, comp * rows : (comp + 1) * rows, :].reshape(tile_rows, lanes).astype(BF16)
            at = comp * slab_rows + tile * tile_rows
            field_ref[at : at + tile_rows, :] = some

    tap = lax.broadcasted_iota(jnp.int32, (2 * rim, LANES), 0)
    lane = lax.broadcasted_iota(jnp.int32, (2 * rim, LANES), 1)
    x_place = (lane == tap).astype(BF16)
    y_place = (lane == (rim - tap) % LANES).astype(BF16)
    x_last = (lane[:1] == 2 * rim).astype(F32)
    y_last = (lane[:1] == LANES - rim).astype(F32)
    for n, (place, last_place) in enumerate(((x_place, x_last), (y_place, y_last))):
        block = got_ref[:, n].astype(F32)
        taps = jnp.concatenate([block[:, :, LANES - rim : LANES], block[:, :, 2 * LANES - rim :]], axis=2)
        for part in range(2):
            first = taps[:, part * ranks : (part + 1) * ranks].reshape(sources * ranks, 2 * rim)
            last = taps[:, 2 * ranks : 3 * ranks].reshape(sources * ranks, 2 * rim)[:, part : part + 1]
            line = jnp.dot(first.astype(BF16), place, preferred_element_type=F32) + last * last_place
            taps_ref[2 * n + part] = line
    k = lax.broadcasted_iota(jnp.int32, (LANES, LANES), 0)
    i = lax.broadcasted_iota(jnp.int32, (LANES, LANES), 1)
    near = jnp.abs(i - k) < half_lanes
    masks = [near] if windows == 1 else [k - i > half_lanes, near, k - i < -half_lanes]
    total_ref[...] = jnp.zeros_like(total_ref)

    def bands(source, slot):
        at = source * ranks if isinstance(source, int) else pl.multiple_of(source * ranks, ranks)
        lines = [taps_ref[n, pl.ds(at, ranks), :] for n in range(4)]
        y_lines = lines[2:]
        for r in range(ranks):
            re, im = (rolled(line[r : r + 1], mine) for line in lines[:2])
            top = 2 * r * mine
            column_ref[slot, top : top + mine, :LANES] = re.astype(column_ref.dtype)
            column_ref[slot, top : top + mine, LANES:] = (-im).astype(column_ref.dtype)
            column_ref[slot, top + mine : top + 2 * mine, :LANES] = im.astype(column_ref.dtype)
            column_ref[slot, top + mine : top + 2 * mine, LANES:] = re.astype(column_ref.dtype)
        for r in range(ranks):
            for part in range(2):
                ring = rolled(y_lines[part][r : r + 1], LANES)
                for n, mask in enumerate(masks):
                    band = [
                        jnp.where(mask[:rim], ring[:rim], 0.0),
                        ring[rim : LANES - rim] if n == windows // 2 else jnp.zeros((LANES - 2 * rim, LANES), F32),
                        jnp.where(mask[LANES - rim :], ring[LANES - rim :], 0.0),
                    ]
                    row_ref[slot, n, r * LANES : (r + 1) * LANES, part * LANES : (part + 1) * LANES] = jnp.concatenate(
                        band, axis=0
                    ).astype(BF16)

    def column_pass(slot):
        passed = lax.dot_general(
            column_ref[slot].astype(BF16), field_ref[...], (((1,), (1,)), ((), ())), preferred_element_type=F32
        )
        for chunk in range(chunks):
            for r in range(ranks):
                cells = []
                for part in range(2):
                    for comp in range(comps):
                        top, left = (2 * r + part) * mine, comp * slab_rows + chunk * LANES
                        cells.append(passed[top : top + mine, left : left + LANES])
                lhs_ref[slot, chunk, :, r * LANES : (r + 1) * LANES] = jnp.concatenate(cells, axis=0).astype(BF16)

    def row_pass(source, slot):
        weight = got_ref[source, 0].astype(F32)[2 * ranks : 2 * ranks + 1, LANES - rim : LANES]
        weight = weight[:, 2:3] + weight[:, 3:4] + weight[:, 4:5]
        for chunk in range(chunks):
            image = None
            for n in range(windows):
                other = chunk + n - windows // 2
                if 0 <= other < chunks:
                    term = jnp.dot(lhs_ref[slot, other], row_ref[slot, n], preferred_element_type=F32)
                    image = term if image is None else image + term
            of_re, of_im = image[: comps * mine], image[comps * mine :]
            image_re = of_re[:, :LANES] - of_im[:, LANES:]
            image_im = of_re[:, LANES:] + of_im[:, :LANES]
            square = image_re * image_re + image_im * image_im
            power = square[:mine]
            for comp in range(1, comps):
                power = power + square[comp * mine : (comp + 1) * mine]
            total_ref[:, chunk * LANES : (chunk + 1) * LANES] += weight * power

    if sources <= 8:
        bands(0, 0)
        column_pass(0)
        bands(1, 1)
        for source in range(sources):
            if source + 1 < sources:
                column_pass(source + 1)
            if source + 2 < sources:
                bands(source + 2, source + 2)
            row_pass(source, source)
    else:

        def one_source(source, _):
            bands(source, 0)
            column_pass(0)
            row_pass(source, 0)

        lax.fori_loop(0, sources, one_source, None)
    for chunk in range(chunks):
        lines = total_ref[:, chunk * LANES : (chunk + 1) * LANES].T
        for piece in range(LANES // rows):
            tile, source = divmod((chunk * LANES) // rows + piece, sources)
            block = lines[piece * rows : (piece + 1) * rows]
            step = out_ref.shape[2]
            groups = [block[n : n + step] for n in range(0, rows, step)]
            out_ref[source, tile] = jnp.concatenate(groups, axis=1)


def merge_kernel(parts_ref, out_ref):
    devices = parts_ref.shape[0]
    mine = out_ref.shape[2] // devices
    blocks = []
    for device in range(devices):
        part = parts_ref[device]
        groups = [part[:, at : at + mine] for at in range(0, part.shape[1], mine)]
        blocks.append(jnp.concatenate(groups, axis=0))
    out_ref[0] = jnp.concatenate(blocks, axis=1)


def per_device(near_field, x_taps, y_taps, source_weight):
    sources, tiles = lax.axis_size("src"), lax.axis_size("tile")
    _, rows, _, comps, width = near_field.shape
    ranks, taps = x_taps.shape[-2:]
    rim = (taps - 1) // 2
    devices = sources * tiles
    mine = width // devices
    lanes = 2 * LANES
    slab_rows = devices * rows
    chunks = slab_rows // LANES
    windows = 1 if chunks == 1 else 3
    height = comps * rows
    step = max(1, rows * mine // LANES)
    params = pltpu.CompilerParams(vmem_limit_bytes=48 * 1024 * 1024)
    whole = pl.BlockSpec(memory_space=pltpu.VMEM)

    def in_hbm(array):
        return pltpu.with_memory_space_constraint(array, pltpu.HBM)

    send = pl.pallas_call(
        functools.partial(send_kernel, rim),
        out_shape=jax.ShapeDtypeStruct((sources, tiles, height, lanes), BF16),
        in_specs=[pl.BlockSpec(memory_space=pltpu.HBM)] * 3 + [pl.BlockSpec(memory_space=pltpu.SMEM)],
        out_specs=whole,
        scratch_shapes=[
            pltpu.VMEM((1, rows, comps, 2, width), BF16),
            pltpu.VMEM(x_taps.shape, BF16),
            pltpu.VMEM(y_taps.shape, BF16),
            pltpu.SemaphoreType.DMA((3,)),
        ],
        compiler_params=params,
        name="send_columns",
    )(in_hbm(near_field.transpose(0, 1, 3, 2, 4)), in_hbm(x_taps), in_hbm(y_taps), source_weight)
    got = lax.all_to_all(send.reshape(devices, height, lanes), ("src", "tile"), 0, 0).reshape(send.shape)
    slots = sources if sources <= 8 else 1
    image = pl.pallas_call(
        functools.partial(image_kernel, rim, comps, rows, ranks),
        out_shape=jax.ShapeDtypeStruct((sources, tiles, step, rows // step * mine), F32),
        in_specs=[whole],
        out_specs=whole,
        scratch_shapes=[
            pltpu.VMEM((comps * slab_rows, lanes), BF16),
            pltpu.VMEM((4, sources * ranks, LANES), F32),
            pltpu.VMEM((slots, 2 * ranks * mine, lanes), BF16 if mine % 16 == 0 else F32),
            pltpu.VMEM((slots, chunks, 2 * comps * mine, ranks * LANES), BF16),
            pltpu.VMEM((slots, windows, ranks * LANES, 2 * LANES), BF16),
            pltpu.VMEM((mine, slab_rows), F32),
        ],
        compiler_params=params,
        name="image",
    )(got)
    parts = lax.all_to_all(image.reshape((devices,) + image.shape[2:]), ("src", "tile"), 0, 0)
    return pl.pallas_call(
        merge_kernel,
        out_shape=jax.ShapeDtypeStruct((1, rows, width), F32),
        in_specs=[whole],
        out_specs=whole,
        compiler_params=params,
        name="merge_columns",
    )(parts)


def solution(mesh):
    placed = (
        P(("group", "tile"), "src", None, None, None),
        P("src", None, None, None),
        P("src", None, None, None),
        P("src"),
    )
    return jax.shard_map(
        per_device,
        mesh=mesh,
        in_specs=placed,
        out_specs=P(("group", "tile"), "src", None),
        check_vma=False,
    )
```

```python
import functools

import jax
import jax.numpy as jnp
from jax import lax
from jax.experimental import pallas as pl
from jax.experimental.pallas import tpu as pltpu
from jax.sharding import PartitionSpec as P

LANES = 128
F32 = jnp.float32
BF16 = jnp.bfloat16


def send_kernel(
    rim, field_hbm, x_taps_hbm, y_taps_hbm, weight_ref, send_ref, field_ref, x_taps_ref, y_taps_ref, sems
):
    pairs = ((field_hbm, field_ref), (x_taps_hbm, x_taps_ref), (y_taps_hbm, y_taps_ref))
    copies = [pltpu.make_async_copy(source, target, sems.at[n]) for n, (source, target) in enumerate(pairs)]
    for copy in copies:
        copy.start()
    for copy in copies:
        copy.wait()
    _, rows, comps, _, width = field_ref.shape
    sources, tiles, height, lanes = send_ref.shape
    ranks, taps = x_taps_ref.shape[2:]
    mine = width // (sources * tiles)
    window = mine + 2 * rim
    edge = jnp.zeros((rows, rim), F32)
    field = field_ref[0].astype(F32)
    padded = [
        [jnp.concatenate([edge, field[:, comp, part, :], edge], axis=1) for part in range(2)] for comp in range(comps)
    ]
    lower = lax.axis_index("tile") == 0
    lines = [
        jnp.where(lower, x_taps_ref[0, part].astype(F32), y_taps_ref[0, part].astype(F32)) for part in range(2)
    ]
    weight = jnp.full((ranks, 1), weight_ref[0], F32)
    high = weight.astype(BF16).astype(F32)
    middle = (weight - high).astype(BF16).astype(F32)
    low = weight - high - middle
    last = [line[:, taps - 1 :] for line in lines] + [high, middle, low]
    last.append(jnp.zeros((ranks, taps - 1 - len(last)), F32))
    spare = jnp.concatenate([line[:, : taps - 1] for line in lines] + [jnp.concatenate(last, axis=1)], axis=0)
    spares = [spare[:, :rim], spare[:, rim:]]
    if window < LANES - rim:
        gap = jnp.zeros((height, LANES - rim - window), F32)
        spares = [jnp.concatenate([gap, part], axis=1) for part in spares]
    for device in range(sources * tiles):
        at = device * mine
        cells = []
        for part in range(2):
            plane = [padded[comp][part][:, at : at + window] for comp in range(comps)]
            cells += [jnp.concatenate(plane, axis=0), spares[part]]
        source, tile = divmod(device, tiles)
        send_ref[source, tile] = jnp.concatenate(cells, axis=1).astype(BF16)


def rolled(line, count):
    return pltpu.roll(jnp.broadcast_to(line, (count, line.shape[1])), 0, 1, stride=1, stride_axis=0)


def image_kernel(rim, comps, rows, ranks, got_ref, out_ref, field_ref, taps_ref, column_ref, lhs_ref, row_ref, total_ref):
    sources, tiles, _, lanes = got_ref.shape
    mine, slab_rows = total_ref.shape
    window = mine + 2 * rim
    tile_rows = sources * rows
    chunks = slab_rows // LANES
    windows = row_ref.shape[1]
    half_lanes = LANES // 2
    for tile in range(tiles):
        cells = got_ref[:, tile].astype(F32)
        for comp in range(comps):
            some = cells[:, comp * rows : (comp + 1) * rows, :].reshape(tile_rows, lanes).astype(BF16)
            at = comp * slab_rows + tile * tile_rows
            field_ref[at : at + tile_rows, :] = some

    tap = lax.broadcasted_iota(jnp.int32, (2 * rim, LANES), 0)
    lane = lax.broadcasted_iota(jnp.int32, (2 * rim, LANES), 1)
    x_place = (lane == tap).astype(BF16)
    y_place = (lane == (rim - tap) % LANES).astype(BF16)
    x_last = (lane[:1] == 2 * rim).astype(F32)
    y_last = (lane[:1] == LANES - rim).astype(F32)
    for n, (place, last_place) in enumerate(((x_place, x_last), (y_place, y_last))):
        block = got_ref[:, n].astype(F32)
        taps = jnp.concatenate([block[:, :, LANES - rim : LANES], block[:, :, 2 * LANES - rim :]], axis=2)
        for part in range(2):
            first = taps[:, part * ranks : (part + 1) * ranks].reshape(sources * ranks, 2 * rim)
            last = taps[:, 2 * ranks : 3 * ranks].reshape(sources * ranks, 2 * rim)[:, part : part + 1]
            line = jnp.dot(first.astype(BF16), place, preferred_element_type=F32) + last * last_place
            taps_ref[2 * n + part] = line
    k = lax.broadcasted_iota(jnp.int32, (LANES, LANES), 0)
    i = lax.broadcasted_iota(jnp.int32, (LANES, LANES), 1)
    near = jnp.abs(i - k) < half_lanes
    masks = [near] if windows == 1 else [k - i > half_lanes, near, k - i < -half_lanes]
    total_ref[...] = jnp.zeros_like(total_ref)

    def bands(source, slot):
        at = source * ranks if isinstance(source, int) else pl.multiple_of(source * ranks, ranks)
        lines = [taps_ref[n, pl.ds(at, ranks), :] for n in range(4)]
        y_lines = lines[2:]
        for r in range(ranks):
            re, im = (rolled(line[r : r + 1], mine) for line in lines[:2])
            top = 2 * r * mine
            column_ref[slot, top : top + mine, :LANES] = re.astype(column_ref.dtype)
            column_ref[slot, top : top + mine, LANES:] = (-im).astype(column_ref.dtype)
            column_ref[slot, top + mine : top + 2 * mine, :LANES] = im.astype(column_ref.dtype)
            column_ref[slot, top + mine : top + 2 * mine, LANES:] = re.astype(column_ref.dtype)
        for r in range(ranks):
            for part in range(2):
                ring = rolled(y_lines[part][r : r + 1], LANES)
                for n, mask in enumerate(masks):
                    band = [
                        jnp.where(mask[:rim], ring[:rim], 0.0),
                        ring[rim : LANES - rim] if n == windows // 2 else jnp.zeros((LANES - 2 * rim, LANES), F32),
                        jnp.where(mask[LANES - rim :], ring[LANES - rim :], 0.0),
                    ]
                    row_ref[slot, n, r * LANES : (r + 1) * LANES, part * LANES : (part + 1) * LANES] = jnp.concatenate(
                        band, axis=0
                    ).astype(BF16)

    def column_pass(slot):
        passed = lax.dot_general(
            column_ref[slot].astype(BF16), field_ref[...], (((1,), (1,)), ((), ())), preferred_element_type=F32
        )
        for chunk in range(chunks):
            for r in range(ranks):
                cells = []
                for part in range(2):
                    for comp in range(comps):
                        top, left = (2 * r + part) * mine, comp * slab_rows + chunk * LANES
                        cells.append(passed[top : top + mine, left : left + LANES])
                lhs_ref[slot, chunk, :, r * LANES : (r + 1) * LANES] = jnp.concatenate(cells, axis=0).astype(BF16)

    def row_pass(source, slot):
        weight = got_ref[source, 0].astype(F32)[2 * ranks : 2 * ranks + 1, LANES - rim : LANES]
        weight = weight[:, 2:3] + weight[:, 3:4] + weight[:, 4:5]
        for chunk in range(chunks):
            image = None
            for n in range(windows):
                other = chunk + n - windows // 2
                if 0 <= other < chunks:
                    term = jnp.dot(lhs_ref[slot, other], row_ref[slot, n], preferred_element_type=F32)
                    image = term if image is None else image + term
            of_re, of_im = image[: comps * mine], image[comps * mine :]
            image_re = of_re[:, :LANES] - of_im[:, LANES:]
            image_im = of_re[:, LANES:] + of_im[:, :LANES]
            square = image_re * image_re + image_im * image_im
            power = square[:mine]
            for comp in range(1, comps):
                power = power + square[comp * mine : (comp + 1) * mine]
            total_ref[:, chunk * LANES : (chunk + 1) * LANES] += weight * power

    if sources <= 8:
        bands(0, 0)
        column_pass(0)
        bands(1, 1)
        for source in range(sources):
            if source + 1 < sources:
                column_pass(source + 1)
            if source + 2 < sources:
                bands(source + 2, source + 2)
            row_pass(source, source)
    else:

        def one_source(source, _):
            bands(source, 0)
            column_pass(0)
            row_pass(source, 0)

        lax.fori_loop(0, sources, one_source, None)
    for chunk in range(chunks):
        lines = total_ref[:, chunk * LANES : (chunk + 1) * LANES].T
        for piece in range(LANES // rows):
            tile, source = divmod((chunk * LANES) // rows + piece, sources)
            block = lines[piece * rows : (piece + 1) * rows]
            step = out_ref.shape[2]
            groups = [block[n : n + step] for n in range(0, rows, step)]
            out_ref[source, tile] = jnp.concatenate(groups, axis=1)


def merge_kernel(parts_ref, out_ref):
    devices = parts_ref.shape[0]
    rows = out_ref.shape[1]
    mine = out_ref.shape[2] // devices
    _, step, held = parts_ref.shape
    count = rows // step
    if held == LANES and LANES // mine == count:
        row_group = lax.broadcasted_iota(jnp.int32, (rows, LANES), 0) // step
        lane_group = lax.broadcasted_iota(jnp.int32, (rows, LANES), 1) // mine
        apart = (row_group - lane_group + count) % count
        for first in range(0, devices, count):
            cells = jnp.concatenate([parts_ref[first + n] for n in range(count)], axis=0)
            block = cells
            for k in range(1, count):
                moved = pltpu.roll(pltpu.roll(cells, k * step, 0), LANES - k * mine, 1)
                block = jnp.where(apart == k, moved, block)
            out_ref[0, :, first * mine : (first + count) * mine] = block
        return
    blocks = []
    for device in range(devices):
        part = parts_ref[device]
        groups = [part[:, at : at + mine] for at in range(0, part.shape[1], mine)]
        blocks.append(jnp.concatenate(groups, axis=0))
    out_ref[0] = jnp.concatenate(blocks, axis=1)


def per_device(near_field, x_taps, y_taps, source_weight):
    sources, tiles = lax.axis_size("src"), lax.axis_size("tile")
    _, rows, _, comps, width = near_field.shape
    ranks, taps = x_taps.shape[-2:]
    rim = (taps - 1) // 2
    devices = sources * tiles
    mine = width // devices
    lanes = 2 * LANES
    slab_rows = devices * rows
    chunks = slab_rows // LANES
    windows = 1 if chunks == 1 else 3
    height = comps * rows
    step = max(1, rows * mine // LANES)
    params = pltpu.CompilerParams(vmem_limit_bytes=48 * 1024 * 1024)
    whole = pl.BlockSpec(memory_space=pltpu.VMEM)

    def in_hbm(array):
        return pltpu.with_memory_space_constraint(array, pltpu.HBM)

    send = pl.pallas_call(
        functools.partial(send_kernel, rim),
        out_shape=jax.ShapeDtypeStruct((sources, tiles, height, lanes), BF16),
        in_specs=[pl.BlockSpec(memory_space=pltpu.HBM)] * 3 + [pl.BlockSpec(memory_space=pltpu.SMEM)],
        out_specs=whole,
        scratch_shapes=[
            pltpu.VMEM((1, rows, comps, 2, width), BF16),
            pltpu.VMEM(x_taps.shape, BF16),
            pltpu.VMEM(y_taps.shape, BF16),
            pltpu.SemaphoreType.DMA((3,)),
        ],
        compiler_params=params,
        name="send_columns",
    )(in_hbm(near_field.transpose(0, 1, 3, 2, 4)), in_hbm(x_taps), in_hbm(y_taps), source_weight)
    got = lax.all_to_all(send.reshape(devices, height, lanes), ("src", "tile"), 0, 0).reshape(send.shape)
    slots = sources if sources <= 8 else 1
    image = pl.pallas_call(
        functools.partial(image_kernel, rim, comps, rows, ranks),
        out_shape=jax.ShapeDtypeStruct((sources, tiles, step, rows // step * mine), F32),
        in_specs=[whole],
        out_specs=whole,
        scratch_shapes=[
            pltpu.VMEM((comps * slab_rows, lanes), BF16),
            pltpu.VMEM((4, sources * ranks, LANES), F32),
            pltpu.VMEM((slots, 2 * ranks * mine, lanes), BF16 if mine % 16 == 0 else F32),
            pltpu.VMEM((slots, chunks, 2 * comps * mine, ranks * LANES), BF16),
            pltpu.VMEM((slots, windows, ranks * LANES, 2 * LANES), BF16),
            pltpu.VMEM((mine, slab_rows), F32),
        ],
        compiler_params=params,
        name="image",
    )(got)
    parts = lax.all_to_all(image.reshape((devices,) + image.shape[2:]), ("src", "tile"), 0, 0)
    return pl.pallas_call(
        merge_kernel,
        out_shape=jax.ShapeDtypeStruct((1, rows, width), F32),
        in_specs=[whole],
        out_specs=whole,
        compiler_params=params,
        name="merge_columns",
    )(parts)


def solution(mesh):
    placed = (
        P(("group", "tile"), "src", None, None, None),
        P("src", None, None, None),
        P("src", None, None, None),
        P("src"),
    )
    return jax.shard_map(
        per_device,
        mesh=mesh,
        in_specs=placed,
        out_specs=P(("group", "tile"), "src", None),
        check_vma=False,
    )
```
